32 devices in a mesh: groups: 2 (over y), frame: 8 (over z, x), row: 2 (over core).
Axes of the slice: x: 2, y: 2, z: 4, core: 2. Of those that a mesh axis runs over, the one named last changes fastest.
Arguments:
- latents: bfloat16 [16, 1024, 256], P(('groups', 'frame'), 'row'), parts along dimension 0, may hold values from -8 to 8
- ref_frames: int32 [16, 2], P(('groups', 'frame')), parts along dimension 0, may hold values from 0 to 7, as said below
- windows: int32 [16], P(('groups', 'frame')), parts along dimension 0, may hold values from 1 to 2, as said below
- quant_level: int32 [16], P(('groups', 'frame')), parts along dimension 0, may hold values from 0 to 63
- quant_scale: float32 [64, 256], replicated, may hold values from 0.5 to 2
- shared_proj: bfloat16 [256, 256], replicated, may hold values from -0.375 to 0.375
- value_proj: bfloat16 [256, 256], replicated, may hold values from -0.375 to 0.375
- output_proj: bfloat16 [256, 256], replicated, may hold values from -0.75 to 0.75
- conv_taps: bfloat16 [3, 256, 256], replicated, may hold values from -0.21875 to 0.21875
- cotangent: bfloat16 [16, 1024, 256], P(('groups', 'frame'), 'row'), parts along dimension 0, may hold values from -6 to 6
Outputs:
- coded_latent: bfloat16 [16, 1024, 256], P(('groups', 'frame'), 'row'), parts along dimension 0
- grad_latents: bfloat16 [16, 1024, 256], P(('groups', 'frame'), 'row'), parts along dimension 0
- grad_shared: float32 [512, 256], P('groups'), parts along dimension 0
- grad_values: float32 [512, 256], P('groups'), parts along dimension 0
- grad_output: float32 [512, 256], P('groups'), parts along dimension 0
- grad_taps: float32 [6, 256, 256], P('groups'), parts along dimension 0
The draws below stay inside these ranges and needn't reach their ends.
There are 2 independent parts, one for each index of `groups`. The reference program is written for one: setup_inputs(seed, part) draws one part's arguments, and reference() takes and returns one part's arrays. A program takes and returns all parts, laid end to end along the dimension named above; an argument that names none is the same for every part. Nothing has to cross between parts.
Inputs may be any that keep to these rules, and one draw needn't show every extreme that they name: ref_frames[f, s] differs from f by a power of two no larger than 2 ** 2, and that largest distance occurs. `windows`: some frame has a window of 2 rows.
All inputs are finite; a program needn't handle non-finite values.
Results may differ from the reference program's by a relative error of at most 0.0045.
The reference program's roundings to bfloat16 on the way count: a program that leaves them out, or rounds other values in their place, can miss the bound.
Values may be sent and summed in bfloat16 or wider, within the bound.
No kernel may reach another device: no remote copies, remote signals or barrier semaphores. Data moves between devices by JAX's collectives and lax.ppermute only.
A program may use at most 128 MiB of HBM per device.

```python
import math
import jax
import jax.numpy as jnp
from jax import lax

C = 256
HEADS = 8
DH = 32
COLS = 64
QROWS = 8
WMAX = 2
LEVELS = 3
NQ = 64
FRAMES = 8
HROWS = 16
TOKF = 1024


def draw_latents(key, part):
    shape = (FRAMES, HROWS * COLS, C)
    values = jnp.clip(jax.random.normal(jax.random.fold_in(key, 1), shape, jnp.float32), -4.0, 4.0)
    return values.astype(jnp.bfloat16)


def draw_ref_frames(key, part):
    depth = jax.random.randint(jax.random.fold_in(key, 1), (FRAMES, 2), 0, LEVELS)
    depth = depth.at[0, 0].set(LEVELS - 1)
    distance = jnp.left_shift(jnp.ones((FRAMES, 2), jnp.int32), depth.astype(jnp.int32))
    side = jax.random.randint(jax.random.fold_in(key, 2), (FRAMES, 2), 0, 2)
    frame_ids = jnp.arange(FRAMES, dtype=jnp.int32)[:, None]
    earlier = frame_ids - distance
    later = frame_ids + distance
    pick_earlier = jnp.where(side == 0, earlier >= 0, later > FRAMES - 1)
    return jnp.where(pick_earlier, earlier, later).astype(jnp.int32)


def draw_windows(key, part):
    window = jax.random.randint(jax.random.fold_in(key, 3), (FRAMES,), 1, WMAX + 1)
    return window.at[0].set(WMAX).astype(jnp.int32)


def with_ends(drawn, stream_key, low, largest):
    shape = drawn.shape
    place = [jax.random.randint(jax.random.fold_in(stream_key, axis), (), 0, shape[axis]) for axis in range(len(shape))]
    drawn = drawn.at[tuple(place)].set(low)
    longest = shape.index(max(shape))
    place[longest] = (place[longest] + 1) % shape[longest]
    return drawn.at[tuple(place)].set(largest)


def shard_levels(key, extent, shards, low, largest):
    factor_of, own = 1.0, jax.random.fold_in(key, 6)
    for position, parts in shards:
        draws = jnp.exp(jax.random.uniform(jax.random.fold_in(own, position), (parts,), jnp.float32, low / len(shards), largest / len(shards)))
        factor_of = factor_of * jnp.repeat(draws, extent[position] // parts).reshape([-1 if axis == position else 1 for axis in range(len(extent))])
    return factor_of


def noise(rng, dims, scale, most, split=(), kind=jnp.bfloat16):
    loudness = shard_levels(rng, dims, split, -0.22, 0.18) if split else 1.0
    array = jax.random.normal(rng, dims, jnp.float32) * scale * loudness
    return jnp.minimum(jnp.maximum(array, -most), most).astype(kind)


def setup_inputs(seed: int = 0, part: int = 0) -> dict:
    seeds = jax.random.split(jax.random.key(seed), 11)
    own_keys = jax.random.split(jax.random.fold_in(seeds[10], part), 11)
    latents = draw_latents(jax.random.fold_in(jax.random.fold_in(seeds[10], part), 71), part)
    ref_frames = draw_ref_frames(jax.random.fold_in(jax.random.fold_in(seeds[10], part), 71), part)
    windows = draw_windows(jax.random.fold_in(jax.random.fold_in(seeds[10], part), 71), part)
    quant_level = with_ends(jax.random.randint(own_keys[3], (FRAMES,), 0, NQ), jax.random.fold_in(own_keys[3], 1), 0, NQ - 1).astype(jnp.int32)
    quant_scale = jnp.clip(jnp.exp(jax.random.uniform(seeds[4], (NQ, C), jnp.float32, math.log(0.5), math.log(2.0))), 0.5, 2.0)
    shared_proj = noise(seeds[5], (C, C), C ** -0.5, 0.375)
    value_proj = noise(seeds[6], (C, C), C ** -0.5, 0.375)
    output_proj = noise(seeds[7], (C, C), (C // 4) ** -0.5, 0.75)
    conv_taps = noise(seeds[8], (3, C, C), (3 * C) ** -0.5, 0.21875)
    cotangent = noise(own_keys[9], (FRAMES, TOKF, C), 1.0, 6.0, ((0, 8), (1, 2)))
    return {"latents": latents, "ref_frames": ref_frames, "windows": windows, "quant_level": quant_level, "quant_scale": quant_scale, "shared_proj": shared_proj, "value_proj": value_proj, "output_proj": output_proj, "conv_taps": conv_taps, "cotangent": cotangent}


SCORE_GAIN = 1.5
LAST_DIMS = (((1,), (1,)), ((), ()))
FIRST_DIMS = (((0,), (0,)), ((), ()))

def split_heads(block):
    return jnp.transpose(block.reshape(block.shape[0], HEADS, DH), (1, 0, 2))

def merge_heads(block):
    return jnp.transpose(block, (1, 0, 2)).reshape(block.shape[1], HEADS * DH)

def head_weights(query_head, key_head, allowed):
    scores = jnp.dot(query_head, key_head.T, preferred_element_type=jnp.float32) * (SCORE_GAIN / math.sqrt(DH))
    scores = jnp.where(allowed, scores, -jnp.inf)
    row_max = lax.optimization_barrier(jnp.max(scores, axis=1, keepdims=True))
    exp_terms = jnp.where(allowed, jnp.exp(scores - row_max), 0.0)
    return exp_terms / lax.optimization_barrier(jnp.sum(exp_terms, axis=1, keepdims=True))

def block_forward(query, keys, values, allowed):

    def one_head(head_parts):
        query_head, key_head, value_head = head_parts
        weights = head_weights(query_head, key_head, allowed)
        return jnp.dot(weights.astype(jnp.bfloat16), value_head, preferred_element_type=jnp.float32)
    result = lax.map(one_head, (split_heads(query), split_heads(keys), split_heads(values)))
    return merge_heads(result).astype(jnp.bfloat16)

def block_backward(query, keys, values, allowed, upstream):

    def one_head(head_parts):
        query_head, key_head, value_head, grad_head = head_parts
        weights = head_weights(query_head, key_head, allowed)
        prob = weights.astype(jnp.bfloat16)
        grad_prob = jnp.dot(grad_head, value_head.T, preferred_element_type=jnp.float32)
        value_grad = jnp.dot(prob.T, grad_head, preferred_element_type=jnp.float32)
        row_inner = lax.optimization_barrier(jnp.sum(weights * grad_prob, axis=1, keepdims=True))
        grad_score = (weights * (grad_prob - row_inner) * (SCORE_GAIN / math.sqrt(DH))).astype(jnp.bfloat16)
        query_grad = jnp.dot(grad_score, key_head, preferred_element_type=jnp.float32)
        key_grad = jnp.dot(grad_score.T, query_head, preferred_element_type=jnp.float32)
        return (query_grad, key_grad, value_grad)
    query_grad, key_grad, value_grad = lax.map(one_head, (split_heads(query), split_heads(keys), split_heads(values), split_heads(upstream)))
    return (merge_heads(query_grad), merge_heads(key_grad), merge_heads(value_grad))

def allowed_mask(begin_row, window, total_rows):
    key_span = QROWS + 2 * WMAX
    query_rows = begin_row + jnp.repeat(jnp.arange(QROWS, dtype=jnp.int32), COLS)
    key_rows = jnp.tile(jnp.repeat(begin_row - WMAX + jnp.arange(key_span, dtype=jnp.int32), COLS), 2)
    nearby = jnp.abs(query_rows[:, None] - key_rows[None, :]) <= window
    inside = (key_rows >= 0) & (key_rows < total_rows)
    return nearby & inside[None, :]

def add_window(summed, addend, begin_row):
    current = lax.dynamic_slice_in_dim(summed, begin_row, addend.shape[1], 1)
    return lax.dynamic_update_slice_in_dim(summed, current + addend, begin_row, 1)

def against(left_side, weight):
    return lax.dot_general(left_side, weight, LAST_DIMS, preferred_element_type=jnp.float32)

def cross_rows(left_side, right_side):
    return lax.dot_general(left_side, right_side, FIRST_DIMS, preferred_element_type=jnp.float32)

def exact_against(left_side, weight):
    return lax.dot_general(left_side, weight.astype(jnp.float32), LAST_DIMS, precision=lax.Precision.HIGHEST, preferred_element_type=jnp.float32)

def exact_cross(left_side, right_side):
    return lax.dot_general(left_side.astype(jnp.float32), right_side, FIRST_DIMS, precision=lax.Precision.HIGHEST, preferred_element_type=jnp.float32)

def reference(latents, ref_frames, windows, quant_level, quant_scale, shared_proj, value_proj, output_proj, conv_taps, cotangent):
    frames = latents.shape[0]
    width = latents.shape[2]
    flat_rows = latents.reshape(-1, width)
    queries = jnp.dot(flat_rows, shared_proj, preferred_element_type=jnp.float32).astype(jnp.bfloat16)
    value_rows = jnp.dot(flat_rows, value_proj, preferred_element_type=jnp.float32).astype(jnp.bfloat16)
    query_grid = queries.reshape(frames, HROWS, COLS, width)
    value_grid = value_rows.reshape(frames, HROWS, COLS, width)
    margins = ((0, 0), (WMAX, WMAX), (0, 0), (0, 0))
    query_pad = jnp.pad(query_grid, margins)
    value_pad = jnp.pad(value_grid, margins)
    key_span = QROWS + 2 * WMAX
    ext_rows = HROWS + 2 * WMAX
    block_ids = jnp.arange(HROWS // QROWS, dtype=jnp.int32)

    def gather_slots(frame):
        ref_pair = ref_frames[frame]
        keys = jnp.stack([query_pad[ref_pair[0]], query_pad[ref_pair[1]]])
        values = jnp.stack([value_pad[ref_pair[0]], value_pad[ref_pair[1]]])
        return (keys, values)

    def block_parts(frame, keys, values, block):
        begin_row = block * QROWS
        query = lax.dynamic_slice_in_dim(query_grid[frame], begin_row, QROWS, 0).reshape(-1, width)
        key_block = lax.dynamic_slice_in_dim(keys, begin_row, key_span, 1).reshape(-1, width)
        value_block = lax.dynamic_slice_in_dim(values, begin_row, key_span, 1).reshape(-1, width)
        allowed = allowed_mask(begin_row, windows[frame], HROWS)
        return (query, key_block, value_block, allowed)

    def frame_forward(frame):
        keys, values = gather_slots(frame)

        def one_block(block):
            query, key_block, value_block, allowed = block_parts(frame, keys, values, block)
            return block_forward(query, key_block, value_block, allowed)
        return lax.map(one_block, block_ids).reshape(HROWS * COLS, width)
    mixed_rows = lax.map(frame_forward, jnp.arange(frames, dtype=jnp.int32)).reshape(-1, width)
    residual = flat_rows.astype(jnp.float32) + jnp.dot(mixed_rows, output_proj, preferred_element_type=jnp.float32)
    hidden = residual.astype(jnp.bfloat16).reshape(frames, HROWS, COLS, width)
    hidden_pad = jnp.pad(hidden, ((0, 0), (1, 1), (0, 0), (0, 0)))
    context = jnp.zeros_like(residual)
    for tap_shift in (-1, 0, 1):
        shifted = hidden_pad[:, 1 + tap_shift:1 + tap_shift + HROWS].reshape(-1, width)
        context = context + jnp.dot(shifted, conv_taps[tap_shift + 1], preferred_element_type=jnp.float32)
    gain_rows = quant_scale[quant_level]
    coded_latent = ((residual + context).reshape(frames, -1, width) * gain_rows[:, None, :]).astype(jnp.bfloat16)
    grad_z = cotangent.astype(jnp.float32) * gain_rows[:, None, :]
    grad_zb = grad_z.astype(jnp.bfloat16)
    grad_pad = jnp.pad(grad_zb.reshape(frames, HROWS, COLS, width), ((0, 0), (1, 1), (0, 0), (0, 0)))
    grad_resid = grad_z.reshape(-1, width)
    for tap_shift in (-1, 0, 1):
        shifted = grad_pad[:, 1 - tap_shift:1 - tap_shift + HROWS].reshape(-1, width)
        grad_resid = grad_resid + against(shifted, conv_taps[tap_shift + 1])
    grad_rb = grad_resid.astype(jnp.bfloat16)
    grad_mixed = against(grad_rb, output_proj).astype(jnp.bfloat16).reshape(frames, HROWS, COLS, width)
    zero_sums = jnp.zeros((frames, ext_rows, COLS, width), jnp.float32)

    def frame_backward(running, frame):
        key_sums, value_sums = running
        keys, values = gather_slots(frame)

        def one_block(inner_sums, block):
            query_grad, key_grad, value_grad = inner_sums
            query, key_block, value_block, allowed = block_parts(frame, keys, values, block)
            begin_row = block * QROWS
            upstream = lax.dynamic_slice_in_dim(grad_mixed[frame], begin_row, QROWS, 0).reshape(-1, width)
            block_query, block_key, block_value = block_backward(query, key_block, value_block, allowed, upstream)
            query_grad = lax.dynamic_update_slice_in_dim(query_grad, block_query.reshape(QROWS, COLS, width), begin_row, 0)
            key_grad = add_window(key_grad, block_key.reshape(2, key_span, COLS, width), begin_row)
            value_grad = add_window(value_grad, block_value.reshape(2, key_span, COLS, width), begin_row)
            return ((query_grad, key_grad, value_grad), None)
        initial = (jnp.zeros((HROWS, COLS, width), jnp.float32), jnp.zeros((2, ext_rows, COLS, width), jnp.float32), jnp.zeros((2, ext_rows, COLS, width), jnp.float32))
        (query_grad, key_grad, value_grad), _ = lax.scan(one_block, initial, block_ids)
        ref_pair = ref_frames[frame]
        key_sums = key_sums.at[ref_pair[0]].add(key_grad[0]).at[ref_pair[1]].add(key_grad[1])
        value_sums = value_sums.at[ref_pair[0]].add(value_grad[0]).at[ref_pair[1]].add(value_grad[1])
        return ((key_sums, value_sums), query_grad)
    (key_sums, value_sums), query_grads = lax.scan(frame_backward, (zero_sums, zero_sums), jnp.arange(frames, dtype=jnp.int32))
    grad_proj = (query_grads + key_sums[:, WMAX:WMAX + HROWS]).reshape(-1, width)
    grad_vals = value_sums[:, WMAX:WMAX + HROWS].reshape(-1, width)
    grad_latents = grad_resid + exact_against(grad_proj, shared_proj) + exact_against(grad_vals, value_proj)
    grad_latents = grad_latents.astype(jnp.bfloat16).reshape(frames, -1, width)
    norm_scale = 1.0 / math.sqrt(frames * HROWS * COLS)
    grad_shared = exact_cross(flat_rows, grad_proj) * norm_scale
    grad_values = exact_cross(flat_rows, grad_vals) * norm_scale
    grad_output = cross_rows(mixed_rows, grad_rb) * norm_scale
    flat_grad = grad_zb.reshape(-1, width)
    grad_taps = jnp.stack([cross_rows(hidden_pad[:, 1 + tap_shift:1 + tap_shift + HROWS].reshape(-1, width), flat_grad) for tap_shift in (-1, 0, 1)]) * norm_scale
    return (coded_latent, grad_latents, grad_shared, grad_values, grad_output, grad_taps)
```

```python
import functools
import math

import jax
import jax.numpy as jnp
from jax import lax
from jax.experimental import pallas as pl
from jax.experimental.pallas import tpu as pltpu
from jax.sharding import PartitionSpec as P

HEADS = 8
DH = 32
COLS = 64
WMAX = 2
BROWS = 2

SCALE = 1.5 / math.sqrt(DH)
MASKED = -1e30
F32 = jnp.float32
BF16 = jnp.bfloat16
NN = (((1,), (0,)), ((), ()))
NT = (((1,), (1,)), ((), ()))


def dot(left, right, dims=NN):
    return lax.dot_general(left, right, dims, preferred_element_type=F32)


def halves_of(value):
    high = value.astype(BF16)
    return high, (value - high.astype(F32)).astype(BF16)


def left_split_dot(left, right, dims=NN):
    high, low = halves_of(left)
    return dot(high, right, dims) + dot(low, right, dims)


def right_split_dot(left, right, dims=NN):
    high, low = halves_of(right)
    return dot(left, high, dims) + dot(left, low, dims)


def shifted(array, by):
    devices = lax.axis_size("frame")
    pairs = [(i, i + by) for i in range(devices) if 0 <= i + by < devices]
    return lax.ppermute(array, "frame", pairs)


def swapped(array, axis, mask):
    pairs = [(i, i ^ mask) for i in range(lax.axis_size(axis))]
    return lax.ppermute(array, axis, pairs)


def whole_call(body, outs, args, smem=(), scratch=(), grid=None, flops=0, moved=0, name=None):
    specs = [
        pl.BlockSpec(memory_space=pltpu.SMEM if i in smem else pltpu.VMEM)
        for i in range(len(args))
    ]
    more = {} if grid is None else {"grid": grid}
    return pl.pallas_call(
        body,
        out_shape=[jax.ShapeDtypeStruct(shape, dtype) for shape, dtype in outs],
        in_specs=specs,
        out_specs=[pl.BlockSpec(memory_space=pltpu.VMEM)] * len(outs),
        scratch_shapes=list(scratch),
        compiler_params=pltpu.CompilerParams(vmem_limit_bytes=48 * 1024 * 1024),
        cost_estimate=pl.CostEstimate(flops=flops, bytes_accessed=moved, transcendentals=0),
        name=name,
        **more,
    )(*args)


def before_kernel(
    meta, cot, gain, edge, tokens, taps, shared, outp,
    resid_out, rb_out, ext_out, up_out, upt_out, query_out, queryt_out,
):
    row_id = meta[2]
    count = cot.shape[0]
    grad_z = cot[...].astype(F32) * gain[...]
    got = edge[...]
    none = jnp.zeros_like(got)
    ext_out[:COLS] = jnp.where(row_id == 0, none, got)
    ext_out[COLS : COLS + count] = grad_z.astype(BF16)
    ext_out[COLS + count :] = jnp.where(row_id == 0, got, none)
    total = grad_z
    for tap in range(3):
        begin = (2 - tap) * COLS
        total = total + dot(ext_out[begin : begin + count], taps[tap], NT)
    resid_out[...] = total
    rounded = total.astype(BF16)
    rb_out[...] = rounded
    upstream = dot(rounded, outp[...], NT).astype(BF16)
    up_out[...] = upstream
    upt_out[...] = upstream.T
    query = dot(tokens[...], shared[...]).astype(BF16)
    query_out[...] = query
    queryt_out[...] = query.T


def attention_kernel(
    meta, slots, halo, query, queryt, up, upt, tokens, rb, ext, resid_grad, shared, value, outp,
    mid_out, edge_out, hidden_out, resid_out, base_out, weights_out,
    key_all, val_all, key_blk, val_blk, bias, mixed_all, dq_all, dkt, dvt,
):
    step = pl.program_id(0)
    window, row_id, total_rows = meta[1], meta[2], meta[3]
    width = query.shape[1]
    count = query.shape[0]
    rim = WMAX * COLS
    ext_count = count + 2 * rim
    block = BROWS * COLS
    span = block + 2 * rim

    @pl.when(step == 0)
    def _():
        for slot in range(2):
            for weight, full in ((shared, key_all), (value, val_all)):
                full[slot, rim : rim + count] = dot(slots[slot], weight[...]).astype(BF16)
                far = dot(halo[slot], weight[...]).astype(BF16)
                none = jnp.zeros_like(far)
                full[slot, :rim] = jnp.where(row_id == 0, none, far)
                full[slot, rim + count :] = jnp.where(row_id == 0, far, none)
        dkt[...] = jnp.zeros_like(dkt)
        dvt[...] = jnp.zeros_like(dvt)

    begin = pl.multiple_of(step * block, block)
    for slot in range(2):
        key_blk[slot * span : (slot + 1) * span] = key_all[slot, pl.ds(begin, span)]
        val_blk[slot * span : (slot + 1) * span] = val_all[slot, pl.ds(begin, span)]
    first_row = row_id * (count // COLS) + step * BROWS
    query_row = first_row + lax.broadcasted_iota(jnp.int32, (block, span), 0) // COLS
    key_row = first_row - WMAX + lax.broadcasted_iota(jnp.int32, (block, span), 1) // COLS
    near = jnp.abs(query_row - key_row) <= window
    allowed = near & (key_row >= 0) & (key_row < total_rows)
    one_bias = jnp.where(allowed, 0.0, MASKED)
    bias[:, :span] = one_bias
    bias[:, span:] = one_bias

    query_b = query[pl.ds(begin, block), :]
    up_b = up[pl.ds(begin, block), :]
    lane_head = lax.broadcasted_iota(jnp.int32, (1, width), 1) // DH
    mixed = jnp.zeros((block, width), F32)
    grad_q = jnp.zeros((block, width), F32)
    for head in range(HEADS):
        mask = (lane_head == head).astype(F32)
        mask_b = mask.astype(BF16)
        scores = dot(query_b * mask_b, key_blk[...], NT) * SCALE + bias[...]
        top = jnp.max(scores, axis=1, keepdims=True)
        terms = jnp.exp(scores - top)
        weights = terms * (1.0 / jnp.sum(terms, axis=1, keepdims=True))
        prob = weights.astype(BF16)
        mixed = mixed + dot(prob, val_blk[...]) * mask
        grad_prob = dot(up_b * mask_b, val_blk[...], NT)
        weighted = weights * grad_prob
        inner = jnp.sum(weighted, axis=1, keepdims=True)
        grad_score = ((weights * (grad_prob - inner)) * SCALE).astype(BF16)
        grad_q = grad_q + dot(grad_score, key_blk[...]) * mask
        lanes = slice(head * DH, (head + 1) * DH)
        up_h = upt[lanes, pl.ds(begin, block)]
        query_h = queryt[lanes, pl.ds(begin, block)]
        dv = dot(up_h, prob)
        dk = dot(query_h, grad_score)
        for slot in range(2):
            dvt[slot, lanes, pl.ds(begin, span)] += dv[:, slot * span : (slot + 1) * span]
            dkt[slot, lanes, pl.ds(begin, span)] += dk[:, slot * span : (slot + 1) * span]
    mixed_all[pl.ds(begin, block), :] = mixed.astype(BF16)
    dq_all[pl.ds(begin, block), :] = grad_q

    @pl.when(step == pl.num_programs(0) - 1)
    def _():
        mixed_full = mixed_all[...]
        residual = tokens[...].astype(F32) + dot(mixed_full, outp[...])
        resid_out[...] = residual
        hidden = residual.astype(BF16)
        hidden_out[...] = hidden
        weights_out[2] = dot(mixed_full.T, rb[...])
        hidden_t = hidden.T
        for tap in range(3):
            start = (2 - tap) * COLS
            weights_out[3 + tap] = dot(hidden_t, ext[start : start + count])
        grad_q_full = dq_all[...]
        base_out[...] = resid_grad[...] + left_split_dot(grad_q_full, shared[...], NT)
        shared_grad = right_split_dot(tokens[...].T, grad_q_full)
        shared_t = jnp.zeros((width, width), F32)
        value_t = jnp.zeros((width, width), F32)
        for slot in range(2):
            key_high, key_low = halves_of(dkt[slot])
            val_high, val_low = halves_of(dvt[slot])
            part = (
                dot(shared[...], key_high)
                + dot(shared[...], key_low)
                + dot(value[...], val_high)
                + dot(value[...], val_low)
            )
            mid_out[slot] = part[:, rim : rim + count]
            edge_out[slot] = jnp.where(
                row_id == 0, part[:, rim + count :], part[:, :rim]
            ).astype(BF16)
            middle = slice(rim, rim + count)
            for high_low in (key_high, key_low):
                rims = jnp.where(
                    row_id == 0,
                    high_low[:, rim + count :].astype(F32),
                    high_low[:, :rim].astype(F32),
                ).astype(BF16)
                shared_t += dot(high_low[:, middle], slots[slot]) + dot(rims, halo[slot])
            for high_low in (val_high, val_low):
                rims = jnp.where(
                    row_id == 0,
                    high_low[:, rim + count :].astype(F32),
                    high_low[:, :rim].astype(F32),
                ).astype(BF16)
                value_t += dot(high_low[:, middle], slots[slot]) + dot(rims, halo[slot])
        weights_out[0] = shared_grad + shared_t.T
        weights_out[1] = value_t.T


def coded_kernel(meta, hidden, halo, residual, gain, taps, coded_out, ext):
    row_id = meta[2]
    count = hidden.shape[0]
    got = halo[...]
    none = jnp.zeros_like(got)
    ext[:COLS] = jnp.where(row_id == 0, none, got)
    ext[COLS : COLS + count] = hidden[...]
    ext[COLS + count :] = jnp.where(row_id == 0, got, none)
    total = jnp.zeros((count, hidden.shape[1]), F32)
    for tap in range(3):
        begin = tap * COLS
        total = total + dot(ext[begin : begin + count], taps[tap])
    coded_out[...] = ((residual[...] + total) * gain[...]).astype(BF16)


def final_kernel(base, first, second, third, grad_out):
    returned = first[...].astype(F32) + second[...].astype(F32) + third[...].astype(F32)
    grad_out[...] = (base[...] + returned.T).astype(BF16)


def summed_over(value, stages, direct):
    row_of = {axis: lax.axis_index(axis) for axis in ("frame", "row")}
    for axis, mask in stages:
        bit = (row_of[axis] & mask) != 0
        half = value.shape[0] // 2
        low, high = value[:half], value[half:]
        got = swapped(jnp.where(bit, low, high).astype(BF16), axis, mask)
        value = jnp.where(bit, high, low) + got.astype(F32)
    own = value.astype(BF16)
    level = [own] + [swapped(own, "frame", mask) for mask in direct]
    level = [part.astype(F32) for part in level]
    while len(level) > 1:
        level = [level[i] + level[i + 1] for i in range(0, len(level), 2)]
    value = level[0].astype(BF16)
    for axis, mask in stages[::-1]:
        bit = (row_of[axis] & mask) != 0
        got = swapped(value, axis, mask)
        value = jnp.concatenate([jnp.where(bit, got, value), jnp.where(bit, value, got)], 0)
    return value


def local(
    latents, ref_frames, windows, quant_level, quant_scale,
    shared_proj, value_proj, output_proj, conv_taps, cotangent,
):
    width = latents.shape[2]
    count = latents.shape[1]
    rows_dev = count // COLS
    frames = lax.axis_size("frame")
    total_rows = rows_dev * lax.axis_size("row")
    frame_id = lax.axis_index("frame")
    row_id = lax.axis_index("row")
    refs = ref_frames[0]
    odd = (frame_id & 1) == 1
    rim = WMAX * COLS
    tokens = latents[0]
    meta = jnp.stack(
        [frame_id, windows[0], row_id, jnp.int32(total_rows)]
    ).astype(jnp.int32)
    gain = lax.dynamic_slice_in_dim(quant_scale, quant_level[0], 1, 0)

    from_before = shifted(tokens, 2)
    from_after = shifted(tokens, -2)
    from_pair = swapped(tokens, "frame", 1)

    cot = cotangent[0]
    cot_edge = jnp.where(row_id == 0, cot[count - COLS :], cot[:COLS])
    grad_edge = swapped((cot_edge.astype(F32) * gain).astype(BF16), "row", 1)
    grad_resid, grad_rb, grad_ext, up, upt, query, queryt = whole_call(
        before_kernel,
        [
            ((count, width), F32),
            ((count, width), BF16),
            ((count + 2 * COLS, width), BF16),
            ((count, width), BF16),
            ((width, count), BF16),
            ((count, width), BF16),
            ((width, count), BF16),
        ],
        (meta, cot, gain, grad_edge, tokens, conv_taps, shared_proj, output_proj),
        smem=(0,),
        flops=2 * 5 * count * width * width,
        moved=4 * count * width * 6,
        name="gradient_path",
    )

    from_before_2 = shifted(from_before, 2)
    from_after_2 = shifted(from_after, -2)
    from_cross = swapped(jnp.where(odd, from_before, from_after), "frame", 1)
    pair_step = jnp.where(odd, -1, 1)
    distance = (refs - frame_id)[:, None, None]
    slots = jnp.where(distance == pair_step, from_pair[None], from_cross[None])
    for step, source in (
        (-2, from_before), (2, from_after), (-4, from_before_2), (4, from_after_2)
    ):
        slots = jnp.where(distance == step, source[None], slots)
    halo = swapped(jnp.where(row_id == 0, slots[:, count - rim :], slots[:, :rim]), "row", 1)

    block = BROWS * COLS
    span = block + 2 * rim
    ext_count = count + 2 * rim
    mid, edge, hidden, residual, base, weight_grads = whole_call(
        attention_kernel,
        [
            ((2, width, count), F32),
            ((2, width, rim), BF16),
            ((count, width), BF16),
            ((count, width), F32),
            ((count, width), F32),
            ((6, width, width), F32),
        ],
        (
            meta, slots, halo, query, queryt, up, upt, tokens, grad_rb, grad_ext, grad_resid,
            shared_proj, value_proj, output_proj,
        ),
        smem=(0,),
        scratch=[
            pltpu.VMEM((2, ext_count, width), BF16),
            pltpu.VMEM((2, ext_count, width), BF16),
            pltpu.VMEM((2 * span, width), BF16),
            pltpu.VMEM((2 * span, width), BF16),
            pltpu.VMEM((block, 2 * span), F32),
            pltpu.VMEM((count, width), BF16),
            pltpu.VMEM((count, width), F32),
            pltpu.VMEM((2, width, ext_count), F32),
            pltpu.VMEM((2, width, ext_count), F32),
        ],
        grid=(count // block,),
        flops=6 * 2 * count * 2 * span * width * HEADS,
        moved=count * width * 60,
        name="attention",
    )

    hidden_edge = jnp.where(row_id == 0, hidden[count - COLS :], hidden[:COLS])
    hidden_halo = swapped(hidden_edge, "row", 1)
    edge_got = swapped(edge, "row", 1).astype(F32)
    none = jnp.zeros((2, width, count - rim), F32)
    mid = mid + jnp.where(
        row_id == 0,
        jnp.concatenate([none, edge_got], 2),
        jnp.concatenate([edge_got, none], 2),
    )

    def part_for(step):
        return jnp.sum(jnp.where(distance == step, mid, 0.0), axis=0)

    back = shifted(part_for(-4).astype(BF16), -2)
    ahead = shifted(part_for(4).astype(BF16), 2)
    across = swapped(part_for(-pair_step).astype(BF16), "frame", 1).astype(F32)
    third = swapped(part_for(pair_step).astype(BF16), "frame", 1)
    first = shifted(
        (part_for(-2) + back.astype(F32) + jnp.where(odd, across, 0.0)).astype(BF16), -2
    )
    second = shifted(
        (part_for(2) + ahead.astype(F32) + jnp.where(odd, 0.0, across)).astype(BF16), 2
    )

    stages = [("row", 1), ("frame", 1)]
    mask = 2
    while mask * 4 < frames:
        stages.append(("frame", mask))
        mask *= 2
    direct = [mask, 2 * mask, 3 * mask]
    sums = summed_over(weight_grads.reshape(-1, width), stages, direct).astype(F32)
    sums = sums * (1.0 / math.sqrt(frames * total_rows * COLS))
    sums = sums.reshape(6, width, width)

    (coded,) = whole_call(
        coded_kernel,
        [((count, width), BF16)],
        (meta, hidden, hidden_halo, residual, gain, conv_taps),
        smem=(0,),
        scratch=[pltpu.VMEM((count + 2 * COLS, width), BF16)],
        flops=2 * 3 * count * width * width,
        moved=count * width * 8,
        name="context",
    )
    (grad_latents,) = whole_call(
        final_kernel,
        [((count, width), BF16)],
        (base, first, second, third),
        flops=count * width * 4,
        moved=count * width * 12,
        name="latent_gradient",
    )
    return (
        coded[None],
        grad_latents[None],
        sums[0],
        sums[1],
        sums[2],
        sums[3:],
    )


def solution(mesh):
    placed = (
        P(("groups", "frame"), "row", None),
        P(("groups", "frame"), None),
        P(("groups", "frame")),
        P(("groups", "frame")),
        P(),
        P(),
        P(),
        P(),
        P(),
        P(("groups", "frame"), "row", None),
    )
    return jax.shard_map(
        local,
        mesh=mesh,
        in_specs=placed,
        out_specs=(
            P(("groups", "frame"), "row", None),
            P(("groups", "frame"), "row", None),
            P("groups", None),
            P("groups", None),
            P("groups", None),
            P("groups", None, None),
        ),
        check_vma=False,
    )
```

```python
import functools
import math

import jax
import jax.numpy as jnp
from jax import lax
from jax.experimental import pallas as pl
from jax.experimental.pallas import tpu as pltpu
from jax.sharding import PartitionSpec as P

HEADS = 8
DH = 32
COLS = 64
WMAX = 2
BROWS = 2

SCALE = 1.5 / math.sqrt(DH)
MASKED = -1e30
LOG2E = 1.4426950408889634
F32 = jnp.float32
BF16 = jnp.bfloat16
NN = (((1,), (0,)), ((), ()))
NT = (((1,), (1,)), ((), ()))


def dot(left, right, dims=NN):
    return lax.dot_general(left, right, dims, preferred_element_type=F32)


def halves_of(value):
    high = value.astype(BF16)
    return high, (value - high.astype(F32)).astype(BF16)


def left_split_dot(left, right, dims=NN):
    high, low = halves_of(left)
    return dot(high, right, dims) + dot(low, right, dims)


def right_split_dot(left, right, dims=NN):
    high, low = halves_of(right)
    return dot(left, high, dims) + dot(left, low, dims)


def swapped(array, axis, mask):
    pairs = [(i, i ^ mask) for i in range(lax.axis_size(axis))]
    return lax.ppermute(array, axis, pairs)


def along(array, parity):
    devices = lax.axis_size("frame")
    pairs = [(i, i + 2) for i in range(devices) if (i & 2) == parity and i + 2 < devices]
    return lax.ppermute(array, "frame", pairs + [(j, i) for i, j in pairs])


def whole_call(
    body, outs, args, smem=(), scratch=(), grid=None, flops=0, moved=0, name=None, vmem=16
):
    specs = [
        pl.BlockSpec(memory_space=pltpu.SMEM if i in smem else pltpu.VMEM)
        for i in range(len(args))
    ]
    more = {} if grid is None else {"grid": grid}
    return pl.pallas_call(
        body,
        out_shape=[jax.ShapeDtypeStruct(shape, dtype) for shape, dtype in outs],
        in_specs=specs,
        out_specs=[pl.BlockSpec(memory_space=pltpu.VMEM)] * len(outs),
        scratch_shapes=list(scratch),
        compiler_params=pltpu.CompilerParams(vmem_limit_bytes=vmem * 1024 * 1024),
        cost_estimate=pl.CostEstimate(flops=flops, bytes_accessed=moved, transcendentals=0),
        name=name,
        **more,
    )(*args)


def before_kernel(
    meta, cot, gain, edge, tokens, taps, shared, outp,
    resid_out, rb_out, ext_out, up_out, upt_out, query_out, queryt_out,
):
    row_id = meta[2]
    count = cot.shape[0]
    grad_z = cot[...].astype(F32) * gain[...]
    got = edge[...]
    none = jnp.zeros_like(got)
    ext_out[:COLS] = jnp.where(row_id == 0, none, got)
    ext_out[COLS : COLS + count] = grad_z.astype(BF16)
    ext_out[COLS + count :] = jnp.where(row_id == 0, got, none)
    total = grad_z
    for tap in range(3):
        begin = (2 - tap) * COLS
        total = total + dot(ext_out[begin : begin + count], taps[tap], NT)
    resid_out[...] = total
    rounded = total.astype(BF16)
    rb_out[...] = rounded
    upstream = dot(rounded, outp[...], NT).astype(BF16)
    up_out[...] = upstream
    upt_out[...] = upstream.T
    query = dot(tokens[...], shared[...]).astype(BF16)
    query_out[...] = query
    queryt_out[...] = query.T


def attention_kernel(
    meta, slots, halo, query, queryt, up, upt, tokens, rb, ext, resid_grad, shared, value, outp,
    mid_out, send_out, keep_out, hidden_out, resid_out, base_out,
    key_all, val_all, key_blk, val_blk, keyt_blk, valt_blk, bias, mixed_all, dq_all, dkt, dvt, sums,
):
    step = pl.program_id(0)
    window, row_id, total_rows = meta[1], meta[2], meta[3]
    width = query.shape[1]
    count = query.shape[0]
    rim = WMAX * COLS
    block = BROWS * COLS
    span = block + 2 * rim

    @pl.when(step == 0)
    def _():
        for slot in range(2):
            for weight, full in ((shared, key_all), (value, val_all)):
                full[slot, rim : rim + count] = dot(slots[slot], weight[...]).astype(BF16)
                far = dot(halo[slot], weight[...]).astype(BF16)
                none = jnp.zeros_like(far)
                full[slot, :rim] = jnp.where(row_id == 0, none, far)
                full[slot, rim + count :] = jnp.where(row_id == 0, far, none)
        dkt[...] = jnp.zeros_like(dkt)
        dvt[...] = jnp.zeros_like(dvt)

    begin = pl.multiple_of(step * block, block)
    for slot in range(2):
        key_blk[slot * span : (slot + 1) * span] = key_all[slot, pl.ds(begin, span)]
        val_blk[slot * span : (slot + 1) * span] = val_all[slot, pl.ds(begin, span)]
    keyt_blk[...] = key_blk[...].T
    valt_blk[...] = val_blk[...].T
    first_row = row_id * (count // COLS) + step * BROWS
    query_row = first_row + lax.broadcasted_iota(jnp.int32, (block, span), 0) // COLS
    key_row = first_row - WMAX + lax.broadcasted_iota(jnp.int32, (block, span), 1) // COLS
    near = jnp.abs(query_row - key_row) <= window
    allowed = near & (key_row >= 0) & (key_row < total_rows)
    one_bias = jnp.where(allowed, 0.0, MASKED)
    bias[:, :span] = one_bias
    bias[:, span:] = one_bias

    def all_heads(rows):
        return jnp.concatenate([rows * mask.astype(BF16) for mask in masks], 0)

    def own_lanes(stacked):
        total = jnp.zeros((block, width), F32)
        for head, mask in enumerate(masks):
            total = total + stacked[head * block : (head + 1) * block] * mask
        return total

    lane_head = lax.broadcasted_iota(jnp.int32, (1, width), 1) // DH
    masks = [(lane_head == head).astype(F32) for head in range(HEADS)]
    cube = (HEADS, block, 2 * span)
    flat = (HEADS * block, 2 * span)
    scores = dot(all_heads(query[pl.ds(begin, block), :]), keyt_blk[...]).reshape(cube)
    scores = scores + bias[...][None]
    top = jnp.max(scores, axis=2, keepdims=True)
    terms = jnp.exp2((scores - top) * (SCALE * LOG2E))
    weights = terms * (1.0 / jnp.sum(terms, axis=2, keepdims=True))
    prob = weights.astype(BF16)
    mixed_all[pl.ds(begin, block), :] = own_lanes(
        dot(prob.reshape(flat), val_blk[...])
    ).astype(BF16)
    grad_prob = dot(all_heads(up[pl.ds(begin, block), :]), valt_blk[...]).reshape(cube)
    inner = jnp.sum(weights * grad_prob, axis=2, keepdims=True)
    grad_score = ((weights * (grad_prob - inner)) * SCALE).astype(BF16)
    dq_all[pl.ds(begin, block), :] = own_lanes(dot(grad_score.reshape(flat), key_blk[...]))
    for head in range(HEADS):
        lanes = slice(head * DH, (head + 1) * DH)
        dv = dot(upt[lanes, pl.ds(begin, block)], prob[head])
        dk = dot(queryt[lanes, pl.ds(begin, block)], grad_score[head])
        for slot in range(2):
            dvt[slot, lanes, pl.ds(begin, span)] += dv[:, slot * span : (slot + 1) * span]
            dkt[slot, lanes, pl.ds(begin, span)] += dk[:, slot * span : (slot + 1) * span]

    @pl.when(step == pl.num_programs(0) - 1)
    def _():
        def far_rim(array):
            upper, lower = array[:, :rim], array[:, rim + count :]
            return jnp.where(row_id == 0, lower, upper)

        half = 3 * width
        middle = slice(rim, rim + count)
        grad_q = dq_all[...]
        shared_t = jnp.zeros((width, width), F32)
        value_t = jnp.zeros((width, width), F32)
        for slot in range(2):
            part = jnp.zeros((width, count + 2 * rim), F32)
            for piece in halves_of(dkt[slot]):
                part = part + dot(shared[...], piece)
                rims = far_rim(piece)
                shared_t += dot(piece[:, middle], slots[slot]) + dot(rims, halo[slot])
            for piece in halves_of(dvt[slot]):
                part = part + dot(value[...], piece)
                rims = far_rim(piece)
                value_t += dot(piece[:, middle], slots[slot]) + dot(rims, halo[slot])
            mid_out[slot] = part[:, middle]
            send_out[half:, slot * rim : (slot + 1) * rim] = far_rim(part).astype(BF16)
        base_out[...] = resid_grad[...] + left_split_dot(grad_q, shared[...], NT)
        sums[:width] = right_split_dot(tokens[...].T, grad_q) + shared_t.T
        sums[width : 2 * width] = value_t.T
        mixed_full = mixed_all[...]
        residual = tokens[...].astype(F32) + dot(mixed_full, outp[...])
        resid_out[...] = residual
        hidden = residual.astype(BF16)
        hidden_out[...] = hidden
        sums[2 * width : half] = dot(mixed_full.T, rb[...])
        hidden_t = hidden.T
        for tap in range(3):
            start = (2 - tap) * COLS
            sums[half + tap * width : half + (tap + 1) * width] = dot(
                hidden_t, ext[start : start + count]
            )
        keep_out[...] = sums[pl.ds(pl.multiple_of(row_id * half, half), half)]
        send_out[:half] = sums[pl.ds(pl.multiple_of((1 - row_id) * half, half), half)].astype(BF16)


def spread_kernel(
    meta, mid, keep, got,
    pair_out, across_out, first_out, second_out, third_out, first_keep, second_keep, own_out,
):
    frame_id, row_id = meta[0], meta[2]
    steps = [meta[4] - frame_id, meta[5] - frame_id]
    width, count = mid.shape[1], mid.shape[2]
    rim = WMAX * COLS
    half = keep.shape[0]
    piece = half // 4
    parts = []
    for slot in range(2):
        rims = got[half:, slot * rim : (slot + 1) * rim].astype(F32)
        none = jnp.zeros_like(rims)
        part = mid[slot]
        first = part[:, :rim] + jnp.where(row_id == 0, none, rims)
        last = part[:, count - rim :] + jnp.where(row_id == 0, rims, none)
        parts.append(jnp.concatenate([first, part[:, rim : count - rim], last], 1))

    def part_for(step):
        chosen = jnp.zeros((width, count), F32)
        for slot in range(2):
            chosen = chosen + jnp.where(steps[slot] == step, parts[slot], 0.0)
        return chosen

    pair_step = jnp.where((frame_id & 1) == 0, 1, -1)
    link_step = jnp.where((frame_id & 2) == 0, 1, -1)
    pair_out[...] = part_for(pair_step).astype(BF16)
    across_out[:width] = part_for(-pair_step).astype(BF16)
    first_out[:width] = part_for(4 * link_step).astype(BF16)
    second_out[...] = part_for(-4 * link_step).astype(BF16)
    first_keep[...] = part_for(2 * link_step)
    second_keep[...] = part_for(-2 * link_step)
    me = frame_id & 3

    def rows_of(index):
        rows = pl.ds(pl.multiple_of(index * piece, piece), piece)
        return keep[rows] + got[rows].astype(F32)

    own_out[...] = rows_of(me)
    for mask, out, begin in ((1, across_out, width), (2, first_out, width), (3, third_out, 0)):
        rows = rows_of(me ^ mask).astype(BF16)
        out[begin:, :width] = rows[: piece // 2]
        out[begin:, width:] = rows[piece // 2 :]


def coded_kernel(meta, hidden, halo, residual, gain, taps, coded_out, ext):
    row_id = meta[2]
    count = hidden.shape[0]
    got = halo[...]
    none = jnp.zeros_like(got)
    ext[:COLS] = jnp.where(row_id == 0, none, got)
    ext[COLS : COLS + count] = hidden[...]
    ext[COLS + count :] = jnp.where(row_id == 0, got, none)
    total = jnp.zeros((count, hidden.shape[1]), F32)
    for tap in range(3):
        begin = tap * COLS
        total = total + dot(ext[begin : begin + count], taps[tap])
    coded_out[...] = ((residual[...] + total) * gain[...]).astype(BF16)


def final_kernel(base, first, second, third, grad_out):
    returned = first[...].astype(F32) + second[...].astype(F32) + third[...].astype(F32)
    grad_out[...] = (base[...] + returned.T).astype(BF16)


def weights_kernel(meta, own, other, shared_out, value_out, output_out, taps_out, *, norm):
    row_id = meta[2]
    width = shared_out.shape[1]
    low = jnp.where(row_id == 0, own[...].astype(F32), other[...].astype(F32)) * norm
    high = jnp.where(row_id == 0, other[...].astype(F32), own[...].astype(F32)) * norm
    shared_out[...] = low[:width]
    value_out[...] = low[width : 2 * width]
    output_out[...] = low[2 * width :]
    for tap in range(3):
        taps_out[tap] = high[tap * width : (tap + 1) * width]


def local(
    latents, ref_frames, windows, quant_level, quant_scale,
    shared_proj, value_proj, output_proj, conv_taps, cotangent,
):
    width = latents.shape[2]
    count = latents.shape[1]
    rows_dev = count // COLS
    frames = lax.axis_size("frame")
    total_rows = rows_dev * lax.axis_size("row")
    frame_id = lax.axis_index("frame")
    row_id = lax.axis_index("row")
    refs = ref_frames[0]
    odd = (frame_id & 1) == 1
    rim = WMAX * COLS
    tokens = latents[0]
    low_link = (frame_id & 2) == 0
    meta = jnp.concatenate(
        [jnp.stack([frame_id, windows[0], row_id, jnp.int32(total_rows)]).astype(jnp.int32), refs]
    )
    gain = lax.dynamic_slice_in_dim(quant_scale, quant_level[0], 1, 0)

    from_pair = swapped(tokens, "frame", 1)
    from_first = along(tokens, 0)
    from_second = along(tokens, 2)
    from_before = jnp.where(low_link, from_second, from_first)
    from_after = jnp.where(low_link, from_first, from_second)

    cot = cotangent[0]
    cot_edge = jnp.where(row_id == 0, cot[count - COLS :], cot[:COLS])
    grad_edge = swapped((cot_edge.astype(F32) * gain).astype(BF16), "row", 1)
    grad_resid, grad_rb, grad_ext, up, upt, query, queryt = whole_call(
        before_kernel,
        [
            ((count, width), F32),
            ((count, width), BF16),
            ((count + 2 * COLS, width), BF16),
            ((count, width), BF16),
            ((width, count), BF16),
            ((count, width), BF16),
            ((width, count), BF16),
        ],
        (meta, cot, gain, grad_edge, tokens, conv_taps, shared_proj, output_proj),
        smem=(0,),
        flops=2 * 5 * count * width * width,
        moved=4 * count * width * 6,
        name="gradient_path",
    )

    far_first = along(from_second, 0)
    far_second = along(from_first, 2)
    from_cross = swapped(jnp.where(odd, from_before, from_after), "frame", 1)
    from_before_2 = jnp.where(low_link, far_second, far_first)
    from_after_2 = jnp.where(low_link, far_first, far_second)
    pair_step = jnp.where(odd, -1, 1)
    distance = (refs - frame_id)[:, None, None]
    slots = jnp.where(distance == pair_step, from_pair[None], from_cross[None])
    for step, source in (
        (-2, from_before), (2, from_after), (-4, from_before_2), (4, from_after_2)
    ):
        slots = jnp.where(distance == step, source[None], slots)
    halo = swapped(jnp.where(row_id == 0, slots[:, count - rim :], slots[:, :rim]), "row", 1)

    block = BROWS * COLS
    span = block + 2 * rim
    ext_count = count + 2 * rim
    half = 3 * width
    mid, send, keep, hidden, residual, base = whole_call(
        attention_kernel,
        [
            ((2, width, count), F32),
            ((half + width, width), BF16),
            ((half, width), F32),
            ((count, width), BF16),
            ((count, width), F32),
            ((count, width), F32),
        ],
        (
            meta, slots, halo, query, queryt, up, upt, tokens, grad_rb, grad_ext, grad_resid,
            shared_proj, value_proj, output_proj,
        ),
        smem=(0,),
        scratch=[
            pltpu.VMEM((2, ext_count, width), BF16),
            pltpu.VMEM((2, ext_count, width), BF16),
            pltpu.VMEM((2 * span, width), BF16),
            pltpu.VMEM((2 * span, width), BF16),
            pltpu.VMEM((width, 2 * span), BF16),
            pltpu.VMEM((width, 2 * span), BF16),
            pltpu.VMEM((block, 2 * span), F32),
            pltpu.VMEM((count, width), BF16),
            pltpu.VMEM((count, width), F32),
            pltpu.VMEM((2, width, ext_count), F32),
            pltpu.VMEM((2, width, ext_count), F32),
            pltpu.VMEM((2 * half, width), F32),
        ],
        grid=(count // block,),
        flops=6 * 2 * count * 2 * span * width * HEADS,
        moved=count * width * 60,
        name="attention",
        vmem=28,
    )

    got = swapped(send, "row", 1)
    hidden_edge = jnp.where(row_id == 0, hidden[count - COLS :], hidden[:COLS])
    hidden_halo = swapped(hidden_edge, "row", 1)
    piece = half // 4
    packed = piece // 2
    pair, across, first, second, third, first_keep, second_keep, own = whole_call(
        spread_kernel,
        [
            ((width, count), BF16),
            ((width + packed, count), BF16),
            ((width + packed, count), BF16),
            ((width, count), BF16),
            ((packed, count), BF16),
            ((width, count), F32),
            ((width, count), F32),
            ((piece, width), F32),
        ],
        (meta, mid, keep, got),
        smem=(0,),
        flops=count * width * 12,
        moved=count * width * 30,
        name="spread",
    )

    across = swapped(across, "frame", 1)
    first = along(first, 0)
    second = along(second, 2)
    third = swapped(third, "frame", 3)

    def unpacked(array):
        return jnp.concatenate([array[:, :width], array[:, width:]], 0).astype(F32)

    total = (own + unpacked(across[width:])) + (unpacked(first[width:]) + unpacked(third))
    mask = 4
    while mask < frames:
        total = total.astype(BF16)
        total = total.astype(F32) + swapped(total, "frame", mask).astype(F32)
        mask *= 2
    own = total.astype(BF16)

    back_pair = swapped(pair, "frame", 1)
    crossing = across[:width].astype(F32)
    with_first = odd != low_link
    back_first = along(
        (first_keep + second.astype(F32) + jnp.where(with_first, crossing, 0.0)).astype(BF16), 0
    )
    back_second = along(
        (second_keep + first[:width].astype(F32) + jnp.where(with_first, 0.0, crossing)).astype(
            BF16
        ),
        2,
    )

    me = frame_id & 3
    pieces = jnp.zeros((4, piece, width), BF16)
    pieces = lax.dynamic_update_index_in_dim(pieces, own, me, 0)
    for mask in (1, 2, 3):
        pieces = lax.dynamic_update_index_in_dim(
            pieces, swapped(own, "frame", mask), me ^ mask, 0
        )
    pieces = pieces.reshape(half, width)
    other = swapped(pieces, "row", 1)
    shared_grad, value_grad, output_grad, taps_grad = whole_call(
        functools.partial(
            weights_kernel, norm=1.0 / math.sqrt(frames * total_rows * COLS)
        ),
        [
            ((width, width), F32),
            ((width, width), F32),
            ((width, width), F32),
            ((3, width, width), F32),
        ],
        (meta, pieces, other),
        smem=(0,),
        flops=6 * width * width,
        moved=6 * width * width * 6,
        name="weight_gradients",
    )

    (coded,) = whole_call(
        coded_kernel,
        [((count, width), BF16)],
        (meta, hidden, hidden_halo, residual, gain, conv_taps),
        smem=(0,),
        scratch=[pltpu.VMEM((count + 2 * COLS, width), BF16)],
        flops=2 * 3 * count * width * width,
        moved=count * width * 8,
        name="context",
    )
    (grad_latents,) = whole_call(
        final_kernel,
        [((count, width), BF16)],
        (base, back_first, back_second, back_pair),
        flops=count * width * 4,
        moved=count * width * 12,
        name="latent_gradient",
    )
    return (
        coded[None],
        grad_latents[None],
        shared_grad,
        value_grad,
        output_grad,
        taps_grad,
    )


def solution(mesh):
    placed = (
        P(("groups", "frame"), "row", None),
        P(("groups", "frame"), None),
        P(("groups", "frame")),
        P(("groups", "frame")),
        P(),
        P(),
        P(),
        P(),
        P(),
        P(("groups", "frame"), "row", None),
    )
    return jax.shard_map(
        local,
        mesh=mesh,
        in_specs=placed,
        out_specs=(
            P(("groups", "frame"), "row", None),
            P(("groups", "frame"), "row", None),
            P("groups", None),
            P("groups", None),
            P("groups", None),
            P("groups", None, None),
        ),
        check_vma=False,
    )
```

```python
import functools
import math

import jax
import jax.numpy as jnp
from jax import lax
from jax.experimental import pallas as pl
from jax.experimental.pallas import tpu as pltpu
from jax.sharding import PartitionSpec as P

HEADS = 8
DH = 32
COLS = 64
WMAX = 2
BROWS = 2

SCALE = 1.5 / math.sqrt(DH)
MASKED = -1e30
LOG2E = 1.4426950408889634
F32 = jnp.float32
BF16 = jnp.bfloat16
NN = (((1,), (0,)), ((), ()))
NT = (((1,), (1,)), ((), ()))


def dot(left, right, dims=NN):
    return lax.dot_general(left, right, dims, preferred_element_type=F32)


def halves_of(value):
    high = value.astype(BF16)
    return high, (value - high.astype(F32)).astype(BF16)


def left_split_dot(left, right, dims=NN):
    high, low = halves_of(left)
    return dot(high, right, dims) + dot(low, right, dims)


def right_split_dot(left, right, dims=NN):
    high, low = halves_of(right)
    return dot(left, high, dims) + dot(left, low, dims)


def swapped(array, axis, mask):
    pairs = [(i, i ^ mask) for i in range(lax.axis_size(axis))]
    return lax.ppermute(array, axis, pairs)


def along(array, parity):
    devices = lax.axis_size("frame")
    pairs = [(i, i + 2) for i in range(devices) if (i & 2) == parity and i + 2 < devices]
    return lax.ppermute(array, "frame", pairs + [(j, i) for i, j in pairs])


def whole_call(
    body, outs, args, smem=(), scratch=(), grid=None, flops=0, moved=0, name=None, vmem=16
):
    specs = [
        pl.BlockSpec(memory_space=pltpu.SMEM if i in smem else pltpu.VMEM)
        for i in range(len(args))
    ]
    more = {} if grid is None else {"grid": grid}
    return pl.pallas_call(
        body,
        out_shape=[jax.ShapeDtypeStruct(shape, dtype) for shape, dtype in outs],
        in_specs=specs,
        out_specs=[pl.BlockSpec(memory_space=pltpu.VMEM)] * len(outs),
        scratch_shapes=list(scratch),
        compiler_params=pltpu.CompilerParams(vmem_limit_bytes=vmem * 1024 * 1024),
        cost_estimate=pl.CostEstimate(flops=flops, bytes_accessed=moved, transcendentals=0),
        name=name,
        **more,
    )(*args)


def before_kernel(
    meta, cot, gain, edge, tokens, taps, shared, outp,
    resid_out, rb_out, ext_out, up_out, upt_out, query_out, queryt_out,
):
    row_id = meta[2]
    count = cot.shape[0]
    grad_z = cot[...].astype(F32) * gain[...]
    got = edge[...]
    none = jnp.zeros_like(got)
    ext_out[:COLS] = jnp.where(row_id == 0, none, got)
    ext_out[COLS : COLS + count] = grad_z.astype(BF16)
    ext_out[COLS + count :] = jnp.where(row_id == 0, got, none)
    total = grad_z
    for tap in range(3):
        begin = (2 - tap) * COLS
        total = total + dot(ext_out[begin : begin + count], taps[tap], NT)
    resid_out[...] = total
    rounded = total.astype(BF16)
    rb_out[...] = rounded
    upstream = dot(rounded, outp[...], NT).astype(BF16)
    up_out[...] = upstream
    upt_out[...] = upstream.T
    query = dot(tokens[...], shared[...]).astype(BF16)
    query_out[...] = query
    queryt_out[...] = query.T


def attention_kernel(
    meta, slots, halo, query, queryt, up, upt, tokens, rb, ext, resid_grad, shared, value, outp,
    mid_out, send_out, keep_out, hidden_out, resid_out, base_out,
    key_all, val_all, key_blk, val_blk, keyt_blk, valt_blk, bias, mixed_all, dq_all, dkt, dvt, sums,
):
    step = pl.program_id(0)
    window, row_id, total_rows = meta[1], meta[2], meta[3]
    width = query.shape[1]
    count = query.shape[0]
    rim = WMAX * COLS
    block = BROWS * COLS
    span = block + 2 * rim

    @pl.when(step == 0)
    def _():
        for slot in range(2):
            for weight, full in ((shared, key_all), (value, val_all)):
                full[slot, rim : rim + count] = dot(slots[slot], weight[...]).astype(BF16)
                far = dot(halo[slot], weight[...]).astype(BF16)
                none = jnp.zeros_like(far)
                full[slot, :rim] = jnp.where(row_id == 0, none, far)
                full[slot, rim + count :] = jnp.where(row_id == 0, far, none)
        dkt[...] = jnp.zeros_like(dkt)
        dvt[...] = jnp.zeros_like(dvt)

    begin = pl.multiple_of(step * block, block)
    for slot in range(2):
        key_blk[slot * span : (slot + 1) * span] = key_all[slot, pl.ds(begin, span)]
        val_blk[slot * span : (slot + 1) * span] = val_all[slot, pl.ds(begin, span)]
    keyt_blk[...] = key_blk[...].T
    valt_blk[...] = val_blk[...].T
    first_row = row_id * (count // COLS) + step * BROWS
    query_row = first_row + lax.broadcasted_iota(jnp.int32, (block, span), 0) // COLS
    key_row = first_row - WMAX + lax.broadcasted_iota(jnp.int32, (block, span), 1) // COLS
    near = jnp.abs(query_row - key_row) <= window
    allowed = near & (key_row >= 0) & (key_row < total_rows)
    one_bias = jnp.where(allowed, 0.0, MASKED)
    bias[:, :span] = one_bias
    bias[:, span:] = one_bias

    def all_heads(rows):
        return jnp.concatenate([rows * mask.astype(BF16) for mask in masks], 0)

    def own_lanes(stacked):
        total = jnp.zeros((block, width), F32)
        for head, mask in enumerate(masks):
            total = total + stacked[head * block : (head + 1) * block] * mask
        return total

    lane_head = lax.broadcasted_iota(jnp.int32, (1, width), 1) // DH
    masks = [(lane_head == head).astype(F32) for head in range(HEADS)]
    cube = (HEADS, block, 2 * span)
    flat = (HEADS * block, 2 * span)
    scores = dot(all_heads(query[pl.ds(begin, block), :]), keyt_blk[...]).reshape(cube)
    scores = scores + bias[...][None]
    top = jnp.max(scores, axis=2, keepdims=True)
    terms = jnp.exp2((scores - top) * (SCALE * LOG2E))
    weights = terms * (1.0 / jnp.sum(terms, axis=2, keepdims=True))
    prob = weights.astype(BF16)
    mixed_all[pl.ds(begin, block), :] = own_lanes(
        dot(prob.reshape(flat), val_blk[...])
    ).astype(BF16)
    grad_prob = dot(all_heads(up[pl.ds(begin, block), :]), valt_blk[...]).reshape(cube)
    inner = jnp.sum(weights * grad_prob, axis=2, keepdims=True)
    grad_score = ((weights * (grad_prob - inner)) * SCALE).astype(BF16)
    dq_all[pl.ds(begin, block), :] = own_lanes(dot(grad_score.reshape(flat), key_blk[...]))
    for head in range(HEADS):
        lanes = slice(head * DH, (head + 1) * DH)
        dv = dot(upt[lanes, pl.ds(begin, block)], prob[head])
        dk = dot(queryt[lanes, pl.ds(begin, block)], grad_score[head])
        for slot in range(2):
            dvt[slot, lanes, pl.ds(begin, span)] += dv[:, slot * span : (slot + 1) * span]
            dkt[slot, lanes, pl.ds(begin, span)] += dk[:, slot * span : (slot + 1) * span]

    @pl.when(step == pl.num_programs(0) - 1)
    def _():
        def far_rim(array):
            upper, lower = array[:, :rim], array[:, rim + count :]
            return jnp.where(row_id == 0, lower, upper)

        half = 3 * width
        middle = slice(rim, rim + count)
        grad_q = dq_all[...]
        shared_t = jnp.zeros((width, width), F32)
        value_t = jnp.zeros((width, width), F32)
        for slot in range(2):
            part = jnp.zeros((width, count + 2 * rim), F32)
            for piece in halves_of(dkt[slot]):
                part = part + dot(shared[...], piece)
                rims = far_rim(piece)
                shared_t += dot(piece[:, middle], slots[slot]) + dot(rims, halo[slot])
            for piece in halves_of(dvt[slot]):
                part = part + dot(value[...], piece)
                rims = far_rim(piece)
                value_t += dot(piece[:, middle], slots[slot]) + dot(rims, halo[slot])
            mid_out[slot] = part[:, middle]
            send_out[half:, slot * rim : (slot + 1) * rim] = far_rim(part).astype(BF16)
        base_out[...] = resid_grad[...] + left_split_dot(grad_q, shared[...], NT)
        sums[:width] = right_split_dot(tokens[...].T, grad_q) + shared_t.T
        sums[width : 2 * width] = value_t.T
        mixed_full = mixed_all[...]
        residual = tokens[...].astype(F32) + dot(mixed_full, outp[...])
        resid_out[...] = residual
        hidden = residual.astype(BF16)
        hidden_out[...] = hidden
        sums[2 * width : half] = dot(mixed_full.T, rb[...])
        hidden_t = hidden.T
        for tap in range(3):
            start = (2 - tap) * COLS
            sums[half + tap * width : half + (tap + 1) * width] = dot(
                hidden_t, ext[start : start + count]
            )
        keep_out[...] = sums[pl.ds(pl.multiple_of(row_id * half, half), half)]
        send_out[:half] = sums[pl.ds(pl.multiple_of((1 - row_id) * half, half), half)].astype(BF16)


def spread_kernel(
    meta, mid, keep, got,
    pair_out, across_out, first_out, second_out, third_out, first_keep, second_keep, own_out,
):
    frame_id, row_id = meta[0], meta[2]
    steps = [meta[4] - frame_id, meta[5] - frame_id]
    width, count = mid.shape[1], mid.shape[2]
    rim = WMAX * COLS
    half = keep.shape[0]
    piece = half // 4
    parts = []
    for slot in range(2):
        rims = got[half:, slot * rim : (slot + 1) * rim].astype(F32)
        none = jnp.zeros_like(rims)
        part = mid[slot]
        first = part[:, :rim] + jnp.where(row_id == 0, none, rims)
        last = part[:, count - rim :] + jnp.where(row_id == 0, rims, none)
        parts.append(jnp.concatenate([first, part[:, rim : count - rim], last], 1))

    def part_for(step):
        chosen = jnp.zeros((width, count), F32)
        for slot in range(2):
            chosen = chosen + jnp.where(steps[slot] == step, parts[slot], 0.0)
        return chosen

    pair_step = jnp.where((frame_id & 1) == 0, 1, -1)
    link_step = jnp.where((frame_id & 2) == 0, 1, -1)
    pair_out[...] = part_for(pair_step).astype(BF16)
    across_out[:width] = part_for(-pair_step).astype(BF16)
    first_out[:width] = part_for(4 * link_step).astype(BF16)
    second_out[...] = part_for(-4 * link_step).astype(BF16)
    first_keep[...] = part_for(2 * link_step)
    second_keep[...] = part_for(-2 * link_step)
    me = frame_id & 3

    def rows_of(index):
        rows = pl.ds(pl.multiple_of(index * piece, piece), piece)
        return keep[rows] + got[rows].astype(F32)

    own_out[...] = rows_of(me)
    for mask, out, begin in ((1, across_out, width), (2, first_out, width), (3, third_out, 0)):
        rows = rows_of(me ^ mask).astype(BF16)
        out[begin:, :width] = rows[: piece // 2]
        out[begin:, width:] = rows[piece // 2 :]


def coded_kernel(meta, hidden, halo, residual, gain, taps, coded_out, ext):
    row_id = meta[2]
    count = hidden.shape[0]
    got = halo[...]
    none = jnp.zeros_like(got)
    ext[:COLS] = jnp.where(row_id == 0, none, got)
    ext[COLS : COLS + count] = hidden[...]
    ext[COLS + count :] = jnp.where(row_id == 0, got, none)
    total = jnp.zeros((count, hidden.shape[1]), F32)
    for tap in range(3):
        begin = tap * COLS
        total = total + dot(ext[begin : begin + count], taps[tap])
    coded_out[...] = ((residual[...] + total) * gain[...]).astype(BF16)


def select_kernel(meta, pair, cross, first, second, far_first, far_second, _, slots_out, edge_out):
    frame_id, row_id = meta[0], meta[2]
    count = pair.shape[0]
    rim = WMAX * COLS
    pair_step = jnp.where((frame_id & 1) == 0, 1, -1)
    link_step = jnp.where((frame_id & 2) == 0, 2, -2)
    for slot in range(2):
        step = meta[4 + slot] - frame_id
        for distance, source in (
            (pair_step, pair),
            (-pair_step, cross),
            (link_step, first),
            (-link_step, second),
            (2 * link_step, far_first),
            (-2 * link_step, far_second),
        ):

            @pl.when(step == distance)
            def _(source=source):
                slots_out[slot] = source[...]
                begin = pl.multiple_of((1 - row_id) * (count - rim), rim)
                edge_out[slot] = source[pl.ds(begin, rim)]


def relay_kernel(
    meta, across, first, second, third, first_keep, second_keep, own, pair,
    first_out, second_out, pair_out, own_out,
):
    frame_id = meta[0]
    width = first_keep.shape[0]
    packed = third.shape[0]
    pair_out[...] = pair[...]
    crossing = across[:width].astype(F32)
    none = jnp.zeros_like(crossing)
    with_first = (frame_id & 1) == ((frame_id >> 1) & 1)
    first_out[...] = (
        first_keep[...] + second[...].astype(F32) + jnp.where(with_first, crossing, none)
    ).astype(BF16)
    second_out[...] = (
        second_keep[...] + first[:width].astype(F32) + jnp.where(with_first, none, crossing)
    ).astype(BF16)
    for part in range(2):
        rows = slice(part * packed, (part + 1) * packed)
        lanes = slice(part * width, (part + 1) * width)
        own_out[rows] = (
            (own[rows] + across[width:, lanes].astype(F32))
            + (first[width:, lanes].astype(F32) + third[:, lanes].astype(F32))
        ).astype(BF16)


def final_kernel(base, first, second, pair, own, other, grad_out, own_out):
    returned = first[...].astype(F32) + second[...].astype(F32) + pair[...].astype(F32)
    grad_out[...] = (base[...] + returned.T).astype(BF16)
    own_out[...] = (own[...].astype(F32) + other[...].astype(F32)).astype(BF16)


def gather_kernel(meta, own, first, second, third, pieces_out):
    me = meta[0] & 3
    piece = own.shape[0]
    for mask, part in enumerate((own, first, second, third)):
        begin = pl.multiple_of((me ^ mask) * piece, piece)
        pieces_out[pl.ds(begin, piece)] = part[...]


def weights_kernel(meta, own, other, shared_out, value_out, output_out, taps_out, *, norm):
    row_id = meta[2]
    width = shared_out.shape[1]
    low = jnp.where(row_id == 0, own[...].astype(F32), other[...].astype(F32)) * norm
    high = jnp.where(row_id == 0, other[...].astype(F32), own[...].astype(F32)) * norm
    shared_out[...] = low[:width]
    value_out[...] = low[width : 2 * width]
    output_out[...] = low[2 * width :]
    for tap in range(3):
        taps_out[tap] = high[tap * width : (tap + 1) * width]


def local(
    latents, ref_frames, windows, quant_level, quant_scale,
    shared_proj, value_proj, output_proj, conv_taps, cotangent,
):
    width = latents.shape[2]
    count = latents.shape[1]
    rows_dev = count // COLS
    frames = lax.axis_size("frame")
    total_rows = rows_dev * lax.axis_size("row")
    frame_id = lax.axis_index("frame")
    row_id = lax.axis_index("row")
    refs = ref_frames[0]
    odd = (frame_id & 1) == 1
    rim = WMAX * COLS
    tokens = latents[0]
    low_link = (frame_id & 2) == 0
    meta = jnp.concatenate(
        [jnp.stack([frame_id, windows[0], row_id, jnp.int32(total_rows)]).astype(jnp.int32), refs]
    )
    gain = lax.dynamic_slice_in_dim(quant_scale, quant_level[0], 1, 0)

    from_pair = swapped(tokens, "frame", 1)
    from_first = along(tokens, 0)
    from_second = along(tokens, 2)
    from_before = jnp.where(low_link, from_second, from_first)
    from_after = jnp.where(low_link, from_first, from_second)

    cot = cotangent[0]
    cot_edge = jnp.where(row_id == 0, cot[count - COLS :], cot[:COLS])
    grad_edge = swapped((cot_edge.astype(F32) * gain).astype(BF16), "row", 1)
    grad_resid, grad_rb, grad_ext, up, upt, query, queryt = whole_call(
        before_kernel,
        [
            ((count, width), F32),
            ((count, width), BF16),
            ((count + 2 * COLS, width), BF16),
            ((count, width), BF16),
            ((width, count), BF16),
            ((count, width), BF16),
            ((width, count), BF16),
        ],
        (meta, cot, gain, grad_edge, tokens, conv_taps, shared_proj, output_proj),
        smem=(0,),
        flops=2 * 5 * count * width * width,
        moved=4 * count * width * 6,
        name="gradient_path",
    )

    far_first = along(from_second, 0)
    far_second = along(from_first, 2)
    from_cross = swapped(jnp.where(odd, from_before, from_after), "frame", 1)
    slots, edge = whole_call(
        select_kernel,
        [((2, count, width), BF16), ((2, rim, width), BF16)],
        (meta, from_pair, from_cross, from_first, from_second, far_first, far_second, upt),
        smem=(0,),
        flops=count * width,
        moved=count * width * 8,
        name="slots",
    )
    halo = swapped(edge, "row", 1)

    block = BROWS * COLS
    span = block + 2 * rim
    ext_count = count + 2 * rim
    half = 3 * width
    mid, send, keep, hidden, residual, base = whole_call(
        attention_kernel,
        [
            ((2, width, count), F32),
            ((half + width, width), BF16),
            ((half, width), F32),
            ((count, width), BF16),
            ((count, width), F32),
            ((count, width), F32),
        ],
        (
            meta, slots, halo, query, queryt, up, upt, tokens, grad_rb, grad_ext, grad_resid,
            shared_proj, value_proj, output_proj,
        ),
        smem=(0,),
        scratch=[
            pltpu.VMEM((2, ext_count, width), BF16),
            pltpu.VMEM((2, ext_count, width), BF16),
            pltpu.VMEM((2 * span, width), BF16),
            pltpu.VMEM((2 * span, width), BF16),
            pltpu.VMEM((width, 2 * span), BF16),
            pltpu.VMEM((width, 2 * span), BF16),
            pltpu.VMEM((block, 2 * span), F32),
            pltpu.VMEM((count, width), BF16),
            pltpu.VMEM((count, width), F32),
            pltpu.VMEM((2, width, ext_count), F32),
            pltpu.VMEM((2, width, ext_count), F32),
            pltpu.VMEM((2 * half, width), F32),
        ],
        grid=(count // block,),
        flops=6 * 2 * count * 2 * span * width * HEADS,
        moved=count * width * 60,
        name="attention",
        vmem=28,
    )

    got = swapped(send, "row", 1)
    hidden_edge = jnp.where(row_id == 0, hidden[count - COLS :], hidden[:COLS])
    hidden_halo = swapped(hidden_edge, "row", 1)
    piece = half // 4
    packed = piece // 2
    pair, across, first, second, third, first_keep, second_keep, own = whole_call(
        spread_kernel,
        [
            ((width, count), BF16),
            ((width + packed, count), BF16),
            ((width + packed, count), BF16),
            ((width, count), BF16),
            ((packed, count), BF16),
            ((width, count), F32),
            ((width, count), F32),
            ((piece, width), F32),
        ],
        (meta, mid, keep, got),
        smem=(0,),
        flops=count * width * 12,
        moved=count * width * 30,
        name="spread",
    )

    across = swapped(across, "frame", 1)
    first = along(first, 0)
    second = along(second, 2)
    third = swapped(third, "frame", 3)

    back_first, back_second, back_pair, own = whole_call(
        relay_kernel,
        [
            ((width, count), BF16),
            ((width, count), BF16),
            ((width, count), BF16),
            ((piece, width), BF16),
        ],
        (meta, across, first, second, third, first_keep, second_keep, own, pair),
        smem=(0,),
        flops=count * width * 4,
        moved=count * width * 16,
        name="relay",
    )
    back_first = along(back_first, 0)
    back_second = along(back_second, 2)
    back_pair = swapped(back_pair, "frame", 1)
    mask = 4
    other = swapped(own, "frame", mask)
    while 2 * mask < frames:
        mask *= 2
        own = (own.astype(F32) + other.astype(F32)).astype(BF16)
        other = swapped(own, "frame", mask)
    grad_latents, own = whole_call(
        final_kernel,
        [((count, width), BF16), ((piece, width), BF16)],
        (base, back_first, back_second, back_pair, own, other),
        flops=count * width * 4,
        moved=count * width * 12,
        name="latent_gradient",
    )
    (pieces,) = whole_call(
        gather_kernel,
        [((half, width), BF16)],
        (meta, own, *[swapped(own, "frame", mask) for mask in (1, 2, 3)]),
        smem=(0,),
        flops=half * width,
        moved=half * width * 4,
        name="pieces",
    )
    other = swapped(pieces, "row", 1)
    shared_grad, value_grad, output_grad, taps_grad = whole_call(
        functools.partial(
            weights_kernel, norm=1.0 / math.sqrt(frames * total_rows * COLS)
        ),
        [
            ((width, width), F32),
            ((width, width), F32),
            ((width, width), F32),
            ((3, width, width), F32),
        ],
        (meta, pieces, other),
        smem=(0,),
        flops=6 * width * width,
        moved=6 * width * width * 6,
        name="weight_gradients",
    )

    (coded,) = whole_call(
        coded_kernel,
        [((count, width), BF16)],
        (meta, hidden, hidden_halo, residual, gain, conv_taps),
        smem=(0,),
        scratch=[pltpu.VMEM((count + 2 * COLS, width), BF16)],
        flops=2 * 3 * count * width * width,
        moved=count * width * 8,
        name="context",
    )
    return (
        coded[None],
        grad_latents[None],
        shared_grad,
        value_grad,
        output_grad,
        taps_grad,
    )


def solution(mesh):
    placed = (
        P(("groups", "frame"), "row", None),
        P(("groups", "frame"), None),
        P(("groups", "frame")),
        P(("groups", "frame")),
        P(),
        P(),
        P(),
        P(),
        P(),
        P(("groups", "frame"), "row", None),
    )
    return jax.shard_map(
        local,
        mesh=mesh,
        in_specs=placed,
        out_specs=(
            P(("groups", "frame"), "row", None),
            P(("groups", "frame"), "row", None),
            P("groups", None),
            P("groups", None),
            P("groups", None),
            P("groups", None, None),
        ),
        check_vma=False,
    )
```

```python
import functools
import math

import jax
import jax.numpy as jnp
from jax import lax
from jax.experimental import pallas as pl
from jax.experimental.pallas import tpu as pltpu
from jax.sharding import PartitionSpec as P

HEADS = 8
DH = 32
COLS = 64
WMAX = 2
BROWS = 2

SCALE = 1.5 / math.sqrt(DH)
MASKED = -1e30
LOG2E = 1.4426950408889634
F32 = jnp.float32
BF16 = jnp.bfloat16
NN = (((1,), (0,)), ((), ()))
NT = (((1,), (1,)), ((), ()))


def dot(left, right, dims=NN):
    return lax.dot_general(left, right, dims, preferred_element_type=F32)


def halves_of(value):
    high = value.astype(BF16)
    return high, (value - high.astype(F32)).astype(BF16)


def left_split_dot(left, right, dims=NN):
    high, low = halves_of(left)
    return dot(high, right, dims) + dot(low, right, dims)


def right_split_dot(left, right, dims=NN):
    high, low = halves_of(right)
    return dot(left, high, dims) + dot(left, low, dims)


def swapped(array, axis, mask):
    pairs = [(i, i ^ mask) for i in range(lax.axis_size(axis))]
    return lax.ppermute(array, axis, pairs)


def along(array, parity, relayed=False):
    devices = lax.axis_size("frame")
    pairs = [(i, i + 2) for i in range(devices) if (i & 2) == parity and i + 2 < devices]
    pairs = pairs + [(j, i) for i, j in pairs]
    if relayed:
        pairs = [(i, j) for i, j in pairs if 0 <= 2 * i - j < devices]
    return lax.ppermute(array, "frame", pairs)


def whole_call(
    body, outs, args, smem=(), scratch=(), grid=None, flops=0, moved=0, name=None, vmem=16
):
    specs = [
        pl.BlockSpec(memory_space=pltpu.SMEM if i in smem else pltpu.VMEM)
        for i in range(len(args))
    ]
    more = {} if grid is None else {"grid": grid}
    return pl.pallas_call(
        body,
        out_shape=[jax.ShapeDtypeStruct(shape, dtype) for shape, dtype in outs],
        in_specs=specs,
        out_specs=[pl.BlockSpec(memory_space=pltpu.VMEM)] * len(outs),
        scratch_shapes=list(scratch),
        compiler_params=pltpu.CompilerParams(vmem_limit_bytes=vmem * 1024 * 1024),
        cost_estimate=pl.CostEstimate(flops=flops, bytes_accessed=moved, transcendentals=0),
        name=name,
        **more,
    )(*args)


def before_kernel(
    level, scale, edge, cot, tokens, taps, shared, outp,
    resid_out, rb_out, ext_out, up_out, upt_out, query_out, queryt_out, gain_out,
):
    row_id = lax.axis_index("row")
    count = cot.shape[0]
    gain = scale[pl.ds(level[0], 1), :]
    gain_out[...] = gain
    grad_z = cot[...].astype(F32) * gain
    got = (edge[...].astype(F32) * gain).astype(BF16)
    none = jnp.zeros_like(got)
    ext_out[:COLS] = jnp.where(row_id == 0, none, got)
    ext_out[COLS : COLS + count] = grad_z.astype(BF16)
    ext_out[COLS + count :] = jnp.where(row_id == 0, got, none)
    total = grad_z
    for tap in range(3):
        begin = (2 - tap) * COLS
        total = total + dot(ext_out[begin : begin + count], taps[tap], NT)
    resid_out[...] = total
    rounded = total.astype(BF16)
    rb_out[...] = rounded
    upstream = dot(rounded, outp[...], NT).astype(BF16)
    up_out[...] = upstream
    upt_out[...] = upstream.T
    query = dot(tokens[...], shared[...]).astype(BF16)
    query_out[...] = query
    queryt_out[...] = query.T


def attention_kernel(
    windows, slots, halo, query, queryt, up, upt, tokens, rb, ext, resid_grad, shared, value, outp,
    mid_out, send_out, keep_out, hidden_out, resid_out, base_out,
    key_all, val_all, key_blk, val_blk, keyt_blk, valt_blk, bias, mixed_all, dq_all, dkt, dvt, sums,
    *, total_rows,
):
    step = pl.program_id(0)
    window, row_id = windows[0], lax.axis_index("row")
    width = query.shape[1]
    count = query.shape[0]
    rim = WMAX * COLS
    block = BROWS * COLS
    span = block + 2 * rim

    @pl.when(step == 0)
    def _():
        for slot in range(2):
            for weight, full in ((shared, key_all), (value, val_all)):
                full[slot, rim : rim + count] = dot(slots[slot], weight[...]).astype(BF16)
                far = dot(halo[slot], weight[...]).astype(BF16)
                none = jnp.zeros_like(far)
                full[slot, :rim] = jnp.where(row_id == 0, none, far)
                full[slot, rim + count :] = jnp.where(row_id == 0, far, none)
        dkt[...] = jnp.zeros_like(dkt)
        dvt[...] = jnp.zeros_like(dvt)

    begin = pl.multiple_of(step * block, block)
    for slot in range(2):
        key_blk[slot * span : (slot + 1) * span] = key_all[slot, pl.ds(begin, span)]
        val_blk[slot * span : (slot + 1) * span] = val_all[slot, pl.ds(begin, span)]
    keyt_blk[...] = key_blk[...].T
    valt_blk[...] = val_blk[...].T
    first_row = row_id * (count // COLS) + step * BROWS
    query_row = first_row + lax.broadcasted_iota(jnp.int32, (block, span), 0) // COLS
    key_row = first_row - WMAX + lax.broadcasted_iota(jnp.int32, (block, span), 1) // COLS
    near = jnp.abs(query_row - key_row) <= window
    allowed = near & (key_row >= 0) & (key_row < total_rows)
    one_bias = jnp.where(allowed, 0.0, MASKED)
    bias[:, :span] = one_bias
    bias[:, span:] = one_bias

    def all_heads(rows):
        return jnp.concatenate([rows * mask.astype(BF16) for mask in masks], 0)

    def own_lanes(stacked):
        total = jnp.zeros((block, width), F32)
        for head, mask in enumerate(masks):
            total = total + stacked[head * block : (head + 1) * block] * mask
        return total

    lane_head = lax.broadcasted_iota(jnp.int32, (1, width), 1) // DH
    masks = [(lane_head == head).astype(F32) for head in range(HEADS)]
    cube = (HEADS, block, 2 * span)
    flat = (HEADS * block, 2 * span)
    scores = dot(all_heads(query[pl.ds(begin, block), :]), keyt_blk[...]).reshape(cube)
    scores = scores + bias[...][None]
    top = jnp.max(scores, axis=2, keepdims=True)
    terms = jnp.exp2((scores - top) * (SCALE * LOG2E))
    weights = terms * (1.0 / jnp.sum(terms, axis=2, keepdims=True))
    prob = weights.astype(BF16)
    mixed_all[pl.ds(begin, block), :] = own_lanes(
        dot(prob.reshape(flat), val_blk[...])
    ).astype(BF16)
    grad_prob = dot(all_heads(up[pl.ds(begin, block), :]), valt_blk[...]).reshape(cube)
    inner = jnp.sum(weights * grad_prob, axis=2, keepdims=True)
    grad_score = ((weights * (grad_prob - inner)) * SCALE).astype(BF16)
    dq_all[pl.ds(begin, block), :] = own_lanes(dot(grad_score.reshape(flat), key_blk[...]))
    for head in range(HEADS):
        lanes = slice(head * DH, (head + 1) * DH)
        dv = dot(upt[lanes, pl.ds(begin, block)], prob[head])
        dk = dot(queryt[lanes, pl.ds(begin, block)], grad_score[head])
        for slot in range(2):
            dvt[slot, lanes, pl.ds(begin, span)] += dv[:, slot * span : (slot + 1) * span]
            dkt[slot, lanes, pl.ds(begin, span)] += dk[:, slot * span : (slot + 1) * span]

    @pl.when(step == pl.num_programs(0) - 1)
    def _():
        def far_rim(array):
            upper, lower = array[:, :rim], array[:, rim + count :]
            return jnp.where(row_id == 0, lower, upper)

        half = 3 * width
        middle = slice(rim, rim + count)
        grad_q = dq_all[...]
        shared_t = jnp.zeros((width, width), F32)
        value_t = jnp.zeros((width, width), F32)
        for slot in range(2):
            part = jnp.zeros((width, count + 2 * rim), F32)
            for piece in halves_of(dkt[slot]):
                part = part + dot(shared[...], piece)
                rims = far_rim(piece)
                shared_t += dot(piece[:, middle], slots[slot]) + dot(rims, halo[slot])
            for piece in halves_of(dvt[slot]):
                part = part + dot(value[...], piece)
                rims = far_rim(piece)
                value_t += dot(piece[:, middle], slots[slot]) + dot(rims, halo[slot])
            mid_out[slot] = part[:, middle]
            send_out[half:, slot * rim : (slot + 1) * rim] = far_rim(part).astype(BF16)
        base_out[...] = resid_grad[...] + left_split_dot(grad_q, shared[...], NT)
        sums[:width] = right_split_dot(tokens[...].T, grad_q) + shared_t.T
        sums[width : 2 * width] = value_t.T
        mixed_full = mixed_all[...]
        residual = tokens[...].astype(F32) + dot(mixed_full, outp[...])
        resid_out[...] = residual
        hidden = residual.astype(BF16)
        hidden_out[...] = hidden
        sums[2 * width : half] = dot(mixed_full.T, rb[...])
        hidden_t = hidden.T
        for tap in range(3):
            start = (2 - tap) * COLS
            sums[half + tap * width : half + (tap + 1) * width] = dot(
                hidden_t, ext[start : start + count]
            )
        keep_out[...] = sums[pl.ds(pl.multiple_of(row_id * half, half), half)]
        send_out[:half] = sums[pl.ds(pl.multiple_of((1 - row_id) * half, half), half)].astype(BF16)


def spread_kernel(
    refs, mid, keep, got,
    pair_out, across_out, first_out, second_out, third_out, first_keep, second_keep, own_out,
):
    frame_id, row_id = lax.axis_index("frame"), lax.axis_index("row")
    steps = [refs[0, 0] - frame_id, refs[0, 1] - frame_id]
    width, count = mid.shape[1], mid.shape[2]
    rim = WMAX * COLS
    half = keep.shape[0]
    piece = half // 4
    parts = []
    for slot in range(2):
        rims = got[half:, slot * rim : (slot + 1) * rim].astype(F32)
        none = jnp.zeros_like(rims)
        part = mid[slot]
        first = part[:, :rim] + jnp.where(row_id == 0, none, rims)
        last = part[:, count - rim :] + jnp.where(row_id == 0, rims, none)
        parts.append(jnp.concatenate([first, part[:, rim : count - rim], last], 1))

    def part_for(step):
        chosen = jnp.zeros((width, count), F32)
        for slot in range(2):
            chosen = chosen + jnp.where(steps[slot] == step, parts[slot], 0.0)
        return chosen

    pair_step = jnp.where((frame_id & 1) == 0, 1, -1)
    link_step = jnp.where((frame_id & 2) == 0, 1, -1)
    pair_out[...] = part_for(pair_step).astype(BF16)
    across_out[:width] = part_for(-pair_step).astype(BF16)
    first_out[:width] = part_for(4 * link_step).astype(BF16)
    second_out[...] = part_for(-4 * link_step).astype(BF16)
    first_keep[...] = part_for(2 * link_step)
    second_keep[...] = part_for(-2 * link_step)
    me = frame_id & 3

    def rows_of(index):
        rows = pl.ds(pl.multiple_of(index * piece, piece), piece)
        return keep[rows] + got[rows].astype(F32)

    own_out[...] = rows_of(me)
    for mask, out, begin in ((1, across_out, width), (2, first_out, width), (3, third_out, 0)):
        rows = rows_of(me ^ mask).astype(BF16)
        out[begin:, :width] = rows[: piece // 2]
        out[begin:, width:] = rows[piece // 2 :]


def coded_kernel(hidden, halo, residual, gain, taps, coded_out, gain_out, ext):
    gain_out[...] = gain[...]
    row_id = lax.axis_index("row")
    count = hidden.shape[0]
    got = halo[...]
    none = jnp.zeros_like(got)
    ext[:COLS] = jnp.where(row_id == 0, none, got)
    ext[COLS : COLS + count] = hidden[...]
    ext[COLS + count :] = jnp.where(row_id == 0, got, none)
    total = jnp.zeros((count, hidden.shape[1]), F32)
    for tap in range(3):
        begin = tap * COLS
        total = total + dot(ext[begin : begin + count], taps[tap])
    coded_out[...] = ((residual[...] + total) * gain[...]).astype(BF16)


def select_kernel(refs, pair, cross, first, second, far_first, far_second, _, slots_out, edge_out):
    frame_id, row_id = lax.axis_index("frame"), lax.axis_index("row")
    count = pair.shape[0]
    rim = WMAX * COLS
    pair_step = jnp.where((frame_id & 1) == 0, 1, -1)
    link_step = jnp.where((frame_id & 2) == 0, 2, -2)
    for slot in range(2):
        step = refs[0, slot] - frame_id
        for distance, source in (
            (pair_step, pair),
            (-pair_step, cross),
            (link_step, first),
            (-link_step, second),
            (2 * link_step, far_first),
            (-2 * link_step, far_second),
        ):

            @pl.when(step == distance)
            def _(source=source):
                slots_out[slot] = source[...]
                begin = pl.multiple_of((1 - row_id) * (count - rim), rim)
                edge_out[slot] = source[pl.ds(begin, rim)]


def relay_kernel(
    across, first, second, third, first_keep, second_keep, own, pair, _,
    first_out, second_out, pair_out, own_out,
):
    frame_id = lax.axis_index("frame")
    width = first_keep.shape[0]
    packed = third.shape[0]
    pair_out[...] = pair[...]
    crossing = across[:width].astype(F32)
    none = jnp.zeros_like(crossing)
    with_first = (frame_id & 1) == ((frame_id >> 1) & 1)
    first_out[...] = (
        first_keep[...] + second[...].astype(F32) + jnp.where(with_first, crossing, none)
    ).astype(BF16)
    second_out[...] = (
        second_keep[...] + first[:width].astype(F32) + jnp.where(with_first, none, crossing)
    ).astype(BF16)
    for part in range(2):
        rows = slice(part * packed, (part + 1) * packed)
        lanes = slice(part * width, (part + 1) * width)
        own_out[rows] = (
            (own[rows] + across[width:, lanes].astype(F32))
            + (first[width:, lanes].astype(F32) + third[:, lanes].astype(F32))
        ).astype(BF16)


def final_kernel(base, first, second, pair, grad_out, last_out):
    returned = first[...].astype(F32) + second[...].astype(F32) + pair[...].astype(F32)
    grad_out[...] = (base[...] + returned.T).astype(BF16)
    last_out[...] = returned[:16, :128]


def gather_kernel(own, first, second, third, _, pieces_out):
    me = lax.axis_index("frame") & 3
    piece = own.shape[0]
    for mask, part in enumerate((own, first, second, third)):
        begin = pl.multiple_of((me ^ mask) * piece, piece)
        pieces_out[pl.ds(begin, piece)] = part[...]


def weights_kernel(own, other, shared_out, value_out, output_out, taps_out, *, norm):
    row_id = lax.axis_index("row")
    width = shared_out.shape[1]
    low = jnp.where(row_id == 0, own[...].astype(F32), other[...].astype(F32)) * norm
    high = jnp.where(row_id == 0, other[...].astype(F32), own[...].astype(F32)) * norm
    shared_out[...] = low[:width]
    value_out[...] = low[width : 2 * width]
    output_out[...] = low[2 * width :]
    for tap in range(3):
        taps_out[tap] = high[tap * width : (tap + 1) * width]


def local(
    latents, ref_frames, windows, quant_level, quant_scale,
    shared_proj, value_proj, output_proj, conv_taps, cotangent,
):
    width = latents.shape[2]
    count = latents.shape[1]
    rows_dev = count // COLS
    frames = lax.axis_size("frame")
    total_rows = rows_dev * lax.axis_size("row")
    row_id = lax.axis_index("row")
    rim = WMAX * COLS
    tokens = latents[0]
    cot = cotangent[0]

    cot_edge = swapped(jnp.where(row_id == 0, cot[count - COLS :], cot[:COLS]), "row", 1)
    from_first = along(tokens, 0)
    from_second = along(tokens, 2)
    from_pair = swapped(tokens, "frame", 1)

    grad_resid, grad_rb, grad_ext, up, upt, query, queryt, gain = whole_call(
        before_kernel,
        [
            ((count, width), F32),
            ((count, width), BF16),
            ((count + 2 * COLS, width), BF16),
            ((count, width), BF16),
            ((width, count), BF16),
            ((count, width), BF16),
            ((width, count), BF16),
            ((1, width), F32),
        ],
        (
            quant_level, quant_scale, cot_edge, cot, tokens, conv_taps, shared_proj, output_proj,
        ),
        smem=(0,),
        flops=2 * 5 * count * width * width,
        moved=4 * count * width * 6,
        name="gradient_path",
    )

    frame_id = lax.axis_index("frame")
    by_second = (frame_id & 1) != ((frame_id >> 1) & 1)
    far_first = along(from_second, 0, relayed=True)
    far_second = along(from_first, 2, relayed=True)
    from_cross = swapped(jnp.where(by_second, from_second, from_first), "frame", 1)
    slots, edge = whole_call(
        select_kernel,
        [((2, count, width), BF16), ((2, rim, width), BF16)],
        (ref_frames, from_pair, from_cross, from_first, from_second, far_first, far_second, gain),
        smem=(0,),
        flops=count * width,
        moved=count * width * 8,
        name="slots",
    )
    halo = swapped(edge, "row", 1)

    block = BROWS * COLS
    span = block + 2 * rim
    ext_count = count + 2 * rim
    half = 3 * width
    mid, send, keep, hidden, residual, base = whole_call(
        functools.partial(attention_kernel, total_rows=total_rows),
        [
            ((2, width, count), F32),
            ((half + width, width), BF16),
            ((half, width), F32),
            ((count, width), BF16),
            ((count, width), F32),
            ((count, width), F32),
        ],
        (
            windows, slots, halo, query, queryt, up, upt, tokens, grad_rb, grad_ext, grad_resid,
            shared_proj, value_proj, output_proj,
        ),
        smem=(0,),
        scratch=[
            pltpu.VMEM((2, ext_count, width), BF16),
            pltpu.VMEM((2, ext_count, width), BF16),
            pltpu.VMEM((2 * span, width), BF16),
            pltpu.VMEM((2 * span, width), BF16),
            pltpu.VMEM((width, 2 * span), BF16),
            pltpu.VMEM((width, 2 * span), BF16),
            pltpu.VMEM((block, 2 * span), F32),
            pltpu.VMEM((count, width), BF16),
            pltpu.VMEM((count, width), F32),
            pltpu.VMEM((2, width, ext_count), F32),
            pltpu.VMEM((2, width, ext_count), F32),
            pltpu.VMEM((2 * half, width), F32),
        ],
        grid=(count // block,),
        flops=6 * 2 * count * 2 * span * width * HEADS,
        moved=count * width * 60,
        name="attention",
        vmem=28,
    )

    got = swapped(send, "row", 1)
    hidden_edge = jnp.where(row_id == 0, hidden[count - COLS :], hidden[:COLS])
    hidden_halo = swapped(hidden_edge, "row", 1)
    piece = half // 4
    packed = piece // 2
    pair, across, first, second, third, first_keep, second_keep, own = whole_call(
        spread_kernel,
        [
            ((width, count), BF16),
            ((width + packed, count), BF16),
            ((width + packed, count), BF16),
            ((width, count), BF16),
            ((packed, count), BF16),
            ((width, count), F32),
            ((width, count), F32),
            ((piece, width), F32),
        ],
        (ref_frames, mid, keep, got),
        smem=(0,),
        flops=count * width * 12,
        moved=count * width * 30,
        name="spread",
    )

    third = swapped(third, "frame", 3)
    across = swapped(across, "frame", 1)
    first = along(first, 0)
    second = along(second, 2)
    coded, gain = whole_call(
        coded_kernel,
        [((count, width), BF16), ((1, width), F32)],
        (hidden, hidden_halo, residual, gain, conv_taps),
        scratch=[pltpu.VMEM((count + 2 * COLS, width), BF16)],
        flops=2 * 3 * count * width * width,
        moved=count * width * 8,
        name="context",
    )
    back_first, back_second, back_pair, own = whole_call(
        relay_kernel,
        [
            ((width, count), BF16),
            ((width, count), BF16),
            ((width, count), BF16),
            ((piece, width), BF16),
        ],
        (across, first, second, third, first_keep, second_keep, own, pair, gain),
        flops=count * width * 4,
        moved=count * width * 16,
        name="relay",
    )
    mask = 4
    other = swapped(own, "frame", mask)
    back_first = along(back_first, 0)
    back_second = along(back_second, 2)
    back_pair = swapped(back_pair, "frame", 1)
    while 2 * mask < frames:
        mask *= 2
        own = (own.astype(F32) + other.astype(F32)).astype(BF16)
        other = swapped(own, "frame", mask)
    own = (own.astype(F32) + other.astype(F32)).astype(BF16)
    grad_latents, last = whole_call(
        final_kernel,
        [((count, width), BF16), ((16, 128), F32)],
        (base, back_first, back_second, back_pair),
        flops=count * width * 4,
        moved=count * width * 12,
        name="latent_gradient",
    )
    (pieces,) = whole_call(
        gather_kernel,
        [((half, width), BF16)],
        (own, *[swapped(own, "frame", mask) for mask in (1, 2, 3)], last),
        flops=half * width,
        moved=half * width * 4,
        name="pieces",
    )
    other = swapped(pieces, "row", 1)
    shared_grad, value_grad, output_grad, taps_grad = whole_call(
        functools.partial(
            weights_kernel, norm=1.0 / math.sqrt(frames * total_rows * COLS)
        ),
        [
            ((width, width), F32),
            ((width, width), F32),
            ((width, width), F32),
            ((3, width, width), F32),
        ],
        (pieces, other),
        flops=6 * width * width,
        moved=6 * width * width * 6,
        name="weight_gradients",
    )

    return (
        coded[None],
        grad_latents[None],
        shared_grad,
        value_grad,
        output_grad,
        taps_grad,
    )


def solution(mesh):
    placed = (
        P(("groups", "frame"), "row", None),
        P(("groups", "frame"), None),
        P(("groups", "frame")),
        P(("groups", "frame")),
        P(),
        P(),
        P(),
        P(),
        P(),
        P(("groups", "frame"), "row", None),
    )
    return jax.shard_map(
        local,
        mesh=mesh,
        in_specs=placed,
        out_specs=(
            P(("groups", "frame"), "row", None),
            P(("groups", "frame"), "row", None),
            P("groups", None),
            P("groups", None),
            P("groups", None),
            P("groups", None, None),
        ),
        check_vma=False,
    )
```

```python
import functools
import math

import jax
import jax.numpy as jnp
from jax import lax
from jax.experimental import pallas as pl
from jax.experimental.pallas import tpu as pltpu
from jax.sharding import PartitionSpec as P

HEADS = 8
DH = 32
COLS = 64
WMAX = 2
BROWS = 2
GROUP = 2

SCALE = 1.5 / math.sqrt(DH)
MASKED = -1e30
LOG2E = 1.4426950408889634
F32 = jnp.float32
BF16 = jnp.bfloat16
NN = (((1,), (0,)), ((), ()))
NT = (((1,), (1,)), ((), ()))


def dot(left, right, dims=NN):
    return lax.dot_general(left, right, dims, preferred_element_type=F32)


def halves_of(value):
    high = value.astype(BF16)
    return high, (value - high.astype(F32)).astype(BF16)


def left_split_dot(left, right, dims=NN):
    high, low = halves_of(left)
    return dot(high, right, dims) + dot(low, right, dims)


def right_split_dot(left, right, dims=NN):
    high, low = halves_of(right)
    return dot(left, high, dims) + dot(left, low, dims)


def swapped(array, axis, mask):
    pairs = [(i, i ^ mask) for i in range(lax.axis_size(axis))]
    return lax.ppermute(array, axis, pairs)


def along(array, parity, relayed=False):
    devices = lax.axis_size("frame")
    pairs = [(i, i + 2) for i in range(devices) if (i & 2) == parity and i + 2 < devices]
    pairs = pairs + [(j, i) for i, j in pairs]
    if relayed:
        pairs = [(i, j) for i, j in pairs if 0 <= 2 * i - j < devices]
    return lax.ppermute(array, "frame", pairs)


def whole_call(
    body, outs, args, smem=(), scratch=(), grid=None, flops=0, moved=0, name=None, vmem=16
):
    specs = [
        pl.BlockSpec(memory_space=pltpu.SMEM if i in smem else pltpu.VMEM)
        for i in range(len(args))
    ]
    more = {} if grid is None else {"grid": grid}
    return pl.pallas_call(
        body,
        out_shape=[jax.ShapeDtypeStruct(shape, dtype) for shape, dtype in outs],
        in_specs=specs,
        out_specs=[pl.BlockSpec(memory_space=pltpu.VMEM)] * len(outs),
        scratch_shapes=list(scratch),
        compiler_params=pltpu.CompilerParams(vmem_limit_bytes=vmem * 1024 * 1024),
        cost_estimate=pl.CostEstimate(flops=flops, bytes_accessed=moved, transcendentals=0),
        name=name,
        **more,
    )(*args)


def before_kernel(
    level, scale, edge, cot, tokens, taps, shared, outp,
    resid_out, rb_out, ext_out, up_out, upt_out, query_out, queryt_out, gain_out,
):
    row_id = lax.axis_index("row")
    count = cot.shape[0]
    gain = scale[pl.ds(level[0], 1), :]
    gain_out[...] = gain
    grad_z = cot[...].astype(F32) * gain
    got = (edge[...].astype(F32) * gain).astype(BF16)
    none = jnp.zeros_like(got)
    ext_out[:COLS] = jnp.where(row_id == 0, none, got)
    ext_out[COLS : COLS + count] = grad_z.astype(BF16)
    ext_out[COLS + count :] = jnp.where(row_id == 0, got, none)
    total = grad_z
    for tap in range(3):
        begin = (2 - tap) * COLS
        total = total + dot(ext_out[begin : begin + count], taps[tap], NT)
    resid_out[...] = total
    rounded = total.astype(BF16)
    rb_out[...] = rounded
    upstream = dot(rounded, outp[...], NT).astype(BF16)
    up_out[...] = upstream
    upt_out[...] = upstream.T
    query = dot(tokens[...], shared[...]).astype(BF16)
    query_out[...] = query
    queryt_out[...] = query.T


def attention_kernel(
    windows, slots, halo, query, queryt, up, upt, tokens, rb, ext, resid_grad, shared, value, outp,
    mid_out, send_out, keep_out, hidden_out, resid_out, base_out,
    key_all, val_all, key_blk, val_blk, keyt_blk, valt_blk, bias, mixed_all, dq_all, dkt, dvt, sums,
    score_all, grad_all, *, total_rows,
):
    step = pl.program_id(0)
    window, row_id = windows[0], lax.axis_index("row")
    width = query.shape[1]
    count = query.shape[0]
    rim = WMAX * COLS
    block = BROWS * COLS
    span = block + 2 * rim

    @pl.when(step == 0)
    def _():
        for slot in range(2):
            for weight, full in ((shared, key_all), (value, val_all)):
                full[slot, rim : rim + count] = dot(slots[slot], weight[...]).astype(BF16)
                far = dot(halo[slot], weight[...]).astype(BF16)
                none = jnp.zeros_like(far)
                full[slot, :rim] = jnp.where(row_id == 0, none, far)
                full[slot, rim + count :] = jnp.where(row_id == 0, far, none)
        dkt[...] = jnp.zeros_like(dkt)
        dvt[...] = jnp.zeros_like(dvt)

    begin = pl.multiple_of(step * block, block)
    for slot in range(2):
        key_blk[slot * span : (slot + 1) * span] = key_all[slot, pl.ds(begin, span)]
        val_blk[slot * span : (slot + 1) * span] = val_all[slot, pl.ds(begin, span)]
    keyt_blk[...] = key_blk[...].T
    valt_blk[...] = val_blk[...].T
    first_row = row_id * (count // COLS) + step * BROWS
    query_row = first_row + lax.broadcasted_iota(jnp.int32, (block, span), 0) // COLS
    key_row = first_row - WMAX + lax.broadcasted_iota(jnp.int32, (block, span), 1) // COLS
    near = jnp.abs(query_row - key_row) <= window
    allowed = near & (key_row >= 0) & (key_row < total_rows)
    one_bias = jnp.where(allowed, 0.0, MASKED)
    bias[:, :span] = one_bias
    bias[:, span:] = one_bias

    lane_head = lax.broadcasted_iota(jnp.int32, (1, width), 1) // DH
    masks = [(lane_head == head).astype(F32) for head in range(HEADS)]
    tall = GROUP * block
    group_bias = jnp.concatenate([bias[...]] * GROUP, 0)
    query_b, up_b = query[pl.ds(begin, block), :], up[pl.ds(begin, block), :]
    mixed = jnp.zeros((block, width), F32)
    grad_q = jnp.zeros((block, width), F32)

    def products(group):
        own = masks[group * GROUP : (group + 1) * GROUP]
        stacked_q = jnp.concatenate([query_b * mask.astype(BF16) for mask in own], 0)
        stacked_u = jnp.concatenate([up_b * mask.astype(BF16) for mask in own], 0)
        rows = slice(group * tall, (group + 1) * tall)
        score_all[rows] = dot(stacked_q, keyt_blk[...])
        grad_all[rows] = dot(stacked_u, valt_blk[...])

    products(0)
    for group in range(HEADS // GROUP):
        if (group + 1) * GROUP < HEADS:
            products(group + 1)
        rows = slice(group * tall, (group + 1) * tall)
        scores = score_all[rows] + group_bias
        top = jnp.max(scores, axis=1, keepdims=True)
        terms = jnp.exp2((scores - top) * (SCALE * LOG2E))
        weights = terms * (1.0 / jnp.sum(terms, axis=1, keepdims=True))
        prob = weights.astype(BF16)
        grad_prob = grad_all[rows]
        inner = jnp.sum(weights * grad_prob, axis=1, keepdims=True)
        grad_score = ((weights * (grad_prob - inner)) * SCALE).astype(BF16)
        mixed_g = dot(prob, val_blk[...])
        grad_q_g = dot(grad_score, key_blk[...])
        for member in range(GROUP):
            head = group * GROUP + member
            part = slice(member * block, (member + 1) * block)
            mixed = mixed + mixed_g[part] * masks[head]
            grad_q = grad_q + grad_q_g[part] * masks[head]
            lanes = slice(head * DH, (head + 1) * DH)
            dv = dot(upt[lanes, pl.ds(begin, block)], prob[part])
            dk = dot(queryt[lanes, pl.ds(begin, block)], grad_score[part])
            for slot in range(2):
                keys = slice(slot * span, (slot + 1) * span)
                dvt[slot, lanes, pl.ds(begin, span)] += dv[:, keys]
                dkt[slot, lanes, pl.ds(begin, span)] += dk[:, keys]
    mixed_all[pl.ds(begin, block), :] = mixed.astype(BF16)
    dq_all[pl.ds(begin, block), :] = grad_q

    @pl.when(step == pl.num_programs(0) - 1)
    def _():
        def far_rim(array):
            upper, lower = array[:, :rim], array[:, rim + count :]
            return jnp.where(row_id == 0, lower, upper)

        half = 3 * width
        middle = slice(rim, rim + count)
        grad_q = dq_all[...]
        shared_t = jnp.zeros((width, width), F32)
        value_t = jnp.zeros((width, width), F32)
        for slot in range(2):
            part = jnp.zeros((width, count + 2 * rim), F32)
            for piece in halves_of(dkt[slot]):
                part = part + dot(shared[...], piece)
                rims = far_rim(piece)
                shared_t += dot(piece[:, middle], slots[slot]) + dot(rims, halo[slot])
            for piece in halves_of(dvt[slot]):
                part = part + dot(value[...], piece)
                rims = far_rim(piece)
                value_t += dot(piece[:, middle], slots[slot]) + dot(rims, halo[slot])
            mid_out[slot] = part[:, middle]
            send_out[half:, slot * rim : (slot + 1) * rim] = far_rim(part).astype(BF16)
        base_out[...] = resid_grad[...] + left_split_dot(grad_q, shared[...], NT)
        sums[:width] = right_split_dot(tokens[...].T, grad_q) + shared_t.T
        sums[width : 2 * width] = value_t.T
        mixed_full = mixed_all[...]
        residual = tokens[...].astype(F32) + dot(mixed_full, outp[...])
        resid_out[...] = residual
        hidden = residual.astype(BF16)
        hidden_out[...] = hidden
        sums[2 * width : half] = dot(mixed_full.T, rb[...])
        hidden_t = hidden.T
        for tap in range(3):
            start = (2 - tap) * COLS
            sums[half + tap * width : half + (tap + 1) * width] = dot(
                hidden_t, ext[start : start + count]
            )
        keep_out[...] = sums[pl.ds(pl.multiple_of(row_id * half, half), half)]
        send_out[:half] = sums[pl.ds(pl.multiple_of((1 - row_id) * half, half), half)].astype(BF16)


def spread_kernel(
    refs, mid, keep, got,
    pair_out, across_out, first_out, second_out, third_out, first_keep, second_keep, own_out,
):
    frame_id, row_id = lax.axis_index("frame"), lax.axis_index("row")
    steps = [refs[0, 0] - frame_id, refs[0, 1] - frame_id]
    width, count = mid.shape[1], mid.shape[2]
    rim = WMAX * COLS
    half = keep.shape[0]
    piece = half // 4

    def folded(slot):
        rims = got[half:, slot * rim : (slot + 1) * rim].astype(F32)
        none = jnp.zeros_like(rims)
        part = mid[slot]
        first = part[:, :rim] + jnp.where(row_id == 0, none, rims)
        last = part[:, count - rim :] + jnp.where(row_id == 0, rims, none)
        return jnp.concatenate([first, part[:, rim : count - rim], last], 1)

    pair_step = jnp.where((frame_id & 1) == 0, 1, -1)
    link_step = jnp.where((frame_id & 2) == 0, 1, -1)
    for step, out in (
        (pair_step, pair_out),
        (-pair_step, across_out),
        (4 * link_step, first_out),
        (-4 * link_step, second_out),
        (2 * link_step, first_keep),
        (-2 * link_step, second_keep),
    ):
        by_zero, by_one = steps[0] == step, steps[1] == step

        @pl.when(by_zero & by_one)
        def _(out=out):
            out[:width] = (folded(0) + folded(1)).astype(out.dtype)

        @pl.when(by_zero & ~by_one)
        def _(out=out):
            out[:width] = folded(0).astype(out.dtype)

        @pl.when(by_one & ~by_zero)
        def _(out=out):
            out[:width] = folded(1).astype(out.dtype)

        @pl.when(~by_zero & ~by_one)
        def _(out=out):
            out[:width] = jnp.zeros((width, count), out.dtype)

    me = frame_id & 3

    def rows_of(index):
        rows = pl.ds(pl.multiple_of(index * piece, piece), piece)
        return keep[rows] + got[rows].astype(F32)

    own_out[...] = rows_of(me)
    for mask, out, begin in ((1, across_out, width), (2, first_out, width), (3, third_out, 0)):
        rows = rows_of(me ^ mask).astype(BF16)
        out[begin:, :width] = rows[: piece // 2]
        out[begin:, width:] = rows[piece // 2 :]


def coded_kernel(hidden, halo, residual, gain, taps, coded_out, gain_out, ext):
    gain_out[...] = gain[...]
    row_id = lax.axis_index("row")
    count = hidden.shape[0]
    got = halo[...]
    none = jnp.zeros_like(got)
    ext[:COLS] = jnp.where(row_id == 0, none, got)
    ext[COLS : COLS + count] = hidden[...]
    ext[COLS + count :] = jnp.where(row_id == 0, got, none)
    total = jnp.zeros((count, hidden.shape[1]), F32)
    for tap in range(3):
        begin = tap * COLS
        total = total + dot(ext[begin : begin + count], taps[tap])
    coded_out[...] = ((residual[...] + total) * gain[...]).astype(BF16)


def select_kernel(refs, pair, cross, first, second, far_first, far_second, _, slots_out, edge_out):
    frame_id, row_id = lax.axis_index("frame"), lax.axis_index("row")
    count = pair.shape[0]
    rim = WMAX * COLS
    pair_step = jnp.where((frame_id & 1) == 0, 1, -1)
    link_step = jnp.where((frame_id & 2) == 0, 2, -2)
    for slot in range(2):
        step = refs[0, slot] - frame_id
        for distance, source in (
            (pair_step, pair),
            (-pair_step, cross),
            (link_step, first),
            (-link_step, second),
            (2 * link_step, far_first),
            (-2 * link_step, far_second),
        ):

            @pl.when(step == distance)
            def _(source=source):
                slots_out[slot] = source[:count]
                begin = pl.multiple_of((1 - row_id) * (count - rim), rim)
                edge_out[slot] = source[pl.ds(begin, rim)]


def relay_kernel(
    across, first, second, third, first_keep, second_keep, own, pair, _,
    first_out, second_out, pair_out, own_out,
):
    frame_id = lax.axis_index("frame")
    width = first_keep.shape[0]
    packed = third.shape[0]
    pair_out[...] = pair[...]
    crossing = across[:width].astype(F32)
    none = jnp.zeros_like(crossing)
    with_first = (frame_id & 1) == ((frame_id >> 1) & 1)
    first_out[...] = (
        first_keep[...] + second[...].astype(F32) + jnp.where(with_first, crossing, none)
    ).astype(BF16)
    second_out[...] = (
        second_keep[...] + first[:width].astype(F32) + jnp.where(with_first, none, crossing)
    ).astype(BF16)
    for part in range(2):
        rows = slice(part * packed, (part + 1) * packed)
        lanes = slice(part * width, (part + 1) * width)
        own_out[rows] = (
            (own[rows] + across[width:, lanes].astype(F32))
            + (first[width:, lanes].astype(F32) + third[:, lanes].astype(F32))
        ).astype(BF16)


def final_kernel(base, first, second, pair, grad_out, last_out):
    returned = first[...].astype(F32) + second[...].astype(F32) + pair[...].astype(F32)
    grad_out[...] = (base[...] + returned.T).astype(BF16)
    last_out[...] = returned[:16, :128]


def gather_kernel(own, first, second, third, _, pieces_out):
    me = lax.axis_index("frame") & 3
    piece = own.shape[0]
    for mask, part in enumerate((own, first, second, third)):
        begin = pl.multiple_of((me ^ mask) * piece, piece)
        pieces_out[pl.ds(begin, piece)] = part[...]


def weights_kernel(own, other, shared_out, value_out, output_out, taps_out, *, norm):
    row_id = lax.axis_index("row")
    width = shared_out.shape[1]
    low = jnp.where(row_id == 0, own[...].astype(F32), other[...].astype(F32)) * norm
    high = jnp.where(row_id == 0, other[...].astype(F32), own[...].astype(F32)) * norm
    shared_out[...] = low[:width]
    value_out[...] = low[width : 2 * width]
    output_out[...] = low[2 * width :]
    for tap in range(3):
        taps_out[tap] = high[tap * width : (tap + 1) * width]


def local(
    latents, ref_frames, windows, quant_level, quant_scale,
    shared_proj, value_proj, output_proj, conv_taps, cotangent,
):
    width = latents.shape[2]
    count = latents.shape[1]
    rows_dev = count // COLS
    frames = lax.axis_size("frame")
    total_rows = rows_dev * lax.axis_size("row")
    row_id = lax.axis_index("row")
    rim = WMAX * COLS
    tokens = latents[0]
    cot = cotangent[0]

    cot_edge = swapped(jnp.where(row_id == 0, cot[count - COLS :], cot[:COLS]), "row", 1)
    from_first = along(tokens, 0)
    from_second = along(tokens, 2)
    from_pair = swapped(tokens, "frame", 1)

    grad_resid, grad_rb, grad_ext, up, upt, query, queryt, gain = whole_call(
        before_kernel,
        [
            ((count, width), F32),
            ((count, width), BF16),
            ((count + 2 * COLS, width), BF16),
            ((count, width), BF16),
            ((width, count), BF16),
            ((count, width), BF16),
            ((width, count), BF16),
            ((1, width), F32),
        ],
        (
            quant_level, quant_scale, cot_edge, cot, tokens, conv_taps, shared_proj, output_proj,
        ),
        smem=(0,),
        flops=2 * 5 * count * width * width,
        moved=4 * count * width * 6,
        name="gradient_path",
    )

    frame_id = lax.axis_index("frame")
    by_second = (frame_id & 1) != ((frame_id >> 1) & 1)
    longer = jnp.concatenate([from_second, from_second[:COLS]], 0)
    far_first = along(longer, 0, relayed=True)
    far_second = along(from_first, 2, relayed=True)
    from_cross = swapped(jnp.where(by_second, from_second, from_first), "frame", 1)
    slots, edge = whole_call(
        select_kernel,
        [((2, count, width), BF16), ((2, rim, width), BF16)],
        (ref_frames, from_pair, from_cross, from_first, from_second, far_first, far_second, gain),
        smem=(0,),
        flops=count * width,
        moved=count * width * 8,
        name="slots",
    )
    halo = swapped(edge, "row", 1)

    block = BROWS * COLS
    span = block + 2 * rim
    ext_count = count + 2 * rim
    half = 3 * width
    mid, send, keep, hidden, residual, base = whole_call(
        functools.partial(attention_kernel, total_rows=total_rows),
        [
            ((2, width, count), F32),
            ((half + width, width), BF16),
            ((half, width), F32),
            ((count, width), BF16),
            ((count, width), F32),
            ((count, width), F32),
        ],
        (
            windows, slots, halo, query, queryt, up, upt, tokens, grad_rb, grad_ext, grad_resid,
            shared_proj, value_proj, output_proj,
        ),
        smem=(0,),
        scratch=[
            pltpu.VMEM((2, ext_count, width), BF16),
            pltpu.VMEM((2, ext_count, width), BF16),
            pltpu.VMEM((2 * span, width), BF16),
            pltpu.VMEM((2 * span, width), BF16),
            pltpu.VMEM((width, 2 * span), BF16),
            pltpu.VMEM((width, 2 * span), BF16),
            pltpu.VMEM((block, 2 * span), F32),
            pltpu.VMEM((count, width), BF16),
            pltpu.VMEM((count, width), F32),
            pltpu.VMEM((2, width, ext_count), F32),
            pltpu.VMEM((2, width, ext_count), F32),
            pltpu.VMEM((2 * half, width), F32),
            pltpu.VMEM((HEADS * block, 2 * span), F32),
            pltpu.VMEM((HEADS * block, 2 * span), F32),
        ],
        grid=(count // block,),
        flops=6 * 2 * count * 2 * span * width * HEADS,
        moved=count * width * 60,
        name="attention",
        vmem=28,
    )

    got = swapped(send, "row", 1)
    hidden_edge = jnp.where(row_id == 0, hidden[count - COLS :], hidden[:COLS])
    hidden_halo = swapped(hidden_edge, "row", 1)
    piece = half // 4
    packed = piece // 2
    pair, across, first, second, third, first_keep, second_keep, own = whole_call(
        spread_kernel,
        [
            ((width, count), BF16),
            ((width + packed, count), BF16),
            ((width + packed, count), BF16),
            ((width, count), BF16),
            ((packed, count), BF16),
            ((width, count), F32),
            ((width, count), F32),
            ((piece, width), F32),
        ],
        (ref_frames, mid, keep, got),
        smem=(0,),
        flops=count * width * 12,
        moved=count * width * 30,
        name="spread",
    )

    third = swapped(third, "frame", 3)
    across = swapped(across, "frame", 1)
    first = along(first, 0)
    second = along(second, 2)
    coded, gain = whole_call(
        coded_kernel,
        [((count, width), BF16), ((1, width), F32)],
        (hidden, hidden_halo, residual, gain, conv_taps),
        scratch=[pltpu.VMEM((count + 2 * COLS, width), BF16)],
        flops=2 * 3 * count * width * width,
        moved=count * width * 8,
        name="context",
    )
    back_first, back_second, back_pair, own = whole_call(
        relay_kernel,
        [
            ((width, count), BF16),
            ((width, count), BF16),
            ((width, count), BF16),
            ((piece, width), BF16),
        ],
        (across, first, second, third, first_keep, second_keep, own, pair, gain),
        flops=count * width * 4,
        moved=count * width * 16,
        name="relay",
    )
    mask = 4
    other = swapped(own, "frame", mask)
    back_first = along(back_first, 0)
    back_second = along(back_second, 2)
    back_pair = swapped(back_pair, "frame", 1)
    while 2 * mask < frames:
        mask *= 2
        own = (own.astype(F32) + other.astype(F32)).astype(BF16)
        other = swapped(own, "frame", mask)
    own = (own.astype(F32) + other.astype(F32)).astype(BF16)
    grad_latents, last = whole_call(
        final_kernel,
        [((count, width), BF16), ((16, 128), F32)],
        (base, back_first, back_second, back_pair),
        flops=count * width * 4,
        moved=count * width * 12,
        name="latent_gradient",
    )
    (pieces,) = whole_call(
        gather_kernel,
        [((half, width), BF16)],
        (own, *[swapped(own, "frame", mask) for mask in (1, 2, 3)], last),
        flops=half * width,
        moved=half * width * 4,
        name="pieces",
    )
    other = swapped(pieces, "row", 1)
    shared_grad, value_grad, output_grad, taps_grad = whole_call(
        functools.partial(
            weights_kernel, norm=1.0 / math.sqrt(frames * total_rows * COLS)
        ),
        [
            ((width, width), F32),
            ((width, width), F32),
            ((width, width), F32),
            ((3, width, width), F32),
        ],
        (pieces, other),
        flops=6 * width * width,
        moved=6 * width * width * 6,
        name="weight_gradients",
    )

    return (
        coded[None],
        grad_latents[None],
        shared_grad,
        value_grad,
        output_grad,
        taps_grad,
    )


def solution(mesh):
    placed = (
        P(("groups", "frame"), "row", None),
        P(("groups", "frame"), None),
        P(("groups", "frame")),
        P(("groups", "frame")),
        P(),
        P(),
        P(),
        P(),
        P(),
        P(("groups", "frame"), "row", None),
    )
    return jax.shard_map(
        local,
        mesh=mesh,
        in_specs=placed,
        out_specs=(
            P(("groups", "frame"), "row", None),
            P(("groups", "frame"), "row", None),
            P("groups", None),
            P("groups", None),
            P("groups", None),
            P("groups", None, None),
        ),
        check_vma=False,
    )
```

```python
import functools
import math

import jax
import jax.numpy as jnp
from jax import lax
from jax.experimental import pallas as pl
from jax.experimental.pallas import tpu as pltpu
from jax.sharding import PartitionSpec as P

HEADS = 8
DH = 32
COLS = 64
WMAX = 2
BROWS = 2
GROUP = 2

SCALE = 1.5 / math.sqrt(DH)
MASKED = -1e30
LOG2E = 1.4426950408889634
F32 = jnp.float32
BF16 = jnp.bfloat16
NN = (((1,), (0,)), ((), ()))
NT = (((1,), (1,)), ((), ()))


def dot(left, right, dims=NN):
    return lax.dot_general(left, right, dims, preferred_element_type=F32)


def halves_of(value):
    high = value.astype(BF16)
    return high, (value - high.astype(F32)).astype(BF16)


def left_split_dot(left, right, dims=NN):
    high, low = halves_of(left)
    return dot(high, right, dims) + dot(low, right, dims)


def right_split_dot(left, right, dims=NN):
    high, low = halves_of(right)
    return dot(left, high, dims) + dot(left, low, dims)


def swapped(array, axis, mask):
    pairs = [(i, i ^ mask) for i in range(lax.axis_size(axis))]
    return lax.ppermute(array, axis, pairs)


def along(array, parity, relayed=False):
    devices = lax.axis_size("frame")
    pairs = [(i, i + 2) for i in range(devices) if (i & 2) == parity and i + 2 < devices]
    pairs = pairs + [(j, i) for i, j in pairs]
    if relayed:
        pairs = [(i, j) for i, j in pairs if 0 <= 2 * i - j < devices]
    return lax.ppermute(array, "frame", pairs)


def whole_call(
    body, outs, args, smem=(), scratch=(), grid=None, flops=0, moved=0, name=None, vmem=16
):
    specs = [
        pl.BlockSpec(memory_space=pltpu.SMEM if i in smem else pltpu.VMEM)
        for i in range(len(args))
    ]
    more = {} if grid is None else {"grid": grid}
    return pl.pallas_call(
        body,
        out_shape=[jax.ShapeDtypeStruct(shape, dtype) for shape, dtype in outs],
        in_specs=specs,
        out_specs=[pl.BlockSpec(memory_space=pltpu.VMEM)] * len(outs),
        scratch_shapes=list(scratch),
        compiler_params=pltpu.CompilerParams(vmem_limit_bytes=vmem * 1024 * 1024),
        cost_estimate=pl.CostEstimate(flops=flops, bytes_accessed=moved, transcendentals=0),
        name=name,
        **more,
    )(*args)


def before_kernel(
    level, scale, edge, cot, tokens, taps, shared, outp,
    resid_out, rb_out, ext_out, up_out, upt_out, query_out, queryt_out, gain_out,
):
    row_id = lax.axis_index("row")
    count = cot.shape[0]
    gain = scale[pl.ds(level[0], 1), :]
    gain_out[...] = gain
    grad_z = cot[...].astype(F32) * gain
    got = (edge[...].astype(F32) * gain).astype(BF16)
    none = jnp.zeros_like(got)
    ext_out[:COLS] = jnp.where(row_id == 0, none, got)
    ext_out[COLS : COLS + count] = grad_z.astype(BF16)
    ext_out[COLS + count :] = jnp.where(row_id == 0, got, none)
    total = grad_z
    for tap in range(3):
        begin = (2 - tap) * COLS
        total = total + dot(ext_out[begin : begin + count], taps[tap], NT)
    resid_out[...] = total
    rounded = total.astype(BF16)
    rb_out[...] = rounded
    upstream = dot(rounded, outp[...], NT).astype(BF16)
    up_out[...] = upstream
    upt_out[...] = upstream.T
    query = dot(tokens[...], shared[...]).astype(BF16)
    query_out[...] = query
    queryt_out[...] = query.T


def attention_kernel(
    windows, slots, halo, query, queryt, up, upt, tokens, rb, ext, resid_grad, shared, value, outp,
    mid_out, send_out, keep_out, hidden_out, resid_out, base_out,
    key_all, val_all, key_blk, val_blk, keyt_blk, valt_blk, bias, mixed_all, dq_all, dkt, dvt, sums,
    score_all, grad_all, *, total_rows,
):
    step = pl.program_id(0)
    window, row_id = windows[0], lax.axis_index("row")
    width = query.shape[1]
    count = query.shape[0]
    rim = WMAX * COLS
    block = BROWS * COLS
    span = block + 2 * rim

    @pl.when(step == 0)
    def _():
        for slot in range(2):
            for weight, full in ((shared, key_all), (value, val_all)):
                full[slot, rim : rim + count] = dot(slots[slot], weight[...]).astype(BF16)
                far = dot(halo[slot], weight[...]).astype(BF16)
                none = jnp.zeros_like(far)
                full[slot, :rim] = jnp.where(row_id == 0, none, far)
                full[slot, rim + count :] = jnp.where(row_id == 0, far, none)
        dkt[...] = jnp.zeros_like(dkt)
        dvt[...] = jnp.zeros_like(dvt)

    begin = pl.multiple_of(step * block, block)
    for slot in range(2):
        key_blk[slot * span : (slot + 1) * span] = key_all[slot, pl.ds(begin, span)]
        val_blk[slot * span : (slot + 1) * span] = val_all[slot, pl.ds(begin, span)]
    keyt_blk[...] = key_blk[...].T
    valt_blk[...] = val_blk[...].T
    first_row = row_id * (count // COLS) + step * BROWS
    query_row = first_row + lax.broadcasted_iota(jnp.int32, (block, span), 0) // COLS
    key_row = first_row - WMAX + lax.broadcasted_iota(jnp.int32, (block, span), 1) // COLS
    near = jnp.abs(query_row - key_row) <= window
    allowed = near & (key_row >= 0) & (key_row < total_rows)
    one_bias = jnp.where(allowed, 0.0, MASKED)
    bias[:, :span] = one_bias
    bias[:, span:] = one_bias

    lane_head = lax.broadcasted_iota(jnp.int32, (1, width), 1) // DH
    masks = [(lane_head == head).astype(F32) for head in range(HEADS)]
    tall = GROUP * block
    group_bias = jnp.concatenate([bias[...]] * GROUP, 0)
    query_b, up_b = query[pl.ds(begin, block), :], up[pl.ds(begin, block), :]
    mixed = jnp.zeros((block, width), F32)
    grad_q = jnp.zeros((block, width), F32)

    def products(group):
        own = masks[group * GROUP : (group + 1) * GROUP]
        stacked_q = jnp.concatenate([query_b * mask.astype(BF16) for mask in own], 0)
        stacked_u = jnp.concatenate([up_b * mask.astype(BF16) for mask in own], 0)
        rows = slice(group * tall, (group + 1) * tall)
        score_all[rows] = dot(stacked_q, keyt_blk[...])
        grad_all[rows] = dot(stacked_u, valt_blk[...])

    products(0)
    for group in range(HEADS // GROUP):
        if (group + 1) * GROUP < HEADS:
            products(group + 1)
        rows = slice(group * tall, (group + 1) * tall)
        scores = score_all[rows] + group_bias
        top = jnp.max(scores, axis=1, keepdims=True)
        terms = jnp.exp2((scores - top) * (SCALE * LOG2E))
        weights = terms * (1.0 / jnp.sum(terms, axis=1, keepdims=True))
        prob = weights.astype(BF16)
        grad_prob = grad_all[rows]
        inner = jnp.sum(weights * grad_prob, axis=1, keepdims=True)
        grad_score = ((weights * (grad_prob - inner)) * SCALE).astype(BF16)
        mixed_g = dot(prob, val_blk[...])
        grad_q_g = dot(grad_score, key_blk[...])
        for member in range(GROUP):
            head = group * GROUP + member
            part = slice(member * block, (member + 1) * block)
            mixed = mixed + mixed_g[part] * masks[head]
            grad_q = grad_q + grad_q_g[part] * masks[head]
            lanes = slice(head * DH, (head + 1) * DH)
            dv = dot(upt[lanes, pl.ds(begin, block)], prob[part])
            dk = dot(queryt[lanes, pl.ds(begin, block)], grad_score[part])
            for slot in range(2):
                keys = slice(slot * span, (slot + 1) * span)
                dvt[slot, lanes, pl.ds(begin, span)] += dv[:, keys]
                dkt[slot, lanes, pl.ds(begin, span)] += dk[:, keys]
    mixed_all[pl.ds(begin, block), :] = mixed.astype(BF16)
    dq_all[pl.ds(begin, block), :] = grad_q

    @pl.when(step == pl.num_programs(0) - 1)
    def _():
        def far_rim(array):
            upper, lower = array[:, :rim], array[:, rim + count :]
            return jnp.where(row_id == 0, lower, upper)

        half = 3 * width
        middle = slice(rim, rim + count)
        grad_q = dq_all[...]
        shared_t = jnp.zeros((width, width), F32)
        value_t = jnp.zeros((width, width), F32)
        for slot in range(2):
            part = jnp.zeros((width, count + 2 * rim), F32)
            for piece in halves_of(dkt[slot]):
                part = part + dot(shared[...], piece)
                rims = far_rim(piece)
                shared_t += dot(piece[:, middle], slots[slot]) + dot(rims, halo[slot])
            for piece in halves_of(dvt[slot]):
                part = part + dot(value[...], piece)
                rims = far_rim(piece)
                value_t += dot(piece[:, middle], slots[slot]) + dot(rims, halo[slot])
            mid_out[slot] = part[:, middle]
            send_out[half:, slot * rim : (slot + 1) * rim] = far_rim(part).astype(BF16)
        base_out[...] = resid_grad[...] + left_split_dot(grad_q, shared[...], NT)
        sums[:width] = right_split_dot(tokens[...].T, grad_q) + shared_t.T
        sums[width : 2 * width] = value_t.T
        mixed_full = mixed_all[...]
        residual = tokens[...].astype(F32) + dot(mixed_full, outp[...])
        resid_out[...] = residual
        hidden = residual.astype(BF16)
        hidden_out[...] = hidden
        sums[2 * width : half] = dot(mixed_full.T, rb[...])
        hidden_t = hidden.T
        for tap in range(3):
            start = (2 - tap) * COLS
            sums[half + tap * width : half + (tap + 1) * width] = dot(
                hidden_t, ext[start : start + count]
            )
        keep_out[...] = sums[pl.ds(pl.multiple_of(row_id * half, half), half)]
        send_out[:half] = sums[pl.ds(pl.multiple_of((1 - row_id) * half, half), half)].astype(BF16)


def spread_kernel(
    refs, mid, keep, got,
    pair_out, across_out, first_out, second_out, third_out, first_keep, second_keep, own_out,
):
    frame_id, row_id = lax.axis_index("frame"), lax.axis_index("row")
    steps = [refs[0, 0] - frame_id, refs[0, 1] - frame_id]
    width, count = mid.shape[1], mid.shape[2]
    rim = WMAX * COLS
    half = keep.shape[0]
    piece = half // 4

    def folded(slot):
        rims = got[half:, slot * rim : (slot + 1) * rim].astype(F32)
        none = jnp.zeros_like(rims)
        part = mid[slot]
        first = part[:, :rim] + jnp.where(row_id == 0, none, rims)
        last = part[:, count - rim :] + jnp.where(row_id == 0, rims, none)
        return jnp.concatenate([first, part[:, rim : count - rim], last], 1)

    pair_step = jnp.where((frame_id & 1) == 0, 1, -1)
    link_step = jnp.where((frame_id & 2) == 0, 1, -1)
    for step, out in (
        (pair_step, pair_out),
        (-pair_step, across_out),
        (4 * link_step, first_out),
        (-4 * link_step, second_out),
        (2 * link_step, first_keep),
        (-2 * link_step, second_keep),
    ):
        by_zero, by_one = steps[0] == step, steps[1] == step

        @pl.when(by_zero & by_one)
        def _(out=out):
            out[:width] = (folded(0) + folded(1)).astype(out.dtype)

        @pl.when(by_zero & ~by_one)
        def _(out=out):
            out[:width] = folded(0).astype(out.dtype)

        @pl.when(by_one & ~by_zero)
        def _(out=out):
            out[:width] = folded(1).astype(out.dtype)

        @pl.when(~by_zero & ~by_one)
        def _(out=out):
            out[:width] = jnp.zeros((width, count), out.dtype)

    me = frame_id & 3

    def rows_of(index):
        rows = pl.ds(pl.multiple_of(index * piece, piece), piece)
        return keep[rows] + got[rows].astype(F32)

    own_out[...] = rows_of(me)
    for mask, out, begin in ((1, across_out, width), (2, first_out, width), (3, third_out, 0)):
        rows = rows_of(me ^ mask).astype(BF16)
        out[begin:, :width] = rows[: piece // 2]
        out[begin:, width:] = rows[piece // 2 :]


def coded_kernel(hidden, halo, residual, gain, taps, coded_out, gain_out, ext):
    gain_out[...] = gain[...]
    row_id = lax.axis_index("row")
    count = hidden.shape[0]
    got = halo[...]
    none = jnp.zeros_like(got)
    ext[:COLS] = jnp.where(row_id == 0, none, got)
    ext[COLS : COLS + count] = hidden[...]
    ext[COLS + count :] = jnp.where(row_id == 0, got, none)
    total = jnp.zeros((count, hidden.shape[1]), F32)
    for tap in range(3):
        begin = tap * COLS
        total = total + dot(ext[begin : begin + count], taps[tap])
    coded_out[...] = ((residual[...] + total) * gain[...]).astype(BF16)


def select_kernel(refs, pair, cross, first, second, far_first, far_second, _, slots_out, edge_out):
    frame_id, row_id = lax.axis_index("frame"), lax.axis_index("row")
    count = pair.shape[0]
    rim = WMAX * COLS
    pair_step = jnp.where((frame_id & 1) == 0, 1, -1)
    link_step = jnp.where((frame_id & 2) == 0, 2, -2)
    for slot in range(2):
        step = refs[0, slot] - frame_id
        for distance, source in (
            (pair_step, pair),
            (-pair_step, cross),
            (link_step, first),
            (-link_step, second),
            (2 * link_step, far_first),
            (-2 * link_step, far_second),
        ):

            @pl.when(step == distance)
            def _(source=source):
                slots_out[slot] = source[:count]
                begin = pl.multiple_of((1 - row_id) * (count - rim), rim)
                edge_out[slot] = source[pl.ds(begin, rim)]


def relay_kernel(
    across, first, second, third, first_keep, second_keep, own, _,
    first_out, second_out, own_out,
):
    frame_id = lax.axis_index("frame")
    width = first_keep.shape[0]
    packed = third.shape[0]
    crossing = across[:width].astype(F32)
    none = jnp.zeros_like(crossing)
    with_first = (frame_id & 1) == ((frame_id >> 1) & 1)
    first_out[...] = (
        first_keep[...] + second[...].astype(F32) + jnp.where(with_first, crossing, none)
    ).astype(BF16)
    second_out[...] = (
        second_keep[...] + first[:width].astype(F32) + jnp.where(with_first, none, crossing)
    ).astype(BF16)
    for part in range(2):
        rows = slice(part * packed, (part + 1) * packed)
        lanes = slice(part * width, (part + 1) * width)
        own_out[rows] = (
            (own[rows] + across[width:, lanes].astype(F32))
            + (first[width:, lanes].astype(F32) + third[:, lanes].astype(F32))
        ).astype(BF16)


def final_kernel(base, first, second, pair, grad_out, last_out):
    returned = first[...].astype(F32) + second[...].astype(F32) + pair[...].astype(F32)
    grad_out[...] = (base[...] + returned.T).astype(BF16)
    last_out[...] = returned[:16, :128]


def total_kernel(own, other, _, own_out):
    own_out[...] = (own[...].astype(F32) + other[...].astype(F32)).astype(BF16)


def gather_kernel(own, first, second, third, _, pieces_out):
    me = lax.axis_index("frame") & 3
    piece = own.shape[0]
    for mask, part in enumerate((own, first, second, third)):
        begin = pl.multiple_of((me ^ mask) * piece, piece)
        pieces_out[pl.ds(begin, piece)] = part[...]


def weights_kernel(own, other, shared_out, value_out, output_out, taps_out, *, norm):
    row_id = lax.axis_index("row")
    width = shared_out.shape[1]
    low = jnp.where(row_id == 0, own[...].astype(F32), other[...].astype(F32)) * norm
    high = jnp.where(row_id == 0, other[...].astype(F32), own[...].astype(F32)) * norm
    shared_out[...] = low[:width]
    value_out[...] = low[width : 2 * width]
    output_out[...] = low[2 * width :]
    for tap in range(3):
        taps_out[tap] = high[tap * width : (tap + 1) * width]


def local(
    latents, ref_frames, windows, quant_level, quant_scale,
    shared_proj, value_proj, output_proj, conv_taps, cotangent,
):
    width = latents.shape[2]
    count = latents.shape[1]
    rows_dev = count // COLS
    frames = lax.axis_size("frame")
    total_rows = rows_dev * lax.axis_size("row")
    row_id = lax.axis_index("row")
    rim = WMAX * COLS
    tokens = latents[0]
    cot = cotangent[0]

    cot_edge = swapped(jnp.where(row_id == 0, cot[count - COLS :], cot[:COLS]), "row", 1)
    from_first = along(tokens, 0)
    from_second = along(tokens, 2)
    from_pair = swapped(tokens, "frame", 1)

    grad_resid, grad_rb, grad_ext, up, upt, query, queryt, gain = whole_call(
        before_kernel,
        [
            ((count, width), F32),
            ((count, width), BF16),
            ((count + 2 * COLS, width), BF16),
            ((count, width), BF16),
            ((width, count), BF16),
            ((count, width), BF16),
            ((width, count), BF16),
            ((1, width), F32),
        ],
        (
            quant_level, quant_scale, cot_edge, cot, tokens, conv_taps, shared_proj, output_proj,
        ),
        smem=(0,),
        flops=2 * 5 * count * width * width,
        moved=4 * count * width * 6,
        name="gradient_path",
    )

    frame_id = lax.axis_index("frame")
    by_second = (frame_id & 1) != ((frame_id >> 1) & 1)
    longer = jnp.concatenate([from_second, from_second[:COLS]], 0)
    far_first = along(longer, 0, relayed=True)
    far_second = along(from_first, 2, relayed=True)
    from_cross = swapped(jnp.where(by_second, from_second, from_first), "frame", 1)
    slots, edge = whole_call(
        select_kernel,
        [((2, count, width), BF16), ((2, rim, width), BF16)],
        (ref_frames, from_pair, from_cross, from_first, from_second, far_first, far_second, gain),
        smem=(0,),
        flops=count * width,
        moved=count * width * 8,
        name="slots",
    )
    halo = swapped(edge, "row", 1)

    block = BROWS * COLS
    span = block + 2 * rim
    ext_count = count + 2 * rim
    half = 3 * width
    mid, send, keep, hidden, residual, base = whole_call(
        functools.partial(attention_kernel, total_rows=total_rows),
        [
            ((2, width, count), F32),
            ((half + width, width), BF16),
            ((half, width), F32),
            ((count, width), BF16),
            ((count, width), F32),
            ((count, width), F32),
        ],
        (
            windows, slots, halo, query, queryt, up, upt, tokens, grad_rb, grad_ext, grad_resid,
            shared_proj, value_proj, output_proj,
        ),
        smem=(0,),
        scratch=[
            pltpu.VMEM((2, ext_count, width), BF16),
            pltpu.VMEM((2, ext_count, width), BF16),
            pltpu.VMEM((2 * span, width), BF16),
            pltpu.VMEM((2 * span, width), BF16),
            pltpu.VMEM((width, 2 * span), BF16),
            pltpu.VMEM((width, 2 * span), BF16),
            pltpu.VMEM((block, 2 * span), F32),
            pltpu.VMEM((count, width), BF16),
            pltpu.VMEM((count, width), F32),
            pltpu.VMEM((2, width, ext_count), F32),
            pltpu.VMEM((2, width, ext_count), F32),
            pltpu.VMEM((2 * half, width), F32),
            pltpu.VMEM((HEADS * block, 2 * span), F32),
            pltpu.VMEM((HEADS * block, 2 * span), F32),
        ],
        grid=(count // block,),
        flops=6 * 2 * count * 2 * span * width * HEADS,
        moved=count * width * 60,
        name="attention",
        vmem=28,
    )

    got = swapped(send, "row", 1)
    hidden_edge = jnp.where(row_id == 0, hidden[count - COLS :], hidden[:COLS])
    hidden_halo = swapped(hidden_edge, "row", 1)
    piece = half // 4
    packed = piece // 2
    pair, across, first, second, third, first_keep, second_keep, own = whole_call(
        spread_kernel,
        [
            ((width, count), BF16),
            ((width + packed, count), BF16),
            ((width + packed, count), BF16),
            ((width, count), BF16),
            ((packed, count), BF16),
            ((width, count), F32),
            ((width, count), F32),
            ((piece, width), F32),
        ],
        (ref_frames, mid, keep, got),
        smem=(0,),
        flops=count * width * 12,
        moved=count * width * 30,
        name="spread",
    )

    third = swapped(third, "frame", 3)
    across = swapped(across, "frame", 1)
    first = along(first, 0)
    second = along(second, 2)
    coded, gain = whole_call(
        coded_kernel,
        [((count, width), BF16), ((1, width), F32)],
        (hidden, hidden_halo, residual, gain, conv_taps),
        scratch=[pltpu.VMEM((count + 2 * COLS, width), BF16)],
        flops=2 * 3 * count * width * width,
        moved=count * width * 8,
        name="context",
    )
    back_first, back_second, own = whole_call(
        relay_kernel,
        [
            ((width, count), BF16),
            ((width, count), BF16),
            ((piece, width), BF16),
        ],
        (across, first, second, third, first_keep, second_keep, own, gain),
        flops=count * width * 4,
        moved=count * width * 16,
        name="relay",
    )
    mask = 4
    other = swapped(own, "frame", mask)
    back_first = along(back_first, 0)
    back_second = along(back_second, 2)
    back_pair = swapped(pair, "frame", 1)
    while 2 * mask < frames:
        mask *= 2
        own = (own.astype(F32) + other.astype(F32)).astype(BF16)
        other = swapped(own, "frame", mask)
    own = (own.astype(F32) + other.astype(F32)).astype(BF16)
    grad_latents, last = whole_call(
        final_kernel,
        [((count, width), BF16), ((16, 128), F32)],
        (base, back_first, back_second, back_pair),
        flops=count * width * 4,
        moved=count * width * 12,
        name="latent_gradient",
    )
    (pieces,) = whole_call(
        gather_kernel,
        [((half, width), BF16)],
        (own, *[swapped(own, "frame", mask) for mask in (1, 2, 3)], last),
        flops=half * width,
        moved=half * width * 4,
        name="pieces",
    )
    other = swapped(pieces, "row", 1)
    shared_grad, value_grad, output_grad, taps_grad = whole_call(
        functools.partial(
            weights_kernel, norm=1.0 / math.sqrt(frames * total_rows * COLS)
        ),
        [
            ((width, width), F32),
            ((width, width), F32),
            ((width, width), F32),
            ((3, width, width), F32),
        ],
        (pieces, other),
        flops=6 * width * width,
        moved=6 * width * width * 6,
        name="weight_gradients",
    )

    return (
        coded[None],
        grad_latents[None],
        shared_grad,
        value_grad,
        output_grad,
        taps_grad,
    )


def solution(mesh):
    placed = (
        P(("groups", "frame"), "row", None),
        P(("groups", "frame"), None),
        P(("groups", "frame")),
        P(("groups", "frame")),
        P(),
        P(),
        P(),
        P(),
        P(),
        P(("groups", "frame"), "row", None),
    )
    return jax.shard_map(
        local,
        mesh=mesh,
        in_specs=placed,
        out_specs=(
            P(("groups", "frame"), "row", None),
            P(("groups", "frame"), "row", None),
            P("groups", None),
            P("groups", None),
            P("groups", None),
            P("groups", None, None),
        ),
        check_vma=False,
    )
```

```python
import functools
import math

import jax
import jax.numpy as jnp
from jax import lax
from jax.experimental import pallas as pl
from jax.experimental.pallas import tpu as pltpu
from jax.sharding import PartitionSpec as P

HEADS = 8
DH = 32
COLS = 64
WMAX = 2
BROWS = 2
GROUP = 2

SCALE = 1.5 / math.sqrt(DH)
MASKED = -1e30
LOG2E = 1.4426950408889634
F32 = jnp.float32
BF16 = jnp.bfloat16
NN = (((1,), (0,)), ((), ()))
NT = (((1,), (1,)), ((), ()))


def dot(left, right, dims=NN):
    return lax.dot_general(left, right, dims, preferred_element_type=F32)


def halves_of(value):
    high = value.astype(BF16)
    return high, (value - high.astype(F32)).astype(BF16)


def left_split_dot(left, right, dims=NN):
    high, low = halves_of(left)
    return dot(high, right, dims) + dot(low, right, dims)


def right_split_dot(left, right, dims=NN):
    high, low = halves_of(right)
    return dot(left, high, dims) + dot(left, low, dims)


def swapped(array, axis, mask):
    pairs = [(i, i ^ mask) for i in range(lax.axis_size(axis))]
    return lax.ppermute(array, axis, pairs)


def along(array, parity, relayed=False, passed_on=False):
    devices = lax.axis_size("frame")
    pairs = [(i, i + 2) for i in range(devices) if (i & 2) == parity and i + 2 < devices]
    pairs = pairs + [(j, i) for i, j in pairs]
    if relayed:
        pairs = [(i, j) for i, j in pairs if 0 <= 2 * i - j < devices]
    if passed_on:
        pairs = [(i, j) for i, j in pairs if 0 <= 2 * j - i < devices]
    return lax.ppermute(array, "frame", pairs)


def whole_call(
    body, outs, args, smem=(), scratch=(), grid=None, flops=0, moved=0, name=None, vmem=16
):
    specs = [
        pl.BlockSpec(memory_space=pltpu.SMEM if i in smem else pltpu.VMEM)
        for i in range(len(args))
    ]
    more = {} if grid is None else {"grid": grid}
    return pl.pallas_call(
        body,
        out_shape=[jax.ShapeDtypeStruct(shape, dtype) for shape, dtype in outs],
        in_specs=specs,
        out_specs=[pl.BlockSpec(memory_space=pltpu.VMEM)] * len(outs),
        scratch_shapes=list(scratch),
        compiler_params=pltpu.CompilerParams(vmem_limit_bytes=vmem * 1024 * 1024),
        cost_estimate=pl.CostEstimate(flops=flops, bytes_accessed=moved, transcendentals=0),
        name=name,
        **more,
    )(*args)


def before_kernel(
    level, scale, edge, cot, tokens, taps, shared, outp,
    resid_out, rb_out, ext_out, up_out, upt_out, query_out, queryt_out, gain_out,
):
    row_id = lax.axis_index("row")
    count = cot.shape[0]
    gain = scale[pl.ds(level[0], 1), :]
    gain_out[...] = gain
    grad_z = cot[...].astype(F32) * gain
    got = (edge[...].astype(F32) * gain).astype(BF16)
    none = jnp.zeros_like(got)
    ext_out[:COLS] = jnp.where(row_id == 0, none, got)
    ext_out[COLS : COLS + count] = grad_z.astype(BF16)
    ext_out[COLS + count :] = jnp.where(row_id == 0, got, none)
    total = grad_z
    for tap in range(3):
        begin = (2 - tap) * COLS
        total = total + dot(ext_out[begin : begin + count], taps[tap], NT)
    resid_out[...] = total
    rounded = total.astype(BF16)
    rb_out[...] = rounded
    upstream = dot(rounded, outp[...], NT).astype(BF16)
    up_out[...] = upstream
    upt_out[...] = upstream.T
    query = dot(tokens[...], shared[...]).astype(BF16)
    query_out[...] = query
    queryt_out[...] = query.T


def attention_kernel(
    windows, slots, halo, query, queryt, up, upt, tokens, rb, ext, resid_grad, shared, value, outp,
    mid_out, send_out, keep_out, hidden_out, resid_out, base_out,
    key_all, val_all, key_blk, val_blk, keyt_blk, valt_blk, bias, mixed_all, dq_all, dkt, dvt, sums,
    score_all, grad_all, *, total_rows,
):
    step = pl.program_id(0)
    window, row_id = windows[0], lax.axis_index("row")
    width = query.shape[1]
    count = query.shape[0]
    rim = WMAX * COLS
    block = BROWS * COLS
    span = block + 2 * rim

    @pl.when(step == 0)
    def _():
        for slot in range(2):
            for weight, full in ((shared, key_all), (value, val_all)):
                full[slot, rim : rim + count] = dot(slots[slot], weight[...]).astype(BF16)
                far = dot(halo[slot], weight[...]).astype(BF16)
                none = jnp.zeros_like(far)
                full[slot, :rim] = jnp.where(row_id == 0, none, far)
                full[slot, rim + count :] = jnp.where(row_id == 0, far, none)
        dkt[...] = jnp.zeros_like(dkt)
        dvt[...] = jnp.zeros_like(dvt)

    begin = pl.multiple_of(step * block, block)
    for slot in range(2):
        key_blk[slot * span : (slot + 1) * span] = key_all[slot, pl.ds(begin, span)]
        val_blk[slot * span : (slot + 1) * span] = val_all[slot, pl.ds(begin, span)]
    keyt_blk[...] = key_blk[...].T
    valt_blk[...] = val_blk[...].T
    first_row = row_id * (count // COLS) + step * BROWS
    query_row = first_row + lax.broadcasted_iota(jnp.int32, (block, span), 0) // COLS
    key_row = first_row - WMAX + lax.broadcasted_iota(jnp.int32, (block, span), 1) // COLS
    near = jnp.abs(query_row - key_row) <= window
    allowed = near & (key_row >= 0) & (key_row < total_rows)
    one_bias = jnp.where(allowed, 0.0, MASKED)
    bias[:, :span] = one_bias
    bias[:, span:] = one_bias

    lane_head = lax.broadcasted_iota(jnp.int32, (1, width), 1) // DH
    masks = [(lane_head == head).astype(F32) for head in range(HEADS)]
    tall = GROUP * block
    group_bias = jnp.concatenate([bias[...]] * GROUP, 0)
    query_b, up_b = query[pl.ds(begin, block), :], up[pl.ds(begin, block), :]
    mixed = jnp.zeros((block, width), F32)
    grad_q = jnp.zeros((block, width), F32)

    def products(group):
        own = masks[group * GROUP : (group + 1) * GROUP]
        stacked_q = jnp.concatenate([query_b * mask.astype(BF16) for mask in own], 0)
        stacked_u = jnp.concatenate([up_b * mask.astype(BF16) for mask in own], 0)
        rows = slice(group * tall, (group + 1) * tall)
        score_all[rows] = dot(stacked_q, keyt_blk[...])
        grad_all[rows] = dot(stacked_u, valt_blk[...])

    products(0)
    for group in range(HEADS // GROUP):
        if (group + 1) * GROUP < HEADS:
            products(group + 1)
        rows = slice(group * tall, (group + 1) * tall)
        scores = score_all[rows] + group_bias
        top = jnp.max(scores, axis=1, keepdims=True)
        terms = jnp.exp2((scores - top) * (SCALE * LOG2E))
        weights = terms * (1.0 / jnp.sum(terms, axis=1, keepdims=True))
        prob = weights.astype(BF16)
        grad_prob = grad_all[rows]
        inner = jnp.sum(weights * grad_prob, axis=1, keepdims=True)
        grad_score = ((weights * (grad_prob - inner)) * SCALE).astype(BF16)
        mixed_g = dot(prob, val_blk[...])
        grad_q_g = dot(grad_score, key_blk[...])
        for member in range(GROUP):
            head = group * GROUP + member
            part = slice(member * block, (member + 1) * block)
            mixed = mixed + mixed_g[part] * masks[head]
            grad_q = grad_q + grad_q_g[part] * masks[head]
            lanes = slice(head * DH, (head + 1) * DH)
            dv = dot(upt[lanes, pl.ds(begin, block)], prob[part])
            dk = dot(queryt[lanes, pl.ds(begin, block)], grad_score[part])
            for slot in range(2):
                keys = slice(slot * span, (slot + 1) * span)
                dvt[slot, lanes, pl.ds(begin, span)] += dv[:, keys]
                dkt[slot, lanes, pl.ds(begin, span)] += dk[:, keys]
    mixed_all[pl.ds(begin, block), :] = mixed.astype(BF16)
    dq_all[pl.ds(begin, block), :] = grad_q

    @pl.when(step == pl.num_programs(0) - 1)
    def _():
        def far_rim(array):
            upper, lower = array[:, :rim], array[:, rim + count :]
            return jnp.where(row_id == 0, lower, upper)

        half = 3 * width
        middle = slice(rim, rim + count)
        grad_q = dq_all[...]
        shared_t = jnp.zeros((width, width), F32)
        value_t = jnp.zeros((width, width), F32)
        for slot in range(2):
            part = jnp.zeros((width, count + 2 * rim), F32)
            for piece in halves_of(dkt[slot]):
                part = part + dot(shared[...], piece)
                rims = far_rim(piece)
                shared_t += dot(piece[:, middle], slots[slot]) + dot(rims, halo[slot])
            for piece in halves_of(dvt[slot]):
                part = part + dot(value[...], piece)
                rims = far_rim(piece)
                value_t += dot(piece[:, middle], slots[slot]) + dot(rims, halo[slot])
            mid_out[slot] = part[:, middle]
            send_out[half:, slot * rim : (slot + 1) * rim] = far_rim(part).astype(BF16)
        base_out[...] = resid_grad[...] + left_split_dot(grad_q, shared[...], NT)
        sums[:width] = right_split_dot(tokens[...].T, grad_q) + shared_t.T
        sums[width : 2 * width] = value_t.T
        mixed_full = mixed_all[...]
        residual = tokens[...].astype(F32) + dot(mixed_full, outp[...])
        resid_out[...] = residual
        hidden = residual.astype(BF16)
        hidden_out[...] = hidden
        sums[2 * width : half] = dot(mixed_full.T, rb[...])
        hidden_t = hidden.T
        for tap in range(3):
            start = (2 - tap) * COLS
            sums[half + tap * width : half + (tap + 1) * width] = dot(
                hidden_t, ext[start : start + count]
            )
        keep_out[...] = sums[pl.ds(pl.multiple_of(row_id * half, half), half)]
        send_out[:half] = sums[pl.ds(pl.multiple_of((1 - row_id) * half, half), half)].astype(BF16)


def spread_kernel(
    refs, mid, keep, got,
    pair_out, across_out, first_out, second_out, one_out, two_out, three_out,
    first_keep, second_keep, own_out,
):
    frame_id, row_id = lax.axis_index("frame"), lax.axis_index("row")
    steps = [refs[0, 0] - frame_id, refs[0, 1] - frame_id]
    width, count = mid.shape[1], mid.shape[2]
    rim = WMAX * COLS
    half = keep.shape[0]
    piece = half // 4

    def folded(slot):
        rims = got[half:, slot * rim : (slot + 1) * rim].astype(F32)
        none = jnp.zeros_like(rims)
        part = mid[slot]
        first = part[:, :rim] + jnp.where(row_id == 0, none, rims)
        last = part[:, count - rim :] + jnp.where(row_id == 0, rims, none)
        return jnp.concatenate([first, part[:, rim : count - rim], last], 1)

    pair_step = jnp.where((frame_id & 1) == 0, 1, -1)
    link_step = jnp.where((frame_id & 2) == 0, 1, -1)
    for step, out in (
        (pair_step, pair_out),
        (-pair_step, across_out),
        (4 * link_step, first_out),
        (-4 * link_step, second_out),
        (2 * link_step, first_keep),
        (-2 * link_step, second_keep),
    ):
        by_zero, by_one = steps[0] == step, steps[1] == step

        @pl.when(by_zero & by_one)
        def _(out=out):
            out[:width] = (folded(0) + folded(1)).astype(out.dtype)

        @pl.when(by_zero & ~by_one)
        def _(out=out):
            out[:width] = folded(0).astype(out.dtype)

        @pl.when(by_one & ~by_zero)
        def _(out=out):
            out[:width] = folded(1).astype(out.dtype)

        @pl.when(~by_zero & ~by_one)
        def _(out=out):
            out[:width] = jnp.zeros((width, count), out.dtype)

    me = frame_id & 3

    def rows_of(index):
        rows = pl.ds(pl.multiple_of(index * piece, piece), piece)
        return keep[rows] + got[rows].astype(F32)

    own_out[...] = rows_of(me)
    for mask, out in ((1, one_out), (2, two_out), (3, three_out)):
        out[...] = rows_of(me ^ mask).astype(BF16)


def coded_kernel(hidden, halo, residual, gain, taps, coded_out, gain_out, ext):
    gain_out[...] = gain[...]
    row_id = lax.axis_index("row")
    count = hidden.shape[0]
    got = halo[...]
    none = jnp.zeros_like(got)
    ext[:COLS] = jnp.where(row_id == 0, none, got)
    ext[COLS : COLS + count] = hidden[...]
    ext[COLS + count :] = jnp.where(row_id == 0, got, none)
    total = jnp.zeros((count, hidden.shape[1]), F32)
    for tap in range(3):
        begin = tap * COLS
        total = total + dot(ext[begin : begin + count], taps[tap])
    coded_out[...] = ((residual[...] + total) * gain[...]).astype(BF16)


def select_kernel(refs, pair, cross, first, second, far_first, far_second, _, slots_out, edge_out):
    frame_id, row_id = lax.axis_index("frame"), lax.axis_index("row")
    count = pair.shape[0]
    rim = WMAX * COLS
    pair_step = jnp.where((frame_id & 1) == 0, 1, -1)
    link_step = jnp.where((frame_id & 2) == 0, 2, -2)
    for slot in range(2):
        step = refs[0, slot] - frame_id
        for distance, source in (
            (pair_step, pair),
            (-pair_step, cross),
            (link_step, first),
            (-link_step, second),
            (2 * link_step, far_first),
            (-2 * link_step, far_second),
        ):

            @pl.when(step == distance)
            def _(source=source):
                slots_out[slot] = source[:count]
                begin = pl.multiple_of((1 - row_id) * (count - rim), rim)
                edge_out[slot] = source[pl.ds(begin, rim)]


def relay_kernel(
    across, first, second, first_keep, second_keep, _,
    first_out, second_out,
):
    frame_id = lax.axis_index("frame")
    crossing = across[...].astype(F32)
    none = jnp.zeros_like(crossing)
    with_first = (frame_id & 1) == ((frame_id >> 1) & 1)
    first_out[...] = (
        first_keep[...] + second[...].astype(F32) + jnp.where(with_first, crossing, none)
    ).astype(BF16)
    second_out[...] = (
        second_keep[...] + first[...].astype(F32) + jnp.where(with_first, none, crossing)
    ).astype(BF16)


def final_kernel(base, first, second, pair, grad_out, last_out):
    returned = first[...].astype(F32) + second[...].astype(F32) + pair[...].astype(F32)
    grad_out[...] = (base[...] + returned.T).astype(BF16)
    last_out[...] = returned[:16, :128]


def gather_kernel(own, first, second, third, _, pieces_out):
    me = lax.axis_index("frame") & 3
    piece = own.shape[0]
    for mask, part in enumerate((own, first, second, third)):
        begin = pl.multiple_of((me ^ mask) * piece, piece)
        pieces_out[pl.ds(begin, piece)] = part[...]


def weights_kernel(own, other, shared_out, value_out, output_out, taps_out, *, norm):
    row_id = lax.axis_index("row")
    width = shared_out.shape[1]
    low = jnp.where(row_id == 0, own[...].astype(F32), other[...].astype(F32)) * norm
    high = jnp.where(row_id == 0, other[...].astype(F32), own[...].astype(F32)) * norm
    shared_out[...] = low[:width]
    value_out[...] = low[width : 2 * width]
    output_out[...] = low[2 * width :]
    for tap in range(3):
        taps_out[tap] = high[tap * width : (tap + 1) * width]


def local(
    latents, ref_frames, windows, quant_level, quant_scale,
    shared_proj, value_proj, output_proj, conv_taps, cotangent,
):
    width = latents.shape[2]
    count = latents.shape[1]
    rows_dev = count // COLS
    frames = lax.axis_size("frame")
    total_rows = rows_dev * lax.axis_size("row")
    row_id = lax.axis_index("row")
    rim = WMAX * COLS
    tokens = latents[0]
    cot = cotangent[0]

    cot_edge = swapped(jnp.where(row_id == 0, cot[count - COLS :], cot[:COLS]), "row", 1)
    from_first = along(tokens, 0)
    from_second = along(tokens, 2)
    from_pair = swapped(tokens, "frame", 1)

    grad_resid, grad_rb, grad_ext, up, upt, query, queryt, gain = whole_call(
        before_kernel,
        [
            ((count, width), F32),
            ((count, width), BF16),
            ((count + 2 * COLS, width), BF16),
            ((count, width), BF16),
            ((width, count), BF16),
            ((count, width), BF16),
            ((width, count), BF16),
            ((1, width), F32),
        ],
        (
            quant_level, quant_scale, cot_edge, cot, tokens, conv_taps, shared_proj, output_proj,
        ),
        smem=(0,),
        flops=2 * 5 * count * width * width,
        moved=4 * count * width * 6,
        name="gradient_path",
    )

    frame_id = lax.axis_index("frame")
    by_second = (frame_id & 1) != ((frame_id >> 1) & 1)
    longer = jnp.concatenate([from_second, from_second[:COLS]], 0)
    far_first = along(longer, 0, relayed=True)
    far_second = along(from_first, 2, relayed=True)
    from_cross = swapped(jnp.where(by_second, from_second, from_first), "frame", 1)
    slots, edge = whole_call(
        select_kernel,
        [((2, count, width), BF16), ((2, rim, width), BF16)],
        (ref_frames, from_pair, from_cross, from_first, from_second, far_first, far_second, gain),
        smem=(0,),
        flops=count * width,
        moved=count * width * 8,
        name="slots",
    )
    halo = swapped(edge, "row", 1)

    block = BROWS * COLS
    span = block + 2 * rim
    ext_count = count + 2 * rim
    half = 3 * width
    mid, send, keep, hidden, residual, base = whole_call(
        functools.partial(attention_kernel, total_rows=total_rows),
        [
            ((2, width, count), F32),
            ((half + width, width), BF16),
            ((half, width), F32),
            ((count, width), BF16),
            ((count, width), F32),
            ((count, width), F32),
        ],
        (
            windows, slots, halo, query, queryt, up, upt, tokens, grad_rb, grad_ext, grad_resid,
            shared_proj, value_proj, output_proj,
        ),
        smem=(0,),
        scratch=[
            pltpu.VMEM((2, ext_count, width), BF16),
            pltpu.VMEM((2, ext_count, width), BF16),
            pltpu.VMEM((2 * span, width), BF16),
            pltpu.VMEM((2 * span, width), BF16),
            pltpu.VMEM((width, 2 * span), BF16),
            pltpu.VMEM((width, 2 * span), BF16),
            pltpu.VMEM((block, 2 * span), F32),
            pltpu.VMEM((count, width), BF16),
            pltpu.VMEM((count, width), F32),
            pltpu.VMEM((2, width, ext_count), F32),
            pltpu.VMEM((2, width, ext_count), F32),
            pltpu.VMEM((2 * half, width), F32),
            pltpu.VMEM((HEADS * block, 2 * span), F32),
            pltpu.VMEM((HEADS * block, 2 * span), F32),
        ],
        grid=(count // block,),
        flops=6 * 2 * count * 2 * span * width * HEADS,
        moved=count * width * 60,
        name="attention",
        vmem=28,
    )

    got = swapped(send, "row", 1)
    hidden_edge = jnp.where(row_id == 0, hidden[count - COLS :], hidden[:COLS])
    hidden_halo = swapped(hidden_edge, "row", 1)
    piece = half // 4
    pair, across, first, second, one, two, three, first_keep, second_keep, own = whole_call(
        spread_kernel,
        [
            ((width, count), BF16),
            ((width, count), BF16),
            ((width, count), BF16),
            ((width, count), BF16),
            ((piece, width), BF16),
            ((piece, width), BF16),
            ((piece, width), BF16),
            ((width, count), F32),
            ((width, count), F32),
            ((piece, width), F32),
        ],
        (ref_frames, mid, keep, got),
        smem=(0,),
        flops=count * width * 12,
        moved=count * width * 30,
        name="spread",
    )
    one, two, three = swapped(one, "frame", 1), swapped(two, "frame", 2), swapped(three, "frame", 3)
    own = (own + one.astype(F32)) + (two.astype(F32) + three.astype(F32))
    own = own.astype(BF16)
    mask = 4
    other = swapped(own, "frame", mask)
    while 2 * mask < frames:
        mask *= 2
        own = (own.astype(F32) + other.astype(F32)).astype(BF16)
        other = swapped(own, "frame", mask)
    own = (own.astype(F32) + other.astype(F32)).astype(BF16)

    across = swapped(across, "frame", 1)
    first = along(first, 0, passed_on=True)
    second = along(second, 2)
    coded, gain = whole_call(
        coded_kernel,
        [((count, width), BF16), ((1, width), F32)],
        (hidden, hidden_halo, residual, gain, conv_taps),
        scratch=[pltpu.VMEM((count + 2 * COLS, width), BF16)],
        flops=2 * 3 * count * width * width,
        moved=count * width * 8,
        name="context",
    )
    back_first, back_second = whole_call(
        relay_kernel,
        [((width, count), BF16)] * 2,
        (across, first, second, first_keep, second_keep, gain),
        flops=count * width * 4,
        moved=count * width * 16,
        name="relay",
    )
    back_first = along(back_first, 0)
    back_second = along(back_second, 2)
    back_pair = swapped(pair, "frame", 1)
    grad_latents, last = whole_call(
        final_kernel,
        [((count, width), BF16), ((16, 128), F32)],
        (base, back_first, back_second, back_pair),
        flops=count * width * 4,
        moved=count * width * 12,
        name="latent_gradient",
    )
    (pieces,) = whole_call(
        gather_kernel,
        [((half, width), BF16)],
        (own, *[swapped(own, "frame", mask) for mask in (1, 2, 3)], last),
        flops=half * width,
        moved=half * width * 4,
        name="pieces",
    )
    other = swapped(pieces, "row", 1)
    shared_grad, value_grad, output_grad, taps_grad = whole_call(
        functools.partial(
            weights_kernel, norm=1.0 / math.sqrt(frames * total_rows * COLS)
        ),
        [
            ((width, width), F32),
            ((width, width), F32),
            ((width, width), F32),
            ((3, width, width), F32),
        ],
        (pieces, other),
        flops=6 * width * width,
        moved=6 * width * width * 6,
        name="weight_gradients",
    )

    return (
        coded[None],
        grad_latents[None],
        shared_grad,
        value_grad,
        output_grad,
        taps_grad,
    )


def solution(mesh):
    placed = (
        P(("groups", "frame"), "row", None),
        P(("groups", "frame"), None),
        P(("groups", "frame")),
        P(("groups", "frame")),
        P(),
        P(),
        P(),
        P(),
        P(),
        P(("groups", "frame"), "row", None),
    )
    return jax.shard_map(
        local,
        mesh=mesh,
        in_specs=placed,
        out_specs=(
            P(("groups", "frame"), "row", None),
            P(("groups", "frame"), "row", None),
            P("groups", None),
            P("groups", None),
            P("groups", None),
            P("groups", None, None),
        ),
        check_vma=False,
    )
```

```python
import functools
import math

import jax
import jax.numpy as jnp
from jax import lax
from jax.experimental import pallas as pl
from jax.experimental.pallas import tpu as pltpu
from jax.sharding import PartitionSpec as P

HEADS = 8
DH = 32
COLS = 64
WMAX = 2
BROWS = 2
GROUP = 2

SCALE = 1.5 / math.sqrt(DH)
MASKED = -1e30
LOG2E = 1.4426950408889634
F32 = jnp.float32
BF16 = jnp.bfloat16
NN = (((1,), (0,)), ((), ()))
NT = (((1,), (1,)), ((), ()))


def dot(left, right, dims=NN):
    return lax.dot_general(left, right, dims, preferred_element_type=F32)


def halves_of(value):
    high = value.astype(BF16)
    return high, (value - high.astype(F32)).astype(BF16)


def left_split_dot(left, right, dims=NN):
    high, low = halves_of(left)
    return dot(high, right, dims) + dot(low, right, dims)


def right_split_dot(left, right, dims=NN):
    high, low = halves_of(right)
    return dot(left, high, dims) + dot(left, low, dims)


def swapped(array, axis, mask):
    pairs = [(i, i ^ mask) for i in range(lax.axis_size(axis))]
    return lax.ppermute(array, axis, pairs)


def along(array, parity, relayed=False, passed_on=False):
    devices = lax.axis_size("frame")
    pairs = [(i, i + 2) for i in range(devices) if (i & 2) == parity and i + 2 < devices]
    pairs = pairs + [(j, i) for i, j in pairs]
    if relayed:
        pairs = [(i, j) for i, j in pairs if 0 <= 2 * i - j < devices]
    if passed_on:
        pairs = [(i, j) for i, j in pairs if 0 <= 2 * j - i < devices]
    return lax.ppermute(array, "frame", pairs)


def whole_call(
    body, outs, args, smem=(), scratch=(), grid=None, flops=0, moved=0, name=None, vmem=16
):
    specs = [
        pl.BlockSpec(memory_space=pltpu.SMEM if i in smem else pltpu.VMEM)
        for i in range(len(args))
    ]
    more = {} if grid is None else {"grid": grid}
    return pl.pallas_call(
        body,
        out_shape=[jax.ShapeDtypeStruct(shape, dtype) for shape, dtype in outs],
        in_specs=specs,
        out_specs=[pl.BlockSpec(memory_space=pltpu.VMEM)] * len(outs),
        scratch_shapes=list(scratch),
        compiler_params=pltpu.CompilerParams(vmem_limit_bytes=vmem * 1024 * 1024),
        cost_estimate=pl.CostEstimate(flops=flops, bytes_accessed=moved, transcendentals=0),
        name=name,
        **more,
    )(*args)


def before_kernel(
    level, scale, edge, cot, tokens, taps, shared, outp,
    resid_out, rb_out, ext_out, up_out, upt_out, query_out, queryt_out, gain_out,
):
    row_id = lax.axis_index("row")
    count = cot.shape[0]
    gain = scale[pl.ds(level[0], 1), :]
    gain_out[...] = gain
    grad_z = cot[...].astype(F32) * gain
    got = (edge[...].astype(F32) * gain).astype(BF16)
    none = jnp.zeros_like(got)
    ext_out[:COLS] = jnp.where(row_id == 0, none, got)
    ext_out[COLS : COLS + count] = grad_z.astype(BF16)
    ext_out[COLS + count :] = jnp.where(row_id == 0, got, none)
    total = grad_z
    for tap in range(3):
        begin = (2 - tap) * COLS
        total = total + dot(ext_out[begin : begin + count], taps[tap], NT)
    resid_out[...] = total
    rounded = total.astype(BF16)
    rb_out[...] = rounded
    upstream = dot(rounded, outp[...], NT).astype(BF16)
    up_out[...] = upstream
    upt_out[...] = upstream.T
    query = dot(tokens[...], shared[...]).astype(BF16)
    query_out[...] = query
    queryt_out[...] = query.T


def attention_kernel(
    windows, slots, halo, query, queryt, up, upt, tokens, rb, ext, resid_grad, shared, value, outp,
    mid_out, send_out, keep_out, hidden_out, resid_out, base_out,
    key_all, val_all, key_blk, val_blk, keyt_blk, valt_blk, bias, mixed_all, dq_all, dkt, dvt, sums,
    score_all, grad_all, *, total_rows,
):
    step = pl.program_id(0)
    window, row_id = windows[0], lax.axis_index("row")
    width = query.shape[1]
    count = query.shape[0]
    rim = WMAX * COLS
    block = BROWS * COLS
    span = block + 2 * rim

    @pl.when(step == 0)
    def _():
        for slot in range(2):
            for weight, full in ((shared, key_all), (value, val_all)):
                full[slot, rim : rim + count] = dot(slots[slot], weight[...]).astype(BF16)
                far = dot(halo[slot], weight[...]).astype(BF16)
                none = jnp.zeros_like(far)
                full[slot, :rim] = jnp.where(row_id == 0, none, far)
                full[slot, rim + count :] = jnp.where(row_id == 0, far, none)
        dkt[...] = jnp.zeros_like(dkt)
        dvt[...] = jnp.zeros_like(dvt)

    begin = pl.multiple_of(step * block, block)
    for slot in range(2):
        key_blk[slot * span : (slot + 1) * span] = key_all[slot, pl.ds(begin, span)]
        val_blk[slot * span : (slot + 1) * span] = val_all[slot, pl.ds(begin, span)]
    keyt_blk[...] = key_blk[...].T
    valt_blk[...] = val_blk[...].T
    first_row = row_id * (count // COLS) + step * BROWS
    query_row = first_row + lax.broadcasted_iota(jnp.int32, (block, span), 0) // COLS
    key_row = first_row - WMAX + lax.broadcasted_iota(jnp.int32, (block, span), 1) // COLS
    near = jnp.abs(query_row - key_row) <= window
    allowed = near & (key_row >= 0) & (key_row < total_rows)
    one_bias = jnp.where(allowed, 0.0, MASKED)
    bias[:, :span] = one_bias
    bias[:, span:] = one_bias

    lane_head = lax.broadcasted_iota(jnp.int32, (1, width), 1) // DH
    masks = [(lane_head == head).astype(F32) for head in range(HEADS)]
    tall = GROUP * block
    group_bias = jnp.concatenate([bias[...]] * GROUP, 0)
    query_b, up_b = query[pl.ds(begin, block), :], up[pl.ds(begin, block), :]
    mixed = jnp.zeros((block, width), F32)
    grad_q = jnp.zeros((block, width), F32)

    def products(group):
        own = masks[group * GROUP : (group + 1) * GROUP]
        stacked_q = jnp.concatenate([query_b * mask.astype(BF16) for mask in own], 0)
        stacked_u = jnp.concatenate([up_b * mask.astype(BF16) for mask in own], 0)
        rows = slice(group * tall, (group + 1) * tall)
        score_all[rows] = dot(stacked_q, keyt_blk[...])
        grad_all[rows] = dot(stacked_u, valt_blk[...])

    products(0)
    for group in range(HEADS // GROUP):
        if (group + 1) * GROUP < HEADS:
            products(group + 1)
        rows = slice(group * tall, (group + 1) * tall)
        scores = score_all[rows] + group_bias
        top = jnp.max(scores, axis=1, keepdims=True)
        terms = jnp.exp2((scores - top) * (SCALE * LOG2E))
        weights = terms * (1.0 / jnp.sum(terms, axis=1, keepdims=True))
        prob = weights.astype(BF16)
        grad_prob = grad_all[rows]
        inner = jnp.sum(weights * grad_prob, axis=1, keepdims=True)
        grad_score = ((weights * (grad_prob - inner)) * SCALE).astype(BF16)
        mixed_g = dot(prob, val_blk[...])
        grad_q_g = dot(grad_score, key_blk[...])
        for member in range(GROUP):
            head = group * GROUP + member
            part = slice(member * block, (member + 1) * block)
            mixed = mixed + mixed_g[part] * masks[head]
            grad_q = grad_q + grad_q_g[part] * masks[head]
            lanes = slice(head * DH, (head + 1) * DH)
            dv = dot(upt[lanes, pl.ds(begin, block)], prob[part])
            dk = dot(queryt[lanes, pl.ds(begin, block)], grad_score[part])
            for slot in range(2):
                keys = slice(slot * span, (slot + 1) * span)
                dvt[slot, lanes, pl.ds(begin, span)] += dv[:, keys]
                dkt[slot, lanes, pl.ds(begin, span)] += dk[:, keys]
    mixed_all[pl.ds(begin, block), :] = mixed.astype(BF16)
    dq_all[pl.ds(begin, block), :] = grad_q

    @pl.when(step == pl.num_programs(0) - 1)
    def _():
        def far_rim(array):
            upper, lower = array[:, :rim], array[:, rim + count :]
            return jnp.where(row_id == 0, lower, upper)

        half = 3 * width
        middle = slice(rim, rim + count)
        grad_q = dq_all[...]
        shared_t = jnp.zeros((width, width), F32)
        value_t = jnp.zeros((width, width), F32)
        for slot in range(2):
            part = jnp.zeros((width, count + 2 * rim), F32)
            for piece in halves_of(dkt[slot]):
                part = part + dot(shared[...], piece)
                rims = far_rim(piece)
                shared_t += dot(piece[:, middle], slots[slot]) + dot(rims, halo[slot])
            for piece in halves_of(dvt[slot]):
                part = part + dot(value[...], piece)
                rims = far_rim(piece)
                value_t += dot(piece[:, middle], slots[slot]) + dot(rims, halo[slot])
            mid_out[slot] = part[:, middle]
            send_out[half:, slot * rim : (slot + 1) * rim] = far_rim(part).astype(BF16)
        base_out[...] = resid_grad[...] + left_split_dot(grad_q, shared[...], NT)
        sums[:width] = right_split_dot(tokens[...].T, grad_q) + shared_t.T
        sums[width : 2 * width] = value_t.T
        mixed_full = mixed_all[...]
        residual = tokens[...].astype(F32) + dot(mixed_full, outp[...])
        resid_out[...] = residual
        hidden = residual.astype(BF16)
        hidden_out[...] = hidden
        sums[2 * width : half] = dot(mixed_full.T, rb[...])
        hidden_t = hidden.T
        for tap in range(3):
            start = (2 - tap) * COLS
            sums[half + tap * width : half + (tap + 1) * width] = dot(
                hidden_t, ext[start : start + count]
            )
        keep_out[...] = sums[pl.ds(pl.multiple_of(row_id * half, half), half)]
        send_out[:half] = sums[pl.ds(pl.multiple_of((1 - row_id) * half, half), half)].astype(BF16)


def spread_kernel(
    refs, mid, keep, got,
    pair_out, across_out, first_out, second_out, one_out, two_out, three_out,
    first_keep, second_keep, own_out,
):
    frame_id, row_id = lax.axis_index("frame"), lax.axis_index("row")
    steps = [refs[0, 0] - frame_id, refs[0, 1] - frame_id]
    width, count = mid.shape[1], mid.shape[2]
    rim = WMAX * COLS
    half = keep.shape[0]
    piece = half // 4

    def folded(slot):
        rims = got[half:, slot * rim : (slot + 1) * rim].astype(F32)
        none = jnp.zeros_like(rims)
        part = mid[slot]
        first = part[:, :rim] + jnp.where(row_id == 0, none, rims)
        last = part[:, count - rim :] + jnp.where(row_id == 0, rims, none)
        return jnp.concatenate([first, part[:, rim : count - rim], last], 1)

    pair_step = jnp.where((frame_id & 1) == 0, 1, -1)
    link_step = jnp.where((frame_id & 2) == 0, 1, -1)
    for step, out in (
        (pair_step, pair_out),
        (-pair_step, across_out),
        (4 * link_step, first_out),
        (-4 * link_step, second_out),
        (2 * link_step, first_keep),
        (-2 * link_step, second_keep),
    ):
        by_zero, by_one = steps[0] == step, steps[1] == step

        @pl.when(by_zero & by_one)
        def _(out=out):
            out[:width] = (folded(0) + folded(1)).astype(out.dtype)

        @pl.when(by_zero & ~by_one)
        def _(out=out):
            out[:width] = folded(0).astype(out.dtype)

        @pl.when(by_one & ~by_zero)
        def _(out=out):
            out[:width] = folded(1).astype(out.dtype)

        @pl.when(~by_zero & ~by_one)
        def _(out=out):
            out[:width] = jnp.zeros((width, count), out.dtype)

    me = frame_id & 3

    def rows_of(index):
        rows = pl.ds(pl.multiple_of(index * piece, piece), piece)
        return keep[rows] + got[rows].astype(F32)

    own_out[...] = rows_of(me)
    for mask, out in ((1, one_out), (2, two_out), (3, three_out)):
        out[...] = rows_of(me ^ mask).astype(BF16)


def coded_kernel(hidden, halo, residual, gain, taps, coded_out, gain_out, ext):
    gain_out[...] = gain[...]
    row_id = lax.axis_index("row")
    count = hidden.shape[0]
    got = halo[...]
    none = jnp.zeros_like(got)
    ext[:COLS] = jnp.where(row_id == 0, none, got)
    ext[COLS : COLS + count] = hidden[...]
    ext[COLS + count :] = jnp.where(row_id == 0, got, none)
    total = jnp.zeros((count, hidden.shape[1]), F32)
    for tap in range(3):
        begin = tap * COLS
        total = total + dot(ext[begin : begin + count], taps[tap])
    coded_out[...] = ((residual[...] + total) * gain[...]).astype(BF16)


def select_kernel(refs, pair, cross, first, second, far_first, far_second, _, slots_out, edge_out):
    frame_id, row_id = lax.axis_index("frame"), lax.axis_index("row")
    count = pair.shape[0]
    rim = WMAX * COLS
    pair_step = jnp.where((frame_id & 1) == 0, 1, -1)
    link_step = jnp.where((frame_id & 2) == 0, 2, -2)
    for slot in range(2):
        step = refs[0, slot] - frame_id
        for distance, source in (
            (pair_step, pair),
            (-pair_step, cross),
            (link_step, first),
            (-link_step, second),
            (2 * link_step, far_first),
            (-2 * link_step, far_second),
        ):

            @pl.when(step == distance)
            def _(source=source):
                slots_out[slot] = source[:count]
                begin = pl.multiple_of((1 - row_id) * (count - rim), rim)
                edge_out[slot] = source[pl.ds(begin, rim)]


def relay_kernel(
    across, first, second, first_keep, second_keep, _,
    first_out, second_out,
):
    frame_id = lax.axis_index("frame")
    crossing = across[...].astype(F32)
    none = jnp.zeros_like(crossing)
    with_first = (frame_id & 1) == ((frame_id >> 1) & 1)
    first_out[...] = (
        first_keep[...] + second[...].astype(F32) + jnp.where(with_first, crossing, none)
    ).astype(BF16)
    second_out[...] = (
        second_keep[...] + first[...].astype(F32) + jnp.where(with_first, none, crossing)
    ).astype(BF16)


def final_kernel(base, first, second, pair, grad_out, last_out):
    returned = first[...].astype(F32) + second[...].astype(F32) + pair[...].astype(F32)
    grad_out[...] = (base[...] + returned.T).astype(BF16)
    last_out[...] = returned[:16, :128]


def gather_kernel(own, first, second, third, _, pieces_out):
    me = lax.axis_index("frame") & 3
    piece = own.shape[0]
    for mask, part in enumerate((own, first, second, third)):
        begin = pl.multiple_of((me ^ mask) * piece, piece)
        pieces_out[pl.ds(begin, piece)] = part[...]


def weights_kernel(own, other, shared_out, value_out, output_out, taps_out, *, norm):
    row_id = lax.axis_index("row")
    width = shared_out.shape[1]
    low = jnp.where(row_id == 0, own[...].astype(F32), other[...].astype(F32)) * norm
    high = jnp.where(row_id == 0, other[...].astype(F32), own[...].astype(F32)) * norm
    shared_out[...] = low[:width]
    value_out[...] = low[width : 2 * width]
    output_out[...] = low[2 * width :]
    for tap in range(3):
        taps_out[tap] = high[tap * width : (tap + 1) * width]


def local(
    latents, ref_frames, windows, quant_level, quant_scale,
    shared_proj, value_proj, output_proj, conv_taps, cotangent,
):
    width = latents.shape[2]
    count = latents.shape[1]
    rows_dev = count // COLS
    frames = lax.axis_size("frame")
    total_rows = rows_dev * lax.axis_size("row")
    row_id = lax.axis_index("row")
    rim = WMAX * COLS
    tokens = latents[0]
    cot = cotangent[0]

    cot_edge = swapped(jnp.where(row_id == 0, cot[count - COLS :], cot[:COLS]), "row", 1)
    from_first = along(tokens, 0)
    from_second = along(tokens, 2)
    from_pair = swapped(tokens, "frame", 1)

    grad_resid, grad_rb, grad_ext, up, upt, query, queryt, gain = whole_call(
        before_kernel,
        [
            ((count, width), F32),
            ((count, width), BF16),
            ((count + 2 * COLS, width), BF16),
            ((count, width), BF16),
            ((width, count), BF16),
            ((count, width), BF16),
            ((width, count), BF16),
            ((1, width), F32),
        ],
        (
            quant_level, quant_scale, cot_edge, cot, tokens, conv_taps, shared_proj, output_proj,
        ),
        smem=(0,),
        flops=2 * 5 * count * width * width,
        moved=4 * count * width * 6,
        name="gradient_path",
    )

    frame_id = lax.axis_index("frame")
    by_second = (frame_id & 1) != ((frame_id >> 1) & 1)
    longer = jnp.concatenate([from_second, from_second[:COLS]], 0)
    far_first = along(longer, 0, relayed=True)
    far_second = along(from_first, 2, relayed=True)
    from_cross = swapped(jnp.where(by_second, from_second, from_first), "frame", 1)
    slots, edge = whole_call(
        select_kernel,
        [((2, count, width), BF16), ((2, rim, width), BF16)],
        (ref_frames, from_pair, from_cross, from_first, from_second, far_first, far_second, gain),
        smem=(0,),
        flops=count * width,
        moved=count * width * 8,
        name="slots",
    )
    halo = swapped(edge, "row", 1)

    block = BROWS * COLS
    span = block + 2 * rim
    ext_count = count + 2 * rim
    half = 3 * width
    mid, send, keep, hidden, residual, base = whole_call(
        functools.partial(attention_kernel, total_rows=total_rows),
        [
            ((2, width, count), F32),
            ((half + width, width), BF16),
            ((half, width), F32),
            ((count, width), BF16),
            ((count, width), F32),
            ((count, width), F32),
        ],
        (
            windows, slots, halo, query, queryt, up, upt, tokens, grad_rb, grad_ext, grad_resid,
            shared_proj, value_proj, output_proj,
        ),
        smem=(0,),
        scratch=[
            pltpu.VMEM((2, ext_count, width), BF16),
            pltpu.VMEM((2, ext_count, width), BF16),
            pltpu.VMEM((2 * span, width), BF16),
            pltpu.VMEM((2 * span, width), BF16),
            pltpu.VMEM((width, 2 * span), BF16),
            pltpu.VMEM((width, 2 * span), BF16),
            pltpu.VMEM((block, 2 * span), F32),
            pltpu.VMEM((count, width), BF16),
            pltpu.VMEM((count, width), F32),
            pltpu.VMEM((2, width, ext_count), F32),
            pltpu.VMEM((2, width, ext_count), F32),
            pltpu.VMEM((2 * half, width), F32),
            pltpu.VMEM((HEADS * block, 2 * span), F32),
            pltpu.VMEM((HEADS * block, 2 * span), F32),
        ],
        grid=(count // block,),
        flops=6 * 2 * count * 2 * span * width * HEADS,
        moved=count * width * 60,
        name="attention",
        vmem=28,
    )

    got = swapped(send, "row", 1)
    hidden_edge = jnp.where(row_id == 0, hidden[count - COLS :], hidden[:COLS])
    hidden_halo = swapped(hidden_edge, "row", 1)
    piece = half // 4
    pair, across, first, second, one, two, three, first_keep, second_keep, own = whole_call(
        spread_kernel,
        [
            ((width, count), BF16),
            ((width, count), BF16),
            ((width, count), BF16),
            ((width, count), BF16),
            ((piece, width), BF16),
            ((piece, width), BF16),
            ((piece, width), BF16),
            ((width, count), F32),
            ((width, count), F32),
            ((piece, width), F32),
        ],
        (ref_frames, mid, keep, got),
        smem=(0,),
        flops=count * width * 12,
        moved=count * width * 30,
        name="spread",
    )
    one, two, three = swapped(one, "frame", 1), swapped(two, "frame", 2), swapped(three, "frame", 3)
    own = (own + one.astype(F32)) + (two.astype(F32) + three.astype(F32))
    own = own.astype(BF16)
    mask = 4
    other = swapped(own, "frame", mask)
    while 2 * mask < frames:
        mask *= 2
        own = (own.astype(F32) + other.astype(F32)).astype(BF16)
        other = swapped(own, "frame", mask)
    own = (own.astype(F32) + other.astype(F32)).astype(BF16)

    across = swapped(across, "frame", 1)
    first = along(first, 0)
    second = along(second, 2)
    coded, gain = whole_call(
        coded_kernel,
        [((count, width), BF16), ((1, width), F32)],
        (hidden, hidden_halo, residual, gain, conv_taps),
        scratch=[pltpu.VMEM((count + 2 * COLS, width), BF16)],
        flops=2 * 3 * count * width * width,
        moved=count * width * 8,
        name="context",
    )
    back_first, back_second = whole_call(
        relay_kernel,
        [((width, count), BF16)] * 2,
        (across, first, second, first_keep, second_keep, gain),
        flops=count * width * 4,
        moved=count * width * 16,
        name="relay",
    )
    back_first = along(back_first, 0)
    back_second = along(back_second, 2)
    back_pair = swapped(pair, "frame", 1)
    grad_latents, last = whole_call(
        final_kernel,
        [((count, width), BF16), ((16, 128), F32)],
        (base, back_first, back_second, back_pair),
        flops=count * width * 4,
        moved=count * width * 12,
        name="latent_gradient",
    )
    (pieces,) = whole_call(
        gather_kernel,
        [((half, width), BF16)],
        (own, *[swapped(own, "frame", mask) for mask in (1, 2, 3)], last),
        flops=half * width,
        moved=half * width * 4,
        name="pieces",
    )
    other = swapped(pieces, "row", 1)
    shared_grad, value_grad, output_grad, taps_grad = whole_call(
        functools.partial(
            weights_kernel, norm=1.0 / math.sqrt(frames * total_rows * COLS)
        ),
        [
            ((width, width), F32),
            ((width, width), F32),
            ((width, width), F32),
            ((3, width, width), F32),
        ],
        (pieces, other),
        flops=6 * width * width,
        moved=6 * width * width * 6,
        name="weight_gradients",
    )

    return (
        coded[None],
        grad_latents[None],
        shared_grad,
        value_grad,
        output_grad,
        taps_grad,
    )


def solution(mesh):
    placed = (
        P(("groups", "frame"), "row", None),
        P(("groups", "frame"), None),
        P(("groups", "frame")),
        P(("groups", "frame")),
        P(),
        P(),
        P(),
        P(),
        P(),
        P(("groups", "frame"), "row", None),
    )
    return jax.shard_map(
        local,
        mesh=mesh,
        in_specs=placed,
        out_specs=(
            P(("groups", "frame"), "row", None),
            P(("groups", "frame"), "row", None),
            P("groups", None),
            P("groups", None),
            P("groups", None),
            P("groups", None, None),
        ),
        check_vma=False,
    )
```

```python
import functools
import math

import jax
import jax.numpy as jnp
from jax import lax
from jax.experimental import pallas as pl
from jax.experimental.pallas import tpu as pltpu
from jax.sharding import PartitionSpec as P

HEADS = 8
DH = 32
COLS = 64
WMAX = 2
BROWS = 2
GROUP = 2

SCALE = 1.5 / math.sqrt(DH)
MASKED = -1e30
LOG2E = 1.4426950408889634
F32 = jnp.float32
BF16 = jnp.bfloat16
NN = (((1,), (0,)), ((), ()))
NT = (((1,), (1,)), ((), ()))


def dot(left, right, dims=NN):
    return lax.dot_general(left, right, dims, preferred_element_type=F32)


def halves_of(value):
    high = value.astype(BF16)
    return high, (value - high.astype(F32)).astype(BF16)


def left_split_dot(left, right, dims=NN):
    high, low = halves_of(left)
    return dot(high, right, dims) + dot(low, right, dims)


def right_split_dot(left, right, dims=NN):
    high, low = halves_of(right)
    return dot(left, high, dims) + dot(left, low, dims)


def swapped(array, axis, mask):
    pairs = [(i, i ^ mask) for i in range(lax.axis_size(axis))]
    return lax.ppermute(array, axis, pairs)


def along(array, parity, relayed=False, passed_on=False):
    devices = lax.axis_size("frame")
    pairs = [(i, i + 2) for i in range(devices) if (i & 2) == parity and i + 2 < devices]
    pairs = pairs + [(j, i) for i, j in pairs]
    if relayed:
        pairs = [(i, j) for i, j in pairs if 0 <= 2 * i - j < devices]
    if passed_on:
        pairs = [(i, j) for i, j in pairs if 0 <= 2 * j - i < devices]
    return lax.ppermute(array, "frame", pairs)


def whole_call(
    body, outs, args, smem=(), scratch=(), grid=None, flops=0, moved=0, name=None, vmem=16
):
    specs = [
        pl.BlockSpec(memory_space=pltpu.SMEM if i in smem else pltpu.VMEM)
        for i in range(len(args))
    ]
    more = {} if grid is None else {"grid": grid}
    return pl.pallas_call(
        body,
        out_shape=[jax.ShapeDtypeStruct(shape, dtype) for shape, dtype in outs],
        in_specs=specs,
        out_specs=[pl.BlockSpec(memory_space=pltpu.VMEM)] * len(outs),
        scratch_shapes=list(scratch),
        compiler_params=pltpu.CompilerParams(vmem_limit_bytes=vmem * 1024 * 1024),
        cost_estimate=pl.CostEstimate(flops=flops, bytes_accessed=moved, transcendentals=0),
        name=name,
        **more,
    )(*args)


def before_kernel(
    level, scale, edge, cot, tokens, taps, shared, outp,
    resid_out, rb_out, ext_out, up_out, upt_out, query_out, queryt_out, gain_out,
):
    row_id = lax.axis_index("row")
    count = cot.shape[0]
    gain = scale[pl.ds(level[0], 1), :]
    gain_out[...] = gain
    grad_z = cot[...].astype(F32) * gain
    got = (edge[...].astype(F32) * gain).astype(BF16)
    none = jnp.zeros_like(got)
    ext_out[:COLS] = jnp.where(row_id == 0, none, got)
    ext_out[COLS : COLS + count] = grad_z.astype(BF16)
    ext_out[COLS + count :] = jnp.where(row_id == 0, got, none)
    total = grad_z
    for tap in range(3):
        begin = (2 - tap) * COLS
        total = total + dot(ext_out[begin : begin + count], taps[tap], NT)
    resid_out[...] = total
    rounded = total.astype(BF16)
    rb_out[...] = rounded
    upstream = dot(rounded, outp[...], NT).astype(BF16)
    up_out[...] = upstream
    upt_out[...] = upstream.T
    query = dot(tokens[...], shared[...]).astype(BF16)
    query_out[...] = query
    queryt_out[...] = query.T


def attention_kernel(
    windows, slots, halo, query, queryt, up, upt, tokens, rb, ext, resid_grad, shared, value, outp,
    mid_out, send_out, keep_out, hidden_out, resid_out, base_out,
    key_all, val_all, key_blk, val_blk, keyt_blk, valt_blk, bias, mixed_all, dq_all, dkt, dvt, sums,
    score_all, grad_all, *, total_rows,
):
    step = pl.program_id(0)
    window, row_id = windows[0], lax.axis_index("row")
    width = query.shape[1]
    count = query.shape[0]
    rim = WMAX * COLS
    block = BROWS * COLS
    span = block + 2 * rim

    @pl.when(step == 0)
    def _():
        for slot in range(2):
            for weight, full in ((shared, key_all), (value, val_all)):
                full[slot, rim : rim + count] = dot(slots[slot], weight[...]).astype(BF16)
                far = dot(halo[slot], weight[...]).astype(BF16)
                none = jnp.zeros_like(far)
                full[slot, :rim] = jnp.where(row_id == 0, none, far)
                full[slot, rim + count :] = jnp.where(row_id == 0, far, none)
        dkt[...] = jnp.zeros_like(dkt)
        dvt[...] = jnp.zeros_like(dvt)

    begin = pl.multiple_of(step * block, block)
    for slot in range(2):
        key_blk[slot * span : (slot + 1) * span] = key_all[slot, pl.ds(begin, span)]
        val_blk[slot * span : (slot + 1) * span] = val_all[slot, pl.ds(begin, span)]
    keyt_blk[...] = key_blk[...].T
    valt_blk[...] = val_blk[...].T
    first_row = row_id * (count // COLS) + step * BROWS
    query_row = first_row + lax.broadcasted_iota(jnp.int32, (block, span), 0) // COLS
    key_row = first_row - WMAX + lax.broadcasted_iota(jnp.int32, (block, span), 1) // COLS
    near = jnp.abs(query_row - key_row) <= window
    allowed = near & (key_row >= 0) & (key_row < total_rows)
    one_bias = jnp.where(allowed, 0.0, MASKED)
    bias[:, :span] = one_bias
    bias[:, span:] = one_bias

    lane_head = lax.broadcasted_iota(jnp.int32, (1, width), 1) // DH
    masks = [(lane_head == head).astype(F32) for head in range(HEADS)]
    tall = GROUP * block
    group_bias = jnp.concatenate([bias[...]] * GROUP, 0)
    query_b, up_b = query[pl.ds(begin, block), :], up[pl.ds(begin, block), :]
    mixed = jnp.zeros((block, width), F32)
    grad_q = jnp.zeros((block, width), F32)

    def products(group):
        own = masks[group * GROUP : (group + 1) * GROUP]
        stacked_q = jnp.concatenate([query_b * mask.astype(BF16) for mask in own], 0)
        stacked_u = jnp.concatenate([up_b * mask.astype(BF16) for mask in own], 0)
        rows = slice(group * tall, (group + 1) * tall)
        score_all[rows] = dot(stacked_q, keyt_blk[...])
        grad_all[rows] = dot(stacked_u, valt_blk[...])

    products(0)
    for group in range(HEADS // GROUP):
        if (group + 1) * GROUP < HEADS:
            products(group + 1)
        rows = slice(group * tall, (group + 1) * tall)
        scores = score_all[rows] + group_bias
        top = jnp.max(scores, axis=1, keepdims=True)
        terms = jnp.exp2((scores - top) * (SCALE * LOG2E))
        weights = terms * (1.0 / jnp.sum(terms, axis=1, keepdims=True))
        prob = weights.astype(BF16)
        grad_prob = grad_all[rows]
        inner = jnp.sum(weights * grad_prob, axis=1, keepdims=True)
        grad_score = ((weights * (grad_prob - inner)) * SCALE).astype(BF16)
        mixed_g = dot(prob, val_blk[...])
        grad_q_g = dot(grad_score, key_blk[...])
        for member in range(GROUP):
            head = group * GROUP + member
            part = slice(member * block, (member + 1) * block)
            mixed = mixed + mixed_g[part] * masks[head]
            grad_q = grad_q + grad_q_g[part] * masks[head]
            lanes = slice(head * DH, (head + 1) * DH)
            dv = dot(upt[lanes, pl.ds(begin, block)], prob[part])
            dk = dot(queryt[lanes, pl.ds(begin, block)], grad_score[part])
            for slot in range(2):
                keys = slice(slot * span, (slot + 1) * span)
                dvt[slot, lanes, pl.ds(begin, span)] += dv[:, keys]
                dkt[slot, lanes, pl.ds(begin, span)] += dk[:, keys]
    mixed_all[pl.ds(begin, block), :] = mixed.astype(BF16)
    dq_all[pl.ds(begin, block), :] = grad_q

    @pl.when(step == pl.num_programs(0) - 1)
    def _():
        def far_rim(array):
            upper, lower = array[:, :rim], array[:, rim + count :]
            return jnp.where(row_id == 0, lower, upper)

        half = 3 * width
        middle = slice(rim, rim + count)
        grad_q = dq_all[...]
        shared_t = jnp.zeros((width, width), F32)
        value_t = jnp.zeros((width, width), F32)
        for slot in range(2):
            part = jnp.zeros((width, count + 2 * rim), F32)
            part = part + dot(shared[...], dkt[slot].astype(BF16))
            for piece in halves_of(dkt[slot]):
                rims = far_rim(piece)
                shared_t += dot(piece[:, middle], slots[slot]) + dot(rims, halo[slot])
            part = part + dot(value[...], dvt[slot].astype(BF16))
            for piece in halves_of(dvt[slot]):
                rims = far_rim(piece)
                value_t += dot(piece[:, middle], slots[slot]) + dot(rims, halo[slot])
            mid_out[slot] = part[:, middle]
            send_out[half:, slot * rim : (slot + 1) * rim] = far_rim(part).astype(BF16)
        base_out[...] = resid_grad[...] + left_split_dot(grad_q, shared[...], NT)
        sums[:width] = right_split_dot(tokens[...].T, grad_q) + shared_t.T
        sums[width : 2 * width] = value_t.T
        mixed_full = mixed_all[...]
        residual = tokens[...].astype(F32) + dot(mixed_full, outp[...])
        resid_out[...] = residual
        hidden = residual.astype(BF16)
        hidden_out[...] = hidden
        sums[2 * width : half] = dot(mixed_full.T, rb[...])
        hidden_t = hidden.T
        for tap in range(3):
            start = (2 - tap) * COLS
            sums[half + tap * width : half + (tap + 1) * width] = dot(
                hidden_t, ext[start : start + count]
            )
        keep_out[...] = sums[pl.ds(pl.multiple_of(row_id * half, half), half)]
        send_out[:half] = sums[pl.ds(pl.multiple_of((1 - row_id) * half, half), half)].astype(BF16)


def spread_kernel(
    refs, mid, keep, got,
    pair_out, across_out, first_out, second_out, one_out, two_out, three_out,
    first_keep, second_keep, own_out,
):
    frame_id, row_id = lax.axis_index("frame"), lax.axis_index("row")
    steps = [refs[0, 0] - frame_id, refs[0, 1] - frame_id]
    width, count = mid.shape[1], mid.shape[2]
    rim = WMAX * COLS
    half = keep.shape[0]
    piece = half // 4

    def folded(slot):
        rims = got[half:, slot * rim : (slot + 1) * rim].astype(F32)
        none = jnp.zeros_like(rims)
        part = mid[slot]
        first = part[:, :rim] + jnp.where(row_id == 0, none, rims)
        last = part[:, count - rim :] + jnp.where(row_id == 0, rims, none)
        return jnp.concatenate([first, part[:, rim : count - rim], last], 1)

    pair_step = jnp.where((frame_id & 1) == 0, 1, -1)
    link_step = jnp.where((frame_id & 2) == 0, 1, -1)
    for step, out in (
        (pair_step, pair_out),
        (-pair_step, across_out),
        (4 * link_step, first_out),
        (-4 * link_step, second_out),
        (2 * link_step, first_keep),
        (-2 * link_step, second_keep),
    ):
        by_zero, by_one = steps[0] == step, steps[1] == step

        @pl.when(by_zero & by_one)
        def _(out=out):
            out[:width] = (folded(0) + folded(1)).astype(out.dtype)

        @pl.when(by_zero & ~by_one)
        def _(out=out):
            out[:width] = folded(0).astype(out.dtype)

        @pl.when(by_one & ~by_zero)
        def _(out=out):
            out[:width] = folded(1).astype(out.dtype)

        @pl.when(~by_zero & ~by_one)
        def _(out=out):
            out[:width] = jnp.zeros((width, count), out.dtype)

    me = frame_id & 3

    def rows_of(index):
        rows = pl.ds(pl.multiple_of(index * piece, piece), piece)
        return keep[rows] + got[rows].astype(F32)

    own_out[...] = rows_of(me)
    for mask, out in ((1, one_out), (2, two_out), (3, three_out)):
        out[...] = rows_of(me ^ mask).astype(BF16)


def coded_kernel(hidden, halo, residual, gain, taps, coded_out, gain_out, ext):
    gain_out[...] = gain[...]
    row_id = lax.axis_index("row")
    count = hidden.shape[0]
    got = halo[...]
    none = jnp.zeros_like(got)
    ext[:COLS] = jnp.where(row_id == 0, none, got)
    ext[COLS : COLS + count] = hidden[...]
    ext[COLS + count :] = jnp.where(row_id == 0, got, none)
    total = jnp.zeros((count, hidden.shape[1]), F32)
    for tap in range(3):
        begin = tap * COLS
        total = total + dot(ext[begin : begin + count], taps[tap])
    coded_out[...] = ((residual[...] + total) * gain[...]).astype(BF16)


def select_kernel(refs, pair, cross, first, second, far_first, far_second, _, slots_out, edge_out):
    frame_id, row_id = lax.axis_index("frame"), lax.axis_index("row")
    count = pair.shape[0]
    rim = WMAX * COLS
    pair_step = jnp.where((frame_id & 1) == 0, 1, -1)
    link_step = jnp.where((frame_id & 2) == 0, 2, -2)
    for slot in range(2):
        step = refs[0, slot] - frame_id
        for distance, source in (
            (pair_step, pair),
            (-pair_step, cross),
            (link_step, first),
            (-link_step, second),
            (2 * link_step, far_first),
            (-2 * link_step, far_second),
        ):

            @pl.when(step == distance)
            def _(source=source):
                slots_out[slot] = source[:count]
                begin = pl.multiple_of((1 - row_id) * (count - rim), rim)
                edge_out[slot] = source[pl.ds(begin, rim)]


def relay_kernel(
    across, first, second, first_keep, second_keep, _,
    first_out, second_out,
):
    frame_id = lax.axis_index("frame")
    crossing = across[...].astype(F32)
    none = jnp.zeros_like(crossing)
    with_first = (frame_id & 1) == ((frame_id >> 1) & 1)
    first_out[...] = (
        first_keep[...] + second[...].astype(F32) + jnp.where(with_first, crossing, none)
    ).astype(BF16)
    second_out[...] = (
        second_keep[...] + first[...].astype(F32) + jnp.where(with_first, none, crossing)
    ).astype(BF16)


def final_kernel(base, first, second, pair, grad_out, last_out):
    returned = first[...].astype(F32) + second[...].astype(F32) + pair[...].astype(F32)
    grad_out[...] = (base[...] + returned.T).astype(BF16)
    last_out[...] = returned[:16, :128]


def gather_kernel(own, first, second, third, _, pieces_out):
    me = lax.axis_index("frame") & 3
    piece = own.shape[0]
    for mask, part in enumerate((own, first, second, third)):
        begin = pl.multiple_of((me ^ mask) * piece, piece)
        pieces_out[pl.ds(begin, piece)] = part[...]


def weights_kernel(own, other, shared_out, value_out, output_out, taps_out, *, norm):
    row_id = lax.axis_index("row")
    width = shared_out.shape[1]
    low = jnp.where(row_id == 0, own[...].astype(F32), other[...].astype(F32)) * norm
    high = jnp.where(row_id == 0, other[...].astype(F32), own[...].astype(F32)) * norm
    shared_out[...] = low[:width]
    value_out[...] = low[width : 2 * width]
    output_out[...] = low[2 * width :]
    for tap in range(3):
        taps_out[tap] = high[tap * width : (tap + 1) * width]


def local(
    latents, ref_frames, windows, quant_level, quant_scale,
    shared_proj, value_proj, output_proj, conv_taps, cotangent,
):
    width = latents.shape[2]
    count = latents.shape[1]
    rows_dev = count // COLS
    frames = lax.axis_size("frame")
    total_rows = rows_dev * lax.axis_size("row")
    row_id = lax.axis_index("row")
    rim = WMAX * COLS
    tokens = latents[0]
    cot = cotangent[0]

    cot_edge = swapped(jnp.where(row_id == 0, cot[count - COLS :], cot[:COLS]), "row", 1)
    from_first = along(tokens, 0)
    from_second = along(tokens, 2)
    from_pair = swapped(tokens, "frame", 1)

    grad_resid, grad_rb, grad_ext, up, upt, query, queryt, gain = whole_call(
        before_kernel,
        [
            ((count, width), F32),
            ((count, width), BF16),
            ((count + 2 * COLS, width), BF16),
            ((count, width), BF16),
            ((width, count), BF16),
            ((count, width), BF16),
            ((width, count), BF16),
            ((1, width), F32),
        ],
        (
            quant_level, quant_scale, cot_edge, cot, tokens, conv_taps, shared_proj, output_proj,
        ),
        smem=(0,),
        flops=2 * 5 * count * width * width,
        moved=4 * count * width * 6,
        name="gradient_path",
    )

    frame_id = lax.axis_index("frame")
    by_second = (frame_id & 1) != ((frame_id >> 1) & 1)
    longer = jnp.concatenate([from_second, from_second[:COLS]], 0)
    far_first = along(longer, 0, relayed=True)
    far_second = along(from_first, 2, relayed=True)
    from_cross = swapped(jnp.where(by_second, from_second, from_first), "frame", 1)
    slots, edge = whole_call(
        select_kernel,
        [((2, count, width), BF16), ((2, rim, width), BF16)],
        (ref_frames, from_pair, from_cross, from_first, from_second, far_first, far_second, gain),
        smem=(0,),
        flops=count * width,
        moved=count * width * 8,
        name="slots",
    )
    halo = swapped(edge, "row", 1)

    block = BROWS * COLS
    span = block + 2 * rim
    ext_count = count + 2 * rim
    half = 3 * width
    mid, send, keep, hidden, residual, base = whole_call(
        functools.partial(attention_kernel, total_rows=total_rows),
        [
            ((2, width, count), F32),
            ((half + width, width), BF16),
            ((half, width), F32),
            ((count, width), BF16),
            ((count, width), F32),
            ((count, width), F32),
        ],
        (
            windows, slots, halo, query, queryt, up, upt, tokens, grad_rb, grad_ext, grad_resid,
            shared_proj, value_proj, output_proj,
        ),
        smem=(0,),
        scratch=[
            pltpu.VMEM((2, ext_count, width), BF16),
            pltpu.VMEM((2, ext_count, width), BF16),
            pltpu.VMEM((2 * span, width), BF16),
            pltpu.VMEM((2 * span, width), BF16),
            pltpu.VMEM((width, 2 * span), BF16),
            pltpu.VMEM((width, 2 * span), BF16),
            pltpu.VMEM((block, 2 * span), F32),
            pltpu.VMEM((count, width), BF16),
            pltpu.VMEM((count, width), F32),
            pltpu.VMEM((2, width, ext_count), F32),
            pltpu.VMEM((2, width, ext_count), F32),
            pltpu.VMEM((2 * half, width), F32),
            pltpu.VMEM((HEADS * block, 2 * span), F32),
            pltpu.VMEM((HEADS * block, 2 * span), F32),
        ],
        grid=(count // block,),
        flops=6 * 2 * count * 2 * span * width * HEADS,
        moved=count * width * 60,
        name="attention",
        vmem=28,
    )

    got = swapped(send, "row", 1)
    hidden_edge = jnp.where(row_id == 0, hidden[count - COLS :], hidden[:COLS])
    hidden_halo = swapped(hidden_edge, "row", 1)
    piece = half // 4
    pair, across, first, second, one, two, three, first_keep, second_keep, own = whole_call(
        spread_kernel,
        [
            ((width, count), BF16),
            ((width, count), BF16),
            ((width, count), BF16),
            ((width, count), BF16),
            ((piece, width), BF16),
            ((piece, width), BF16),
            ((piece, width), BF16),
            ((width, count), F32),
            ((width, count), F32),
            ((piece, width), F32),
        ],
        (ref_frames, mid, keep, got),
        smem=(0,),
        flops=count * width * 12,
        moved=count * width * 30,
        name="spread",
    )
    one, two, three = swapped(one, "frame", 1), swapped(two, "frame", 2), swapped(three, "frame", 3)
    own = (own + one.astype(F32)) + (two.astype(F32) + three.astype(F32))
    own = own.astype(BF16)
    mask = 4
    other = swapped(own, "frame", mask)
    while 2 * mask < frames:
        mask *= 2
        own = (own.astype(F32) + other.astype(F32)).astype(BF16)
        other = swapped(own, "frame", mask)
    own = (own.astype(F32) + other.astype(F32)).astype(BF16)

    across = swapped(across, "frame", 1)
    first = along(first, 0, passed_on=True)
    second = along(second, 2)
    coded, gain = whole_call(
        coded_kernel,
        [((count, width), BF16), ((1, width), F32)],
        (hidden, hidden_halo, residual, gain, conv_taps),
        scratch=[pltpu.VMEM((count + 2 * COLS, width), BF16)],
        flops=2 * 3 * count * width * width,
        moved=count * width * 8,
        name="context",
    )
    back_first, back_second = whole_call(
        relay_kernel,
        [((width, count), BF16)] * 2,
        (across, first, second, first_keep, second_keep, gain),
        flops=count * width * 4,
        moved=count * width * 16,
        name="relay",
    )
    back_first = along(back_first, 0)
    back_second = along(back_second, 2)
    back_pair = swapped(pair, "frame", 1)
    grad_latents, last = whole_call(
        final_kernel,
        [((count, width), BF16), ((16, 128), F32)],
        (base, back_first, back_second, back_pair),
        flops=count * width * 4,
        moved=count * width * 12,
        name="latent_gradient",
    )
    (pieces,) = whole_call(
        gather_kernel,
        [((half, width), BF16)],
        (own, *[swapped(own, "frame", mask) for mask in (1, 2, 3)], last),
        flops=half * width,
        moved=half * width * 4,
        name="pieces",
    )
    other = swapped(pieces, "row", 1)
    shared_grad, value_grad, output_grad, taps_grad = whole_call(
        functools.partial(
            weights_kernel, norm=1.0 / math.sqrt(frames * total_rows * COLS)
        ),
        [
            ((width, width), F32),
            ((width, width), F32),
            ((width, width), F32),
            ((3, width, width), F32),
        ],
        (pieces, other),
        flops=6 * width * width,
        moved=6 * width * width * 6,
        name="weight_gradients",
    )

    return (
        coded[None],
        grad_latents[None],
        shared_grad,
        value_grad,
        output_grad,
        taps_grad,
    )


def solution(mesh):
    placed = (
        P(("groups", "frame"), "row", None),
        P(("groups", "frame"), None),
        P(("groups", "frame")),
        P(("groups", "frame")),
        P(),
        P(),
        P(),
        P(),
        P(),
        P(("groups", "frame"), "row", None),
    )
    return jax.shard_map(
        local,
        mesh=mesh,
        in_specs=placed,
        out_specs=(
            P(("groups", "frame"), "row", None),
            P(("groups", "frame"), "row", None),
            P("groups", None),
            P("groups", None),
            P("groups", None),
            P("groups", None, None),
        ),
        check_vma=False,
    )
```
